128 devices in a mesh: row: 4 (over y), col: 32 (over x, z, core).
Axes of the slice: x: 4, y: 4, z: 4, core: 2. Of those that a mesh axis runs over, the one named last changes fastest.
Arguments:
- basis: bfloat16 [65536, 1024], P(('row', 'col')), may hold values from -6 to 6
- dmat: bfloat16 [8192, 128, 128], P(('row', 'col')), may hold values from -0.0078125 to 0.0078125
- tile_home: int32 [8192], replicated, may hold values from 0 to 8191, as said below
- pair_tiles: int32 [512, 32], P(('row', 'col')), may hold values from 0 to 8191, as said below
- pair_pos: int32 [512, 32], P(('row', 'col')), may hold values from 0 to 63, as said below
- coords: float32 [3, 65536], P(None, ('row', 'col')), may hold values from -5 to 5
- weights: float32 [65536], P(('row', 'col')), may hold values from 0.6 to 6
- grad_sq: float32 [65536], P(('row', 'col')), may hold values from 0.5 to 6
- pair_keep: int32 [512, 512], replicated, may hold values from 0 to 1, as said below
Outputs:
- field_matrix_pieces: float32 [8192, 128, 128], P(('row', 'col'))
- correlation_field: float32 [65536], P(('row', 'col'))
The draws below stay inside these ranges and needn't reach their ends.
Inputs may be any that keep to these rules, and one draw needn't show every extreme that they name: A permutation: tile t is row tile_home[t] of dmat, and rows g * 64 to (g+1) * 64 - 1 lie on device g of row+col. `pair_tiles`: the blocks of one device name at most 2 tiles (repeats counted) stored on any one device, and one storing device is named exactly 2 times by the blocks of every device. `pair_pos`: pair position q stands for orbital tiles q // 8 and q % 8 of the block; the positions of one block are distinct. pair_keep[b,b] = 1 for every block b.
All inputs are finite; a program needn't handle non-finite values.
Results may differ from the reference program's by a relative error of at most 0.004.
Values may be sent and summed in bfloat16 or wider, within the bound.
A program may use at most 128 MiB of HBM per device.

```python
import math
import jax
import jax.numpy as jnp
from jax import lax

TB = 128
ORBS = 1024
KT = 8
NP = 32
PB = 128
BLK_DEV = 4
TD_DEV = 64
CAP = 2
BLOCKS = 512
POINTS = 65536
NDT = 8192
DEVICES = 128


def tile_plan(key):
    requests = BLK_DEV * NP
    favored = jax.random.randint(jax.random.fold_in(key, 101), (), 0, DEVICES)
    spread = 2 ** 30 // NDT
    home_scores = jax.random.randint(jax.random.fold_in(key, 102), (NDT,), 0, spread) * NDT + jnp.arange(NDT, dtype=jnp.int32)
    home_map = jnp.argsort(home_scores).astype(jnp.int32)
    inverse = jnp.argsort(home_map).astype(jnp.int32)
    pool_size = (DEVICES - 1) * CAP
    pool_scores = jax.random.randint(jax.random.fold_in(key, 103), (DEVICES, pool_size), 0, 2 ** 30 // pool_size) * pool_size + jnp.arange(pool_size, dtype=jnp.int32)[None, :]
    picks_order = jnp.argsort(pool_scores, axis=1).astype(jnp.int32)[:, :requests - CAP]
    others = (favored + 1 + picks_order // CAP) % DEVICES
    owners = jnp.concatenate([jnp.zeros((DEVICES, CAP), jnp.int32) + favored, others], axis=1)
    within = jax.random.randint(jax.random.fold_in(key, 104), (DEVICES, requests), 0, TD_DEV)
    retained_submatrices = owners * TD_DEV + within
    logical = inverse[retained_submatrices]
    return (home_map, logical.reshape(BLOCKS, NP).astype(jnp.int32))


def draw_tile_home(key, part):
    shared = tile_plan(key)
    return shared[0]


def draw_pair_tiles(key, part):
    shared = tile_plan(key)
    return shared[1]


def draw_pair_pos(key, part):
    key = jax.random.fold_in(key, 3)
    choices_count = ORBS // TB * (ORBS // TB)
    scores = jax.random.randint(key, (BLOCKS, choices_count), 0, 2 ** 20) * choices_count + jnp.arange(choices_count, dtype=jnp.int32)[None, :]
    return jnp.argsort(scores, axis=1)[:, :NP].astype(jnp.int32)


def draw_pair_keep(key, part):
    key = jax.random.fold_in(key, 5)
    picks = jax.random.randint(key, (BLOCKS, BLOCKS), 0, 128)
    places = jnp.arange(BLOCKS, dtype=jnp.int32)
    same_block = places[:, None] == places[None, :]
    return jnp.where((picks == 0) | same_block, 1, 0).astype(jnp.int32)


def levels(own_key, dims, cuts, least, high):
    def one(axis_at, blocks):
        steps = jax.random.uniform(jax.random.fold_in(jax.random.fold_in(own_key, 6), axis_at), (blocks,), jnp.float32, least / len(cuts), high / len(cuts))
        return jnp.repeat(jnp.exp(steps), dims[axis_at] // blocks).reshape((-1,) + (1,) * (len(dims) - axis_at - 1))

    gain = one(*cuts[0])
    for cut in cuts[1:]:
        gain = gain * one(*cut)
    return gain


def noise(own_key, shape, scale, limit, shards=(), kind=jnp.bfloat16):
    entries = scale * jax.random.normal(own_key, shape, jnp.float32)
    if shards:
        entries = entries * levels(own_key, shape, shards, -0.22, 0.18)
    return jnp.clip(entries, -limit, limit).astype(kind)


def setup_inputs(seed: int = 0) -> dict:
    streams_of = jax.random.split(jax.random.key(seed), 10)
    return {
        "basis": noise(streams_of[0], (POINTS, ORBS), 1.0, 6.0, ((0, 128),)),
        "dmat": noise(streams_of[1], (NDT, TB, TB), (TB * TB * NP) ** -0.5, 0.0078125, ((0, 128),)),
        "tile_home": draw_tile_home(jax.random.fold_in(streams_of[9], 71), 0),
        "pair_tiles": draw_pair_tiles(jax.random.fold_in(streams_of[9], 71), 0),
        "pair_pos": draw_pair_pos(jax.random.fold_in(streams_of[9], 71), 0),
        "coords": noise(streams_of[5], (3, POINTS), 1.0, 5.0, ((1, 128),), jnp.float32),
        "weights": jnp.clip(jnp.exp(math.log(6.0) - 2.3025851 * jax.random.uniform(streams_of[6], (POINTS,), jnp.float32) ** levels(streams_of[6], (POINTS,), ((0, 128),), -0.2, 0.2)), 0.6, 6.0),
        "grad_sq": jnp.clip(0.5 + 5.5 * jax.random.uniform(streams_of[7], (POINTS,), jnp.float32) ** levels(streams_of[7], (POINTS,), ((0, 128),), -0.2, 0.2), 0.5, 6.0),
        "pair_keep": draw_pair_keep(jax.random.fold_in(streams_of[9], 71), 0),
    }


gradient_coef = 0.0093
kappa_coef = 6.3
density_floor = 0.1

def point_features(raw_density, grad_sq):
    density = jax.nn.softplus(raw_density) + density_floor
    ratio = grad_sq / (density * density)
    omega_zero = jnp.sqrt(gradient_coef * ratio * ratio + 4.0 * jnp.pi / 3.0 * density)
    kappa_point = kappa_coef * 1.5 * jnp.pi * (density / (9.0 * jnp.pi)) ** (1.0 / 6.0)
    return (density, omega_zero, kappa_point)

def pair_block(target_feat, source_feat, keep_rows, block_rows):
    distance = jnp.zeros((target_feat.shape[1], source_feat.shape[1]), source_feat.dtype)
    for axis_pos in range(3):
        offset = target_feat[2 + axis_pos][:, None] - source_feat[3 + axis_pos][None, :]
        distance = distance + offset * offset
    target_term = target_feat[0][:, None] * distance + target_feat[1][:, None]
    source_term = source_feat[1][None, :] * distance + source_feat[2][None, :]
    kernel = -1.5 / (target_term * source_term * (target_term + source_term))
    target_blocks = target_feat.shape[1] // block_rows
    source_blocks = source_feat.shape[1] // block_rows
    shaped = kernel.reshape(target_blocks, block_rows, source_blocks, block_rows)
    weight = keep_rows[:, None, :, None] * source_feat[0].reshape(1, 1, source_blocks, block_rows)
    return lax.optimization_barrier(jnp.sum(shaped * weight, axis=(2, 3))).reshape(-1)

def reference(basis, dmat, tile_home, pair_tiles, pair_pos, coords, weights, grad_sq, pair_keep):
    first_slot_number = (pair_pos // KT).astype(jnp.int32)
    second_slot_number = (pair_pos % KT).astype(jnp.int32)
    retained_submatrices = tile_home[pair_tiles].astype(jnp.int32)
    atomic_basis_evaluations = basis.reshape(BLOCKS, PB, KT, TB)

    def block_density(pieces):
        orb_block, left_index, right_index, rows_index = pieces
        tiles = dmat[rows_index].astype(jnp.float32)
        left_part = orb_block[:, left_index, :].astype(jnp.float32)
        right_part = orb_block[:, right_index, :].astype(jnp.float32)
        mixed_rows = jnp.einsum('pna,nac->pnc', left_part, tiles)
        return lax.optimization_barrier(jnp.sum(mixed_rows * right_part, axis=(1, 2)))
    raw_density = lax.map(block_density, (atomic_basis_evaluations, first_slot_number, second_slot_number, retained_submatrices)).reshape(-1)
    density, omega_zero, kappa_point = point_features(raw_density, grad_sq)
    strength = weights * density
    source_feat = jnp.concatenate([jnp.stack([strength, omega_zero, kappa_point]), coords], axis=0)
    target_feat = jnp.concatenate([jnp.stack([omega_zero, kappa_point]), coords], axis=0)
    keep_mask = pair_keep.astype(strength.dtype)

    def block_potential(block_index):
        targets = lax.dynamic_slice_in_dim(target_feat, block_index * PB, PB, 1)
        keep_rows = lax.dynamic_slice_in_dim(keep_mask, block_index, 1, 0)
        return pair_block(targets, source_feat, keep_rows, PB)
    correlation_field = lax.map(block_potential, jnp.arange(BLOCKS, dtype=jnp.int32)).reshape(-1)
    scaled = (basis.astype(jnp.float32) * (weights * correlation_field)[:, None]).astype(jnp.bfloat16)
    weighted_group_entries = scaled.reshape(BLOCKS, PB, KT, TB)

    def submatrices_each_group(running, pieces):
        orb_block, scaled_block, left_index, right_index, rows_index = pieces
        left_part = scaled_block[:, left_index, :].astype(jnp.float32)
        right_part = orb_block[:, right_index, :].astype(jnp.float32)
        rounded = jnp.einsum('pna,pnc->nac', left_part, right_part).astype(jnp.bfloat16)
        rounded = lax.optimization_barrier(rounded)
        return (running.at[rows_index].add(rounded.astype(jnp.float32)), None)
    starting_submatrices = jnp.zeros((NDT, TB, TB), jnp.float32)
    field_matrix_pieces = lax.scan(submatrices_each_group, starting_submatrices, (atomic_basis_evaluations, weighted_group_entries, first_slot_number, second_slot_number, retained_submatrices))[0]
    return (field_matrix_pieces, correlation_field)
```

```python
import functools

import jax
import jax.numpy as jnp
from jax import lax
from jax.experimental import pallas as pl
from jax.experimental.pallas import tpu as pltpu
from jax.sharding import PartitionSpec as P

gradient_coef = 0.0093
kappa_coef = 6.3
density_floor = 0.1
AXES = ("row", "col")
VMEM_LIMIT = 56 * 2**20


def point_features(raw_density, grad_sq):
    density = jnp.maximum(raw_density, 0.0) + jnp.log1p(jnp.exp(-jnp.abs(raw_density))) + density_floor
    ratio = grad_sq / (density * density)
    omega_zero = jnp.sqrt(gradient_coef * ratio * ratio + 4.0 * jnp.pi / 3.0 * density)
    kappa_point = kappa_coef * 1.5 * jnp.pi * jnp.exp(jnp.log(density / (9.0 * jnp.pi)) * (1.0 / 6.0))
    return density, omega_zero, kappa_point


def params(**more):
    return pltpu.CompilerParams(vmem_limit_bytes=VMEM_LIMIT, **more)


def pick_kernel(asked, tiles, out):
    step = pl.program_id(0)
    width = out.shape[0]

    @pl.loop(0, width)
    def _(slot):
        wanted = asked[step * width + slot]

        @pl.when(wanted >= 0)
        def _():
            out[slot] = tiles[wanted]


def pick_tiles(asked, tiles):
    count = asked.shape[0]
    group = 32
    return pl.pallas_call(
        pick_kernel,
        grid=(count // group,),
        in_specs=[
            pl.BlockSpec(memory_space=pltpu.SMEM),
            pl.BlockSpec(memory_space=pltpu.VMEM),
        ],
        out_specs=pl.BlockSpec((group,) + tiles.shape[1:], lambda i: (i, 0, 0)),
        out_shape=jax.ShapeDtypeStruct((count,) + tiles.shape[1:], tiles.dtype),
        compiler_params=params(),
        name="pick_tiles",
    )(asked, tiles)


def density_kernel(slots, positions, basis, arrived, raw, dense, sems):
    blocks, pairs = positions.shape
    rows = basis.shape[0] // blocks
    orbs = basis.shape[1]
    tile = arrived.shape[1]
    kt = orbs // tile

    dense[...] = jnp.zeros_like(dense)

    def fetch(b, k):
        q = positions[b, k]
        left = pl.multiple_of((q // kt) * tile, tile)
        right = pl.multiple_of((q % kt) * tile, tile)
        return pltpu.make_async_copy(
            arrived.at[slots[b * pairs + k]],
            dense.at[b, pl.ds(left, tile), pl.ds(right, tile)],
            sems.at[b * pairs + k],
        )

    for b in range(blocks):

        @pl.loop(0, pairs)
        def _(k):
            fetch(b, k).start()

    for b in range(blocks):

        @pl.loop(0, pairs)
        def _(k):
            fetch(b, k).wait()

        chi = basis[b * rows : (b + 1) * rows, :]
        mixed = jnp.dot(chi, dense[b], preferred_element_type=jnp.float32)
        both = mixed * chi.astype(jnp.float32)
        part = both[:, :tile]
        for m in range(1, kt):
            part = part + both[:, m * tile : (m + 1) * tile]
        raw[b : b + 1, :] = jnp.sum(part.T, axis=0, keepdims=True)


def block_density(slots, positions, basis, arrived):
    blocks = positions.shape[0]
    rows = basis.shape[0] // blocks
    orbs = basis.shape[1]
    return pl.pallas_call(
        density_kernel,
        in_specs=[
            pl.BlockSpec(memory_space=pltpu.SMEM),
            pl.BlockSpec(memory_space=pltpu.SMEM),
            pl.BlockSpec(memory_space=pltpu.VMEM),
            pl.BlockSpec(memory_space=pl.ANY),
        ],
        out_specs=pl.BlockSpec(memory_space=pltpu.VMEM),
        out_shape=jax.ShapeDtypeStruct((blocks, rows), jnp.float32),
        scratch_shapes=[
            pltpu.VMEM((blocks, orbs, orbs), basis.dtype),
            pltpu.SemaphoreType.DMA((positions.size,)),
        ],
        compiler_params=params(),
        name="block_density",
    )(slots, positions, basis, arrived)


def field_kernel(
    kept, counts, slots, positions, first, raw, source, basis, field, tiles_out, feats, column, scaled, staged, sems
):
    blocks, pairs = positions.shape
    rows = raw.shape[1]
    tile = tiles_out.shape[1]
    kt = basis.shape[1] // tile
    weights = source[:, 0]
    density, omega, kappa = point_features(raw[...], source[:, 1])
    feats[0] = weights * density
    feats[1] = omega
    feats[2] = kappa
    for axis in range(3):
        feats[3 + axis] = source[:, 2 + axis]

    def send(b, k):
        return pltpu.make_async_copy(
            staged.at[b * pairs + k], tiles_out.at[slots[b * pairs + k]], sems.at[b * pairs + k]
        )

    for b in range(blocks):
        at = first[0] + b
        for f in range(5):
            row = feats[1 + f, pl.ds(at, 1), :]
            column[f] = jnp.broadcast_to(row, (rows, rows)).T

        def one_source(j, total):
            s = kept[b, j]
            r2 = None
            for axis in range(3):
                gap = column[2 + axis] - feats[3 + axis, pl.ds(s, 1), :]
                r2 = gap * gap if r2 is None else r2 + gap * gap
            g = column[0] * r2 + column[1]
            h = feats[1, pl.ds(s, 1), :] * r2 + feats[2, pl.ds(s, 1), :]
            phi = -1.5 / (g * h * (g + h))
            return total + phi * feats[0, pl.ds(s, 1), :]

        total = lax.fori_loop(0, counts[b], one_source, jnp.zeros((rows, rows), jnp.float32))
        potential = jnp.sum(total, axis=1, keepdims=True)
        wide = jnp.broadcast_to(potential, (rows, rows))
        field[b : b + 1, :] = wide.T[0:1, :]
        weight = jnp.broadcast_to(source[pl.ds(at, 1), 0], (rows, rows)).T
        factor = weight * wide
        for m in range(kt):
            chi = basis[b * rows : (b + 1) * rows, m * tile : (m + 1) * tile]
            scaled[m] = (chi.astype(jnp.float32) * factor).astype(jnp.bfloat16).T
            scaled[kt + m] = chi

        @pl.loop(0, pairs)
        def _(k):
            q = positions[b, k]
            product = jnp.dot(
                scaled[q // kt], scaled[kt + q % kt], preferred_element_type=jnp.float32
            )
            staged[b * pairs + k] = product.astype(jnp.bfloat16)
            send(b, k).start()

    for b in range(blocks):

        @pl.loop(0, pairs)
        def _(k):
            send(b, k).wait()


def field_and_tiles(kept, counts, slots, positions, first, raw, source, basis, slot_count):
    blocks, pairs = positions.shape
    total, rows = raw.shape
    tile = 128
    kt = basis.shape[1] // tile
    smem = pl.BlockSpec(memory_space=pltpu.SMEM)
    vmem = pl.BlockSpec(memory_space=pltpu.VMEM)
    return pl.pallas_call(
        field_kernel,
        in_specs=[smem] * 5 + [vmem] * 3,
        out_specs=[vmem, pl.BlockSpec(memory_space=pl.ANY)],
        out_shape=[
            jax.ShapeDtypeStruct((blocks, rows), jnp.float32),
            jax.ShapeDtypeStruct((slot_count, tile, tile), jnp.bfloat16),
        ],
        scratch_shapes=[
            pltpu.VMEM((6, total, rows), jnp.float32),
            pltpu.VMEM((5, rows, rows), jnp.float32),
            pltpu.VMEM((2 * kt, tile, rows), jnp.bfloat16),
            pltpu.VMEM((blocks * pairs, tile, tile), jnp.bfloat16),
            pltpu.SemaphoreType.DMA((blocks * pairs,)),
        ],
        compiler_params=params(),
        name="field_and_tiles",
    )(kept, counts, slots, positions, first, raw, source, basis)


def collect_kernel(order, starts, landed, out):
    step = pl.program_id(0)
    width = out.shape[0]

    @pl.loop(0, width)
    def _(t):
        g = step * width + t

        def add(j, total):
            return total + landed[order[j]].astype(jnp.float32)

        out[t] = lax.fori_loop(
            starts[g], starts[g + 1], add, jnp.zeros(out.shape[1:], jnp.float32)
        )


def collect_tiles(order, starts, landed, store_count):
    tile = landed.shape[1]
    group = 8
    smem = pl.BlockSpec(memory_space=pltpu.SMEM)
    return pl.pallas_call(
        collect_kernel,
        grid=(store_count // group,),
        in_specs=[smem, smem, pl.BlockSpec(memory_space=pltpu.VMEM)],
        out_specs=pl.BlockSpec((group, tile, tile), lambda i: (i, 0, 0)),
        out_shape=jax.ShapeDtypeStruct((store_count, tile, tile), jnp.float32),
        compiler_params=params(),
        name="collect_tiles",
    )(order, starts, landed)


def kept_list(keep):
    width = keep.shape[1]
    places = jnp.arange(width, dtype=jnp.int32)
    rank = jnp.cumsum(keep, axis=1) - keep
    hit = (rank[:, :, None] == places[None, None, :]) & (keep[:, :, None] > 0)
    return (
        jnp.sum(jnp.where(hit, places[None, :, None], 0), axis=1),
        jnp.sum(keep, axis=1),
    )


def slot_order(asked, store_count):
    count = asked.shape[0]
    places = jnp.arange(count, dtype=jnp.int32)
    key = jnp.where(asked >= 0, asked, store_count) * count + places
    rank = jnp.sum((key[None, :] < key[:, None]).astype(jnp.int32), axis=1)
    order = jnp.sum(jnp.where(rank[:, None] == places[None, :], places[:, None], 0), axis=0)
    stores = jnp.arange(store_count + 1, dtype=jnp.int32)
    starts = jnp.sum(
        ((asked[None, :] >= 0) & (asked[None, :] < stores[:, None])).astype(jnp.int32), axis=1
    )
    return order, starts


def body(basis, dmat, tile_home, pair_tiles, pair_pos, coords, weights, grad_sq, pair_keep):
    peer_count = lax.axis_size(AXES)
    me = lax.axis_index(AXES)
    blocks, pairs = pair_tiles.shape
    store_count, tile = dmat.shape[0], dmat.shape[1]
    rows = basis.shape[0] // blocks
    capacity = 2
    slot_count = peer_count * capacity
    wanted = tile_home[pair_tiles.reshape(-1)]
    owner = wanted // store_count
    within = wanted % store_count
    same = owner[:, None] == owner[None, :]
    places = jnp.arange(blocks * pairs, dtype=jnp.int32)
    earlier = jnp.sum((same & (places[None, :] < places[:, None])).astype(jnp.int32), axis=1)
    slots = owner * capacity + earlier
    slot_places = jnp.arange(slot_count, dtype=jnp.int32)
    asking = (
        jnp.sum(jnp.where(slots[:, None] == slot_places[None, :], within[:, None] + 1, 0), axis=0) - 1
    )
    asked = lax.all_to_all(
        asking.reshape(peer_count, capacity), AXES, split_axis=0, concat_axis=0, tiled=True
    ).reshape(-1)

    arrived = lax.all_to_all(
        pick_tiles(asked, dmat).reshape(peer_count, capacity, tile, tile),
        AXES,
        split_axis=0,
        concat_axis=0,
        tiled=True,
    ).reshape(slot_count, tile, tile)

    mine = jnp.concatenate([weights[None], grad_sq[None], coords], axis=0)
    mine = mine.reshape(5, blocks, rows).transpose(1, 0, 2)
    source = lax.all_gather(mine, AXES, axis=0, tiled=True)
    keep = lax.dynamic_slice_in_dim(pair_keep, me * blocks, blocks, 0)
    kept, counts = kept_list(keep)
    order, starts = slot_order(asked, store_count)

    raw = block_density(slots, pair_pos, basis, arrived)
    raw = lax.all_gather(raw, AXES, axis=0, tiled=True)
    first = (me * blocks).astype(jnp.int32).reshape(1)
    field, returning = field_and_tiles(
        kept, counts, slots, pair_pos, first, raw, source, basis, slot_count
    )
    landed = lax.all_to_all(
        returning.reshape(peer_count, capacity, tile, tile),
        AXES,
        split_axis=0,
        concat_axis=0,
        tiled=True,
    ).reshape(slot_count, tile, tile)
    return collect_tiles(order, starts, landed, store_count), field.reshape(-1)


def solution(mesh):
    in_specs = (
        P(AXES, None),
        P(AXES, None, None),
        P(),
        P(AXES, None),
        P(AXES, None),
        P(None, AXES),
        P(AXES),
        P(AXES),
        P(),
    )
    out_specs = (P(AXES, None, None), P(AXES))
    return jax.shard_map(body, mesh=mesh, in_specs=in_specs, out_specs=out_specs, check_vma=False)
```

```python
import functools

import jax
import jax.numpy as jnp
from jax import lax
from jax.experimental import pallas as pl
from jax.experimental.pallas import tpu as pltpu
from jax.sharding import PartitionSpec as P

gradient_coef = 0.0093
kappa_coef = 6.3
density_floor = 0.1
AXES = ("row", "col")
VMEM_LIMIT = 56 * 2**20
MESH = pl.DeviceIdType.MESH
STRIDE = 37


def point_features(raw_density, grad_sq):
    density = jnp.maximum(raw_density, 0.0) + jnp.log1p(jnp.exp(-jnp.abs(raw_density))) + density_floor
    ratio = grad_sq / (density * density)
    omega_zero = jnp.sqrt(gradient_coef * ratio * ratio + 4.0 * jnp.pi / 3.0 * density)
    kappa_point = kappa_coef * 1.5 * jnp.pi * jnp.exp(jnp.log(density / (9.0 * jnp.pi)) * (1.0 / 6.0))
    return density, omega_zero, kappa_point


def params(**more):
    return pltpu.CompilerParams(vmem_limit_bytes=VMEM_LIMIT, **more)


def neighbour(step):
    row, col = lax.axis_index("row"), lax.axis_index("col")
    x, z, core = col // 8, lax.rem(col // 2, 4), lax.rem(col, 2)
    y = lax.rem(row + step // 32, 4)
    x = lax.rem(x + lax.rem(step // 8, 4), 4)
    z = lax.rem(z + lax.rem(step // 2, 4), 4)
    core = lax.rem(core + lax.rem(step, 2), 2)
    return y, x * 8 + z * 2 + core


def device_number(place):
    return place[0] * 32 + place[1]


def greet_all(peers):
    barrier = pltpu.get_barrier_semaphore()
    for step in range(1, peers):
        pl.semaphore_signal(barrier, inc=1, device_id=neighbour(step), device_id_type=MESH)
    pl.semaphore_wait(barrier, peers - 1)


def fetch_kernel(
    asking,
    table,
    tiles,
    basis,
    asked,
    raw_all,
    wanted,
    stage,
    arrived,
    dense,
    raw,
    smem_sem,
    ask_send,
    ask_recv,
    tile_send,
    tile_recv,
    raw_send,
    raw_recv,
):
    peers = asking.shape[0]
    blocks, places = table.shape
    orbs = basis.shape[1]
    rows = basis.shape[0] // blocks
    tile = tiles.shape[1]
    kt = orbs // tile
    me = device_number((lax.axis_index("row"), lax.axis_index("col")))

    def remote(source, target, send, recv, step, place):
        return pltpu.make_async_remote_copy(
            src_ref=source,
            dst_ref=target,
            send_sem=send.at[step],
            recv_sem=recv.at[step],
            device_id=place,
            device_id_type=MESH,
        )

    def ask(step):
        place = neighbour(step)
        return remote(
            asking.at[device_number(place)], asked.at[me], ask_send, ask_recv, step, place
        )

    def give(step):
        place = neighbour(step)
        return remote(
            stage.at[device_number(place)], arrived.at[me], tile_send, tile_recv, step, place
        )

    def tell(step):
        return remote(raw, raw_all.at[me], raw_send, raw_recv, step, neighbour(step))

    greet_all(peers)

    @pl.loop(1, peers)
    def _(step):
        ask(step).start()

    asked[me] = asking[me]
    arrived[peers] = jnp.zeros(arrived.shape[1:], arrived.dtype)

    @pl.loop(1, peers)
    def _(step):
        ask(step).wait()

    to_smem = pltpu.make_async_copy(asked, wanted, smem_sem)
    to_smem.start()
    to_smem.wait()

    @pl.loop(1, peers)
    def _(turn):
        step = lax.rem(turn * STRIDE, peers)
        to = device_number(neighbour(step))
        for slot in range(2):
            stage[to, slot] = tiles[jnp.maximum(wanted[to, 0, slot] - 1, 0)]
        give(step).start()

    for slot in range(2):
        arrived[me, slot] = tiles[jnp.maximum(wanted[me, 0, slot] - 1, 0)]

    @pl.loop(1, peers)
    def _(step):
        give(step).wait()

    for b in range(blocks):

        @pl.loop(0, kt)
        def _(left):
            for right in range(kt):
                slot = table[b, left * kt + right]
                dense[pl.ds(pl.multiple_of(left * tile, tile), tile), right * tile : (right + 1) * tile] = (
                    arrived[slot // 2, lax.rem(slot, 2)]
                )

        chi = basis[b * rows : (b + 1) * rows, :]
        mixed = jnp.dot(chi, dense[...], preferred_element_type=jnp.float32)
        both = mixed * chi.astype(jnp.float32)
        part = both[:, :tile]
        for m in range(1, kt):
            part = part + both[:, m * tile : (m + 1) * tile]
        raw[b : b + 1, :] = jnp.sum(part.T, axis=0, keepdims=True)

    @pl.loop(1, peers)
    def _(step):
        tell(step).start()

    raw_all[me] = raw[...]

    @pl.loop(1, peers)
    def _(step):
        tell(step).wait()


def fetch_and_density(asking, table, tiles, basis):
    peers = asking.shape[0]
    blocks = table.shape[0]
    tile = tiles.shape[1]
    rows = basis.shape[0] // blocks
    orbs = basis.shape[1]
    smem = pl.BlockSpec(memory_space=pltpu.SMEM)
    vmem = pl.BlockSpec(memory_space=pltpu.VMEM)
    return pl.pallas_call(
        fetch_kernel,
        in_specs=[vmem, smem, vmem, vmem],
        out_specs=[vmem, vmem],
        out_shape=[
            jax.ShapeDtypeStruct(asking.shape, asking.dtype),
            jax.ShapeDtypeStruct((peers, blocks, rows), jnp.float32),
        ],
        scratch_shapes=[
            pltpu.SMEM(asking.shape, asking.dtype),
            pltpu.VMEM((peers, 2, tile, tile), tiles.dtype),
            pltpu.VMEM((peers + 1, 2, tile, tile), tiles.dtype),
            pltpu.VMEM((orbs, orbs), basis.dtype),
            pltpu.VMEM((blocks, rows), jnp.float32),
            pltpu.SemaphoreType.DMA,
        ]
        + [pltpu.SemaphoreType.DMA((peers,))] * 6,
        compiler_params=params(collective_id=0, has_side_effects=True),
        name="fetch_and_density",
    )(asking, table, tiles, basis)


def field_kernel(
    kept, counts, slots, positions, first, raw, source, basis, field, tiles_out, feats, column, scaled, staged, sems
):
    blocks, pairs = positions.shape
    rows = raw.shape[1]
    tile = tiles_out.shape[1]
    kt = basis.shape[1] // tile
    weights = source[:, 0]
    density, omega, kappa = point_features(raw[...], source[:, 1])
    feats[0] = weights * density
    feats[1] = omega
    feats[2] = kappa
    for axis in range(3):
        feats[3 + axis] = source[:, 2 + axis]

    def send(b, k):
        return pltpu.make_async_copy(
            staged.at[b * pairs + k], tiles_out.at[slots[b * pairs + k]], sems.at[b * pairs + k]
        )

    for b in range(blocks):
        at = first[0] + b
        for f in range(5):
            row = feats[1 + f, pl.ds(at, 1), :]
            column[f] = jnp.broadcast_to(row, (rows, rows)).T

        def one_source(j, total):
            s = kept[b, j]
            r2 = None
            for axis in range(3):
                gap = column[2 + axis] - feats[3 + axis, pl.ds(s, 1), :]
                r2 = gap * gap if r2 is None else r2 + gap * gap
            g = column[0] * r2 + column[1]
            h = feats[1, pl.ds(s, 1), :] * r2 + feats[2, pl.ds(s, 1), :]
            phi = -1.5 / (g * h * (g + h))
            return total + phi * feats[0, pl.ds(s, 1), :]

        total = lax.fori_loop(0, counts[b], one_source, jnp.zeros((rows, rows), jnp.float32))
        potential = jnp.sum(total, axis=1, keepdims=True)
        wide = jnp.broadcast_to(potential, (rows, rows))
        field[b : b + 1, :] = wide.T[0:1, :]
        weight = jnp.broadcast_to(source[pl.ds(at, 1), 0], (rows, rows)).T
        factor = weight * wide
        for m in range(kt):
            chi = basis[b * rows : (b + 1) * rows, m * tile : (m + 1) * tile]
            scaled[m] = (chi.astype(jnp.float32) * factor).astype(jnp.bfloat16).T
            scaled[kt + m] = chi

        @pl.loop(0, pairs)
        def _(k):
            q = positions[b, k]
            product = jnp.dot(
                scaled[q // kt], scaled[kt + q % kt], preferred_element_type=jnp.float32
            )
            staged[b * pairs + k] = product.astype(jnp.bfloat16)
            send(b, k).start()

    for b in range(blocks):

        @pl.loop(0, pairs)
        def _(k):
            send(b, k).wait()


def field_and_tiles(kept, counts, slots, positions, first, raw, source, basis, slot_count):
    blocks, pairs = positions.shape
    total, rows = raw.shape
    tile = 128
    kt = basis.shape[1] // tile
    smem = pl.BlockSpec(memory_space=pltpu.SMEM)
    vmem = pl.BlockSpec(memory_space=pltpu.VMEM)
    return pl.pallas_call(
        field_kernel,
        in_specs=[smem] * 5 + [vmem] * 3,
        out_specs=[vmem, pl.BlockSpec(memory_space=pl.ANY)],
        out_shape=[
            jax.ShapeDtypeStruct((blocks, rows), jnp.float32),
            jax.ShapeDtypeStruct((slot_count, tile, tile), jnp.bfloat16),
        ],
        scratch_shapes=[
            pltpu.VMEM((6, total, rows), jnp.float32),
            pltpu.VMEM((5, rows, rows), jnp.float32),
            pltpu.VMEM((2 * kt, tile, rows), jnp.bfloat16),
            pltpu.VMEM((blocks * pairs, tile, tile), jnp.bfloat16),
            pltpu.SemaphoreType.DMA((blocks * pairs,)),
        ],
        compiler_params=params(),
        name="field_and_tiles",
    )(kept, counts, slots, positions, first, raw, source, basis)


def collect_kernel(order, starts, landed, out):
    step = pl.program_id(0)
    width = out.shape[0]

    @pl.loop(0, width)
    def _(t):
        g = step * width + t

        def add(j, total):
            return total + landed[order[j]].astype(jnp.float32)

        out[t] = lax.fori_loop(
            starts[g], starts[g + 1], add, jnp.zeros(out.shape[1:], jnp.float32)
        )


def collect_tiles(order, starts, landed, store_count):
    tile = landed.shape[1]
    group = 8
    smem = pl.BlockSpec(memory_space=pltpu.SMEM)
    return pl.pallas_call(
        collect_kernel,
        grid=(store_count // group,),
        in_specs=[smem, smem, pl.BlockSpec(memory_space=pltpu.VMEM)],
        out_specs=pl.BlockSpec((group, tile, tile), lambda i: (i, 0, 0)),
        out_shape=jax.ShapeDtypeStruct((store_count, tile, tile), jnp.float32),
        compiler_params=params(),
        name="collect_tiles",
    )(order, starts, landed)


def kept_list(keep):
    width = keep.shape[1]
    places = jnp.arange(width, dtype=jnp.int32)
    rank = jnp.cumsum(keep, axis=1) - keep
    hit = (rank[:, :, None] == places[None, None, :]) & (keep[:, :, None] > 0)
    return (
        jnp.sum(jnp.where(hit, places[None, :, None], 0), axis=1),
        jnp.sum(keep, axis=1),
    )


def slot_order(asked, store_count):
    count = asked.shape[0]
    places = jnp.arange(count, dtype=jnp.int32)
    key = jnp.where(asked >= 0, asked, store_count) * count + places
    rank = jnp.sum((key[None, :] < key[:, None]).astype(jnp.int32), axis=1)
    order = jnp.sum(jnp.where(rank[:, None] == places[None, :], places[:, None], 0), axis=0)
    stores = jnp.arange(store_count + 1, dtype=jnp.int32)
    starts = jnp.sum(
        ((asked[None, :] >= 0) & (asked[None, :] < stores[:, None])).astype(jnp.int32), axis=1
    )
    return order, starts


def body(basis, dmat, tile_home, pair_tiles, pair_pos, coords, weights, grad_sq, pair_keep):
    peer_count = lax.axis_size(AXES)
    me = lax.axis_index(AXES)
    blocks, pairs = pair_tiles.shape
    store_count, tile = dmat.shape[0], dmat.shape[1]
    rows = basis.shape[0] // blocks
    capacity = 2
    slot_count = peer_count * capacity
    wanted = tile_home[pair_tiles.reshape(-1)]
    owner = wanted // store_count
    within = wanted % store_count
    same = owner[:, None] == owner[None, :]
    places = jnp.arange(blocks * pairs, dtype=jnp.int32)
    earlier = jnp.sum((same & (places[None, :] < places[:, None])).astype(jnp.int32), axis=1)
    slots = owner * capacity + earlier
    slot_places = jnp.arange(slot_count, dtype=jnp.int32)
    lanes = jnp.arange(tile, dtype=jnp.int32)
    entry = jnp.where(
        (owner[:, None] == jnp.arange(peer_count, dtype=jnp.int32)[None, :])[:, :, None]
        & (earlier[:, None] == lanes[None, :])[:, None, :],
        within[:, None, None] + 1,
        0,
    )
    asking = jnp.sum(entry, axis=0).reshape(peer_count, 1, tile)
    kt = basis.shape[1] // tile
    spot = pair_pos[:, :, None] == jnp.arange(kt * kt, dtype=jnp.int32)[None, None, :]
    table = jnp.sum(
        jnp.where(spot, slots.reshape(blocks, pairs)[:, :, None] - slot_count, 0), axis=1
    ) + slot_count
    mine = jnp.concatenate([weights[None], grad_sq[None], coords], axis=0)
    mine = mine.reshape(5, blocks, rows).transpose(1, 0, 2)
    source = lax.all_gather(mine, AXES, axis=0, tiled=True)
    keep = lax.dynamic_slice_in_dim(pair_keep, me * blocks, blocks, 0)
    kept, counts = kept_list(keep)

    asked, raw = fetch_and_density(asking, table, dmat, basis)
    raw = raw.reshape(peer_count * blocks, rows)
    order, starts = slot_order(asked[:, 0, :capacity].reshape(-1) - 1, store_count)
    first = (me * blocks).astype(jnp.int32).reshape(1)
    field, returning = field_and_tiles(
        kept, counts, slots, pair_pos, first, raw, source, basis, slot_count
    )
    landed = lax.all_to_all(
        returning.reshape(peer_count, capacity, tile, tile),
        AXES,
        split_axis=0,
        concat_axis=0,
        tiled=True,
    ).reshape(slot_count, tile, tile)
    return collect_tiles(order, starts, landed, store_count), field.reshape(-1)


def solution(mesh):
    in_specs = (
        P(AXES, None),
        P(AXES, None, None),
        P(),
        P(AXES, None),
        P(AXES, None),
        P(None, AXES),
        P(AXES),
        P(AXES),
        P(),
    )
    out_specs = (P(AXES, None, None), P(AXES))
    return jax.shard_map(body, mesh=mesh, in_specs=in_specs, out_specs=out_specs, check_vma=False)
```

```python
import functools

import jax
import jax.numpy as jnp
from jax import lax
from jax.experimental import pallas as pl
from jax.experimental.pallas import tpu as pltpu
from jax.sharding import PartitionSpec as P

gradient_coef = 0.0093
kappa_coef = 6.3
density_floor = 0.1
AXES = ("row", "col")
VMEM_LIMIT = 56 * 2**20
MESH = pl.DeviceIdType.MESH
STRIDE = 7
STEPS = (
    (0, 0, 0, 1),
    (0, 1, 0, 0),
    (1, 0, 0, 0),
    (0, 0, 1, 0),
    (0, 3, 0, 0),
    (3, 0, 0, 0),
    (0, 0, 3, 0),
    (0, 1, 1, 1),
    (1, 0, 1, 1),
    (1, 1, 0, 1),
    (0, 3, 3, 1),
    (3, 0, 3, 1),
    (3, 3, 0, 1),
    (0, 1, 3, 1),
    (1, 0, 3, 1),
    (1, 3, 0, 1),
)
ROOM = (56, 8, 8, 8, 4, 4, 4) + (1,) * 9
BASE = tuple(sum(ROOM[:k]) for k in range(len(ROOM)))
LINKS = len(ROOM)
RELAYED = sum(ROOM)
PLAN_ROWS = 2 * LINKS + 8
AT_LOC, AT_SRC, AT_CODE, AT_BACK, AT_LEFT = range(2 * LINKS, 2 * LINKS + 5)


def point_features(raw_density, grad_sq):
    density = jnp.maximum(raw_density, 0.0) + jnp.log1p(jnp.exp(-jnp.abs(raw_density))) + density_floor
    ratio = grad_sq / (density * density)
    omega_zero = jnp.sqrt(gradient_coef * ratio * ratio + 4.0 * jnp.pi / 3.0 * density)
    kappa_point = kappa_coef * 1.5 * jnp.pi * jnp.exp(jnp.log(density / (9.0 * jnp.pi)) * (1.0 / 6.0))
    return density, omega_zero, kappa_point


def params(**more):
    return pltpu.CompilerParams(vmem_limit_bytes=VMEM_LIMIT, **more)


def moved(device, move):
    dy, dx, dz, dc = move
    y = (device // 32 + dy) % 4
    x = (device // 8 + dx) % 4
    z = (device // 2 + dz) % 4
    return y * 32 + x * 8 + z * 2 + (device + dc) % 2


def back(move):
    return tuple((4 - m) % 4 for m in move[:3]) + (move[3],)


def parity(device):
    return (device + device // 2 + device // 8 + device // 32) % 2


def this_device():
    return lax.axis_index("row") * 32 + lax.axis_index("col")


def inside(value, count):
    return jnp.minimum(jnp.maximum(value, 0), count - 1)


def place_of(device):
    return device // 32, lax.rem(device, 32)


def neighbour(step):
    move = (step // 32, lax.rem(step // 8, 4), lax.rem(step // 2, 4), lax.rem(step, 2))
    return moved(this_device(), move)


def narrow_step(turn):
    up = lax.rem(turn * STRIDE, 64)
    return 2 * up + lax.rem(up + up // 4 + up // 16 + 1, 2)


def wide_step(turn):
    up = lax.rem(turn * STRIDE, 64)
    return 2 * up + lax.rem(up + up // 4 + up // 16, 2)


def greet_all(peers):
    barrier = pltpu.get_barrier_semaphore()
    for step in range(1, peers):
        pl.semaphore_signal(
            barrier, inc=1, device_id=place_of(neighbour(step)), device_id_type=MESH
        )


def wait_all(peers):
    pl.semaphore_wait(pltpu.get_barrier_semaphore(), peers - 1)


def remote(source, target, send, recv, at, device):
    return pltpu.make_async_remote_copy(
        src_ref=source,
        dst_ref=target,
        send_sem=send.at[at],
        recv_sem=recv.at[at],
        device_id=place_of(device),
        device_id_type=MESH,
    )


def make_plan(counts, plan):
    peers = counts.shape[0]
    me = this_device()
    asker = lax.broadcasted_iota(jnp.int32, (peers, peers), 0)
    owner = lax.broadcasted_iota(jnp.int32, (peers, peers), 1)
    wide = parity(asker) == parity(owner)
    zero = jnp.zeros((peers, peers), jnp.float32)
    left = jnp.where(wide | (counts < 2), 0.0, 1.0)
    free = jnp.where(wide & (counts < 2), 1.0, 0.0)
    earlier = jnp.where(owner < asker, 1.0, 0.0).astype(jnp.bfloat16)
    loc, src, code, again = zero, zero, zero, zero

    def dot(a, b):
        return jnp.dot(
            a.astype(jnp.bfloat16), b.astype(jnp.bfloat16), preferred_element_type=jnp.float32
        )

    def mine(values):
        return jnp.sum(jnp.where(owner == me, values, 0.0), axis=1, keepdims=True)

    def by_slot(column):
        hit = column == (owner + 1).astype(jnp.float32)
        return jnp.sum(jnp.where(hit, asker, 0), axis=0, keepdims=True)

    for k in range(LINKS):
        move, home = STEPS[k], back(STEPS[k])
        there = moved(owner, move)
        onto = jnp.where(asker == there, 1.0, 0.0)
        off = jnp.where(owner == moved(asker, move), 1.0, 0.0)
        want = left * dot(free, onto)
        rank = dot(earlier, want)
        numbered = jnp.where((want > 0.0) & (rank < ROOM[k]), rank + 1.0, 0.0)
        relay = dot(numbered, off)
        left = jnp.where(numbered > 0.0, 0.0, left)
        free = jnp.where(relay > 0.0, 0.0, free)
        loc = loc + jnp.where(numbered > 0.0, (2 * there + 1).astype(jnp.float32), 0.0)
        src = src + jnp.where(relay > 0.0, (moved(owner, home) + 1).astype(jnp.float32), 0.0)
        code = code + jnp.where(relay > 0.0, relay + BASE[k], 0.0)
        again = again + jnp.where(numbered > 0.0, numbered + (BASE[k] - 1.0), 0.0)
        plan[k : k + 1, :] = by_slot(mine(numbered))
        plan[LINKS + k : LINKS + k + 1, :] = by_slot(mine(relay))

    def row_of(values):
        return jnp.sum(jnp.where(asker == me, values, 0.0), axis=0, keepdims=True)

    def turned(values):
        return jnp.sum(jnp.where(asker == owner, mine(values), 0.0), axis=0, keepdims=True)

    plan[AT_LOC : AT_LOC + 1, :] = row_of(loc).astype(jnp.int32)
    plan[AT_SRC : AT_SRC + 1, :] = row_of(src).astype(jnp.int32)
    plan[AT_CODE : AT_CODE + 1, :] = turned(code).astype(jnp.int32)
    plan[AT_BACK : AT_BACK + 1, :] = turned(again).astype(jnp.int32)
    plan[AT_LEFT : AT_LEFT + 1, :] = jnp.sum(left, axis=0, keepdims=True).astype(jnp.int32)
    plan[AT_LEFT + 1 :, :] = jnp.zeros((PLAN_ROWS - AT_LEFT - 1, peers), jnp.int32)


def fetch_kernel(
    asking,
    table,
    tiles,
    basis,
    asked,
    plan,
    raw_all,
    wanted,
    route,
    stage,
    arrived,
    link_out,
    link_in,
    dense,
    raw,
    smem_sems,
    ask_send,
    ask_recv,
    first_send,
    first_recv,
    second_send,
    second_recv,
    link_send,
    link_recv,
    raw_send,
    raw_recv,
):
    peers = asking.shape[0]
    blocks = table.shape[0]
    orbs = basis.shape[1]
    rows = basis.shape[0] // blocks
    tile = tiles.shape[1]
    kt = orbs // tile
    me = this_device()

    def ask(step):
        to = neighbour(step)
        return remote(asking.at[to], asked.at[me], ask_send, ask_recv, step, to)

    def first(step):
        to = neighbour(step)
        return remote(stage.at[to, 0], arrived.at[me, 0], first_send, first_recv, step, to)

    def second(step):
        to = neighbour(step)
        return remote(stage.at[to, 1], arrived.at[me, 1], second_send, second_recv, step, to)

    def link(k):
        part = pl.ds(BASE[k], ROOM[k])
        return remote(
            link_out.at[part], link_in.at[part], link_send, link_recv, k, moved(me, STEPS[k])
        )

    def tell(step):
        return remote(raw, raw_all.at[me], raw_send, raw_recv, step, neighbour(step))

    def tile_for(device, slot):
        return tiles[inside(wanted[inside(device, peers), 0, slot] - 1, tiles.shape[0])]

    def second_for(device):
        at = route[AT_CODE, device]
        return jnp.where(at > 0, link_in[inside(at - 1, RELAYED)], tile_for(device, 1))

    greet_all(peers)
    wait_all(peers)

    @pl.loop(1, peers)
    def _(step):
        ask(step).start()

    asked[me] = asking[me]
    arrived[peers] = jnp.zeros(arrived.shape[1:], arrived.dtype)

    @pl.loop(1, peers)
    def _(step):
        ask(step).wait()

    to_smem = pltpu.make_async_copy(asked, wanted, smem_sems.at[0])
    to_smem.start()
    to_smem.wait()

    @pl.loop(0, 64)
    def _(turn):
        step = narrow_step(turn)
        to = neighbour(step)
        stage[to, 0] = tile_for(to, 0)
        first(step).start()

    make_plan(asked[:, 1, :], plan)
    to_smem = pltpu.make_async_copy(plan, route, smem_sems.at[1])
    to_smem.start()
    to_smem.wait()

    for k in range(LINKS):

        @pl.loop(0, ROOM[k])
        def _(s):
            link_out[BASE[k] + s] = tile_for(route[k, s], 1)

        link(k).start()

    @pl.loop(1, 64)
    def _(turn):
        step = wide_step(turn)
        to = neighbour(step)
        stage[to, 0] = tile_for(to, 0)
        first(step).start()

    arrived[me, 0] = tile_for(me, 0)

    for k in range(LINKS):
        link(k).wait()

    @pl.loop(1, 64)
    def _(turn):
        step = wide_step(turn)
        to = neighbour(step)
        stage[to, 1] = second_for(to)
        second(step).start()

    arrived[me, 1] = second_for(me)

    @pl.loop(1, peers)
    def _(step):
        first(step).wait()

    @pl.loop(1, 64)
    def _(turn):
        second(wide_step(turn)).wait()

    for b in range(blocks):

        @pl.loop(0, kt)
        def _(row):
            for column in range(kt):
                slot = table[b, row * kt + column]
                slot = jnp.where(
                    slot >= 4 * peers, route[AT_LOC, inside(slot - 4 * peers, peers)], slot
                )
                slot = inside(slot, 2 * peers + 1)
                dense[
                    pl.ds(pl.multiple_of(row * tile, tile), tile),
                    column * tile : (column + 1) * tile,
                ] = arrived[slot // 2, lax.rem(slot, 2)]

        chi = basis[b * rows : (b + 1) * rows, :]
        mixed = jnp.dot(chi, dense[...], preferred_element_type=jnp.float32)
        both = mixed * chi.astype(jnp.float32)
        part = both[:, :tile]
        for m in range(1, kt):
            part = part + both[:, m * tile : (m + 1) * tile]
        raw[b : b + 1, :] = jnp.sum(part.T, axis=0, keepdims=True)

    @pl.loop(1, peers)
    def _(step):
        tell(step).start()

    raw_all[me] = raw[...]

    @pl.loop(1, peers)
    def _(step):
        tell(step).wait()


def fetch_and_density(asking, table, tiles, basis):
    peers = asking.shape[0]
    blocks = table.shape[0]
    tile = tiles.shape[1]
    rows = basis.shape[0] // blocks
    orbs = basis.shape[1]
    smem = pl.BlockSpec(memory_space=pltpu.SMEM)
    vmem = pl.BlockSpec(memory_space=pltpu.VMEM)
    pair = pltpu.SemaphoreType.DMA((peers,))
    return pl.pallas_call(
        fetch_kernel,
        in_specs=[vmem, smem, vmem, vmem],
        out_specs=[vmem, vmem, vmem],
        out_shape=[
            jax.ShapeDtypeStruct(asking.shape, asking.dtype),
            jax.ShapeDtypeStruct((PLAN_ROWS, peers), jnp.int32),
            jax.ShapeDtypeStruct((peers, blocks, rows), jnp.float32),
        ],
        scratch_shapes=[
            pltpu.SMEM(asking.shape, asking.dtype),
            pltpu.SMEM((PLAN_ROWS, peers), jnp.int32),
            pltpu.VMEM((peers, 2, tile, tile), tiles.dtype),
            pltpu.VMEM((peers + 1, 2, tile, tile), tiles.dtype),
            pltpu.VMEM((RELAYED, tile, tile), tiles.dtype),
            pltpu.VMEM((RELAYED, tile, tile), tiles.dtype),
            pltpu.VMEM((orbs, orbs), basis.dtype),
            pltpu.VMEM((blocks, rows), jnp.float32),
            pltpu.SemaphoreType.DMA((2,)),
            pair,
            pair,
            pair,
            pair,
            pair,
            pair,
            pltpu.SemaphoreType.DMA((LINKS,)),
            pltpu.SemaphoreType.DMA((LINKS,)),
            pair,
            pair,
        ],
        compiler_params=params(collective_id=0, has_side_effects=True),
        name="fetch_and_density",
    )(asking, table, tiles, basis)


def field_only_kernel(kept, counts, first, raw, source, field, factor, feats, column):
    blocks, rows = field.shape
    weights = source[:, 0]
    density, omega, kappa = point_features(raw[...], source[:, 1])
    feats[0] = weights * density
    feats[1] = omega
    feats[2] = kappa
    for axis in range(3):
        feats[3 + axis] = source[:, 2 + axis]

    for b in range(blocks):
        at = first[0] + b
        for f in range(5):
            row = feats[1 + f, pl.ds(at, 1), :]
            column[f] = jnp.broadcast_to(row, (rows, rows)).T

        def one_source(j, total):
            s = kept[b, j]
            r2 = None
            for axis in range(3):
                gap = column[2 + axis] - feats[3 + axis, pl.ds(s, 1), :]
                r2 = gap * gap if r2 is None else r2 + gap * gap
            g = column[0] * r2 + column[1]
            h = feats[1, pl.ds(s, 1), :] * r2 + feats[2, pl.ds(s, 1), :]
            phi = -1.5 / (g * h * (g + h))
            return total + phi * feats[0, pl.ds(s, 1), :]

        total = lax.fori_loop(0, counts[b], one_source, jnp.zeros((rows, rows), jnp.float32))
        wide = jnp.broadcast_to(jnp.sum(total, axis=1, keepdims=True), (rows, rows))
        field[b : b + 1, :] = wide.T[0:1, :]
        weight = jnp.broadcast_to(source[pl.ds(at, 1), 0], (rows, rows)).T
        factor[b * rows : (b + 1) * rows, :] = weight * wide


def field_only(kept, counts, first, raw, source, blocks):
    total, rows = raw.shape
    smem = pl.BlockSpec(memory_space=pltpu.SMEM)
    vmem = pl.BlockSpec(memory_space=pltpu.VMEM)
    return pl.pallas_call(
        field_only_kernel,
        in_specs=[smem] * 3 + [vmem] * 2,
        out_specs=[vmem, vmem],
        out_shape=[
            jax.ShapeDtypeStruct((blocks, rows), jnp.float32),
            jax.ShapeDtypeStruct((blocks * rows, rows), jnp.float32),
        ],
        scratch_shapes=[
            pltpu.VMEM((6, total, rows), jnp.float32),
            pltpu.VMEM((5, rows, rows), jnp.float32),
        ],
        compiler_params=params(),
        name="field_only",
    )(kept, counts, first, raw, source)


def return_kernel(
    route,
    mine,
    factor,
    basis,
    land,
    seconds,
    products,
    stage,
    link_out,
    scaled,
    own_sems,
    first_send,
    first_recv,
    second_send,
    second_recv,
    link_send,
    link_recv,
):
    peers = mine.shape[0] // 2
    tile = land.shape[1]
    kt = basis.shape[1] // tile
    rows = tile
    blocks = basis.shape[0] // rows
    me = this_device()

    def first(step):
        to = neighbour(step)
        return remote(stage.at[to, 0], land.at[me], first_send, first_recv, step, to)

    def second(step):
        to = neighbour(step)
        return remote(stage.at[to, 1], seconds.at[me], second_send, second_recv, step, to)

    def link(k):
        return remote(
            link_out.at[pl.ds(BASE[k], ROOM[k])],
            land.at[pl.ds(2 * peers + BASE[k], ROOM[k])],
            link_send,
            link_recv,
            k,
            moved(me, back(STEPS[k])),
        )

    def product_for(at):
        return products[inside(mine[at], 2 * peers)]

    def second_for(device):
        via = route[AT_SRC, device]
        holder = inside(jnp.where(via > 0, via - 1, device), peers)
        return product_for(2 * holder + 1)

    greet_all(peers)

    @pl.loop(0, blocks)
    def _(b):
        chi = basis[pl.ds(pl.multiple_of(b * rows, rows), rows), :]
        by = factor[pl.ds(pl.multiple_of(b * rows, rows), rows), :]
        for m in range(kt):
            part = chi[:, m * tile : (m + 1) * tile].astype(jnp.float32) * by
            scaled[...] = part.astype(jnp.bfloat16).T
            product = jnp.dot(scaled[...], chi, preferred_element_type=jnp.float32)
            for n in range(kt):
                products[b * kt * kt + m * kt + n] = product[
                    :, n * tile : (n + 1) * tile
                ].astype(jnp.bfloat16)

    wait_all(peers)

    @pl.loop(1, 64)
    def _(turn):
        step = wide_step(turn)
        to = neighbour(step)
        stage[to, 1] = second_for(to)
        second(step).start()

    seconds[me] = second_for(me)
    stage[me, 0] = product_for(2 * me)
    own = pltpu.make_async_copy(stage.at[me, 0], land.at[me], own_sems.at[0])
    own.start()

    @pl.loop(0, 64)
    def _(turn):
        step = narrow_step(turn)
        to = neighbour(step)
        stage[to, 0] = product_for(2 * to)
        first(step).start()

    @pl.loop(1, 64)
    def _(turn):
        second(wide_step(turn)).wait()

    for k in range(LINKS):

        @pl.loop(0, ROOM[k])
        def _(s):
            link_out[BASE[k] + s] = seconds[inside(route[LINKS + k, s], peers)]

        link(k).start()

    keep = pltpu.make_async_copy(seconds, land.at[pl.ds(peers, peers)], own_sems.at[1])
    keep.start()

    @pl.loop(1, 64)
    def _(turn):
        step = wide_step(turn)
        to = neighbour(step)
        stage[to, 0] = product_for(2 * to)
        first(step).start()

    for k in range(LINKS):
        link(k).wait()

    @pl.loop(1, peers)
    def _(step):
        first(step).wait()

    own.wait()
    keep.wait()


def return_tiles(plan, mine, factor, basis, peers):
    tile = 128
    smem = pl.BlockSpec(memory_space=pltpu.SMEM)
    vmem = pl.BlockSpec(memory_space=pltpu.VMEM)
    pair = pltpu.SemaphoreType.DMA((peers,))
    return pl.pallas_call(
        return_kernel,
        in_specs=[smem, smem, vmem, vmem],
        out_specs=pl.BlockSpec(memory_space=pl.ANY),
        out_shape=jax.ShapeDtypeStruct((2 * peers + RELAYED, tile, tile), jnp.bfloat16),
        scratch_shapes=[
            pltpu.VMEM((peers, tile, tile), jnp.bfloat16),
            pltpu.VMEM((mine.shape[0], tile, tile), jnp.bfloat16),
            pltpu.VMEM((peers, 2, tile, tile), jnp.bfloat16),
            pltpu.VMEM((RELAYED, tile, tile), jnp.bfloat16),
            pltpu.VMEM((tile, tile), jnp.bfloat16),
            pltpu.SemaphoreType.DMA((2,)),
            pair,
            pair,
            pair,
            pair,
            pltpu.SemaphoreType.DMA((LINKS,)),
            pltpu.SemaphoreType.DMA((LINKS,)),
        ],
        compiler_params=params(collective_id=1, has_side_effects=True),
        name="return_tiles",
    )(plan, mine, factor, basis)


def pick_kernel(asked, tiles, out):
    step = pl.program_id(0)
    width = out.shape[0]

    @pl.loop(0, width)
    def _(slot):
        wanted = asked[step * width + slot]

        @pl.when(wanted >= 0)
        def _():
            out[slot] = tiles[wanted]


def pick_tiles(asked, tiles):
    count = asked.shape[0]
    group = 32
    return pl.pallas_call(
        pick_kernel,
        grid=(count // group,),
        in_specs=[
            pl.BlockSpec(memory_space=pltpu.SMEM),
            pl.BlockSpec(memory_space=pltpu.VMEM),
        ],
        out_specs=pl.BlockSpec((group,) + tiles.shape[1:], lambda i: (i, 0, 0)),
        out_shape=jax.ShapeDtypeStruct((count,) + tiles.shape[1:], tiles.dtype),
        compiler_params=params(),
        name="pick_tiles",
    )(asked, tiles)


def density_kernel(slots, positions, basis, arrived, raw, dense, sems):
    blocks, pairs = positions.shape
    rows = basis.shape[0] // blocks
    orbs = basis.shape[1]
    tile = arrived.shape[1]
    kt = orbs // tile

    dense[...] = jnp.zeros_like(dense)

    def fetch(b, k):
        q = positions[b, k]
        left = pl.multiple_of((q // kt) * tile, tile)
        right = pl.multiple_of((q % kt) * tile, tile)
        return pltpu.make_async_copy(
            arrived.at[slots[b * pairs + k]],
            dense.at[b, pl.ds(left, tile), pl.ds(right, tile)],
            sems.at[b * pairs + k],
        )

    for b in range(blocks):

        @pl.loop(0, pairs)
        def _(k):
            fetch(b, k).start()

    for b in range(blocks):

        @pl.loop(0, pairs)
        def _(k):
            fetch(b, k).wait()

        chi = basis[b * rows : (b + 1) * rows, :]
        mixed = jnp.dot(chi, dense[b], preferred_element_type=jnp.float32)
        both = mixed * chi.astype(jnp.float32)
        part = both[:, :tile]
        for m in range(1, kt):
            part = part + both[:, m * tile : (m + 1) * tile]
        raw[b : b + 1, :] = jnp.sum(part.T, axis=0, keepdims=True)


def block_density(slots, positions, basis, arrived):
    blocks = positions.shape[0]
    rows = basis.shape[0] // blocks
    orbs = basis.shape[1]
    return pl.pallas_call(
        density_kernel,
        in_specs=[
            pl.BlockSpec(memory_space=pltpu.SMEM),
            pl.BlockSpec(memory_space=pltpu.SMEM),
            pl.BlockSpec(memory_space=pltpu.VMEM),
            pl.BlockSpec(memory_space=pl.ANY),
        ],
        out_specs=pl.BlockSpec(memory_space=pltpu.VMEM),
        out_shape=jax.ShapeDtypeStruct((blocks, rows), jnp.float32),
        scratch_shapes=[
            pltpu.VMEM((blocks, orbs, orbs), basis.dtype),
            pltpu.SemaphoreType.DMA((positions.size,)),
        ],
        compiler_params=params(),
        name="block_density",
    )(slots, positions, basis, arrived)


def field_kernel(
    kept, counts, slots, positions, first, raw, source, basis, field, tiles_out, feats, column, scaled, staged, sems
):
    blocks, pairs = positions.shape
    rows = raw.shape[1]
    tile = tiles_out.shape[1]
    kt = basis.shape[1] // tile
    weights = source[:, 0]
    density, omega, kappa = point_features(raw[...], source[:, 1])
    feats[0] = weights * density
    feats[1] = omega
    feats[2] = kappa
    for axis in range(3):
        feats[3 + axis] = source[:, 2 + axis]

    def send(b, k):
        return pltpu.make_async_copy(
            staged.at[b * pairs + k], tiles_out.at[slots[b * pairs + k]], sems.at[b * pairs + k]
        )

    for b in range(blocks):
        at = first[0] + b
        for f in range(5):
            row = feats[1 + f, pl.ds(at, 1), :]
            column[f] = jnp.broadcast_to(row, (rows, rows)).T

        def one_source(j, total):
            s = kept[b, j]
            r2 = None
            for axis in range(3):
                gap = column[2 + axis] - feats[3 + axis, pl.ds(s, 1), :]
                r2 = gap * gap if r2 is None else r2 + gap * gap
            g = column[0] * r2 + column[1]
            h = feats[1, pl.ds(s, 1), :] * r2 + feats[2, pl.ds(s, 1), :]
            phi = -1.5 / (g * h * (g + h))
            return total + phi * feats[0, pl.ds(s, 1), :]

        total = lax.fori_loop(0, counts[b], one_source, jnp.zeros((rows, rows), jnp.float32))
        potential = jnp.sum(total, axis=1, keepdims=True)
        wide = jnp.broadcast_to(potential, (rows, rows))
        field[b : b + 1, :] = wide.T[0:1, :]
        weight = jnp.broadcast_to(source[pl.ds(at, 1), 0], (rows, rows)).T
        factor = weight * wide
        for m in range(kt):
            chi = basis[b * rows : (b + 1) * rows, m * tile : (m + 1) * tile]
            scaled[m] = (chi.astype(jnp.float32) * factor).astype(jnp.bfloat16).T
            scaled[kt + m] = chi

        @pl.loop(0, pairs)
        def _(k):
            q = positions[b, k]
            product = jnp.dot(
                scaled[q // kt], scaled[kt + q % kt], preferred_element_type=jnp.float32
            )
            staged[b * pairs + k] = product.astype(jnp.bfloat16)
            send(b, k).start()

    for b in range(blocks):

        @pl.loop(0, pairs)
        def _(k):
            send(b, k).wait()


def field_and_tiles(kept, counts, slots, positions, first, raw, source, basis, slot_count):
    blocks, pairs = positions.shape
    total, rows = raw.shape
    tile = 128
    kt = basis.shape[1] // tile
    smem = pl.BlockSpec(memory_space=pltpu.SMEM)
    vmem = pl.BlockSpec(memory_space=pltpu.VMEM)
    return pl.pallas_call(
        field_kernel,
        in_specs=[smem] * 5 + [vmem] * 3,
        out_specs=[vmem, pl.BlockSpec(memory_space=pl.ANY)],
        out_shape=[
            jax.ShapeDtypeStruct((blocks, rows), jnp.float32),
            jax.ShapeDtypeStruct((slot_count, tile, tile), jnp.bfloat16),
        ],
        scratch_shapes=[
            pltpu.VMEM((6, total, rows), jnp.float32),
            pltpu.VMEM((5, rows, rows), jnp.float32),
            pltpu.VMEM((2 * kt, tile, rows), jnp.bfloat16),
            pltpu.VMEM((blocks * pairs, tile, tile), jnp.bfloat16),
            pltpu.SemaphoreType.DMA((blocks * pairs,)),
        ],
        compiler_params=params(),
        name="field_and_tiles",
    )(kept, counts, slots, positions, first, raw, source, basis)


def collect_kernel(order, starts, landed, out):
    step = pl.program_id(0)
    width = out.shape[0]

    @pl.loop(0, width)
    def _(t):
        g = step * width + t

        def add(j, total):
            return total + landed[order[j]].astype(jnp.float32)

        out[t] = lax.fori_loop(
            starts[g], starts[g + 1], add, jnp.zeros(out.shape[1:], jnp.float32)
        )


def collect_tiles(order, starts, landed, store_count):
    tile = landed.shape[1]
    group = 8
    smem = pl.BlockSpec(memory_space=pltpu.SMEM)
    return pl.pallas_call(
        collect_kernel,
        grid=(store_count // group,),
        in_specs=[smem, smem, pl.BlockSpec(memory_space=pltpu.VMEM)],
        out_specs=pl.BlockSpec((group, tile, tile), lambda i: (i, 0, 0)),
        out_shape=jax.ShapeDtypeStruct((store_count, tile, tile), jnp.float32),
        compiler_params=params(),
        name="collect_tiles",
    )(order, starts, landed)


def kept_list(keep):
    width = keep.shape[1]
    places = jnp.arange(width, dtype=jnp.int32)
    rank = jnp.cumsum(keep, axis=1) - keep
    hit = (rank[:, :, None] == places[None, None, :]) & (keep[:, :, None] > 0)
    return (
        jnp.sum(jnp.where(hit, places[None, :, None], 0), axis=1),
        jnp.sum(keep, axis=1),
    )


def slot_order(asked, positions, store_count):
    count = asked.shape[0]
    places = jnp.arange(count, dtype=jnp.int32)
    key = jnp.where(asked >= 0, asked, store_count) * count + places
    rank = jnp.sum((key[None, :] < key[:, None]).astype(jnp.int32), axis=1)
    order = jnp.sum(jnp.where(rank[:, None] == places[None, :], positions[:, None], 0), axis=0)
    stores = jnp.arange(store_count + 1, dtype=jnp.int32)
    starts = jnp.sum(
        ((asked[None, :] >= 0) & (asked[None, :] < stores[:, None])).astype(jnp.int32), axis=1
    )
    return order, starts


def body(basis, dmat, tile_home, pair_tiles, pair_pos, coords, weights, grad_sq, pair_keep):
    peers = lax.axis_size(AXES)
    me = lax.axis_index(AXES)
    blocks, pairs = pair_tiles.shape
    store_count, tile = dmat.shape[0], dmat.shape[1]
    rows = basis.shape[0] // blocks
    kt = basis.shape[1] // tile
    capacity = 2
    slot_count = peers * capacity
    wanted = tile_home[pair_tiles.reshape(-1)]
    owner = wanted // store_count
    within = wanted % store_count
    same = owner[:, None] == owner[None, :]
    places = jnp.arange(blocks * pairs, dtype=jnp.int32)
    earlier = jnp.sum((same & (places[None, :] < places[:, None])).astype(jnp.int32), axis=1)
    slots = owner * capacity + earlier
    devices = jnp.arange(peers, dtype=jnp.int32)
    lanes = jnp.arange(tile, dtype=jnp.int32)
    held = owner[:, None] == devices[None, :]
    entry = jnp.where(
        held[:, :, None] & (earlier[:, None] == lanes[None, :])[:, None, :],
        within[:, None, None] + 1,
        0,
    )
    named = jnp.sum(held.astype(jnp.int32), axis=0)
    asking = jnp.stack(
        [jnp.sum(entry, axis=0), jnp.broadcast_to(named[None, :], (peers, tile))], axis=1
    )
    even_me = parity(me.astype(jnp.int32))
    relayed = (earlier == 1) & (parity(owner) != even_me)
    spot = pair_pos[:, :, None] == jnp.arange(kt * kt, dtype=jnp.int32)[None, None, :]
    found = jnp.where(relayed, 2 * slot_count + owner, slots).reshape(blocks, pairs)
    table = (
        jnp.sum(jnp.where(spot, found[:, :, None] - slot_count, 0), axis=1) + slot_count
    )
    product_at = pair_pos + kt * kt * jnp.arange(blocks, dtype=jnp.int32)[:, None]
    mine = jnp.sum(
        jnp.where(
            slots[:, None] == jnp.arange(slot_count, dtype=jnp.int32)[None, :],
            product_at.reshape(-1)[:, None],
            0,
        ),
        axis=0,
    )

    local = jnp.concatenate([weights[None], grad_sq[None], coords], axis=0)
    local = local.reshape(5, blocks, rows).transpose(1, 0, 2)
    source = lax.all_gather(local, AXES, axis=0, tiled=True)
    keep = lax.dynamic_slice_in_dim(pair_keep, me * blocks, blocks, 0)
    kept, counts = kept_list(keep)
    first = (me * blocks).astype(jnp.int32).reshape(1)

    asked, plan, raw = fetch_and_density(asking, table, dmat, basis)
    raw = raw.reshape(peers * blocks, rows)
    asked = asked[:, 0, :capacity].reshape(-1) - 1

    def two_slots():
        shape = (peers, capacity, tile, tile)

        def exchange(values):
            return lax.all_to_all(
                values.reshape(shape), AXES, split_axis=0, concat_axis=0, tiled=True
            ).reshape(slot_count, tile, tile)

        arrived = exchange(pick_tiles(asked, dmat))
        again = block_density(slots, pair_pos, basis, arrived)
        again = lax.all_gather(again, AXES, axis=0, tiled=True)
        field, returning = field_and_tiles(
            kept, counts, slots, pair_pos, first, again, source, basis, slot_count
        )
        order, starts = slot_order(
            asked, jnp.arange(slot_count, dtype=jnp.int32), store_count
        )
        return collect_tiles(order, starts, exchange(returning), store_count), field

    def relays():
        field, factor = field_only(kept, counts, first, raw, source, blocks)
        wide = parity(devices) == even_me
        seconds = jnp.where(wide, peers + devices, 2 * peers + plan[AT_BACK])
        places = jnp.stack([devices, seconds], axis=1).reshape(-1)
        order, starts = slot_order(asked, places, store_count)
        land = return_tiles(plan, mine, factor, basis, peers)
        return collect_tiles(order, starts, land, store_count), field

    pieces, field = lax.cond(jnp.sum(plan[AT_LEFT]) > 0, two_slots, relays)
    return pieces, field.reshape(-1)


def solution(mesh):
    in_specs = (
        P(AXES, None),
        P(AXES, None, None),
        P(),
        P(AXES, None),
        P(AXES, None),
        P(None, AXES),
        P(AXES),
        P(AXES),
        P(),
    )
    out_specs = (P(AXES, None, None), P(AXES))
    return jax.shard_map(body, mesh=mesh, in_specs=in_specs, out_specs=out_specs, check_vma=False)
```

```python
import functools

import jax
import jax.numpy as jnp
from jax import lax
from jax.experimental import pallas as pl
from jax.experimental.pallas import tpu as pltpu
from jax.sharding import PartitionSpec as P

gradient_coef = 0.0093
kappa_coef = 6.3
density_floor = 0.1
AXES = ("row", "col")
VMEM_LIMIT = 56 * 2**20
MESH = pl.DeviceIdType.MESH
STRIDE = 7
STEPS = (
    (0, 0, 0, 1),
    (0, 1, 0, 0),
    (1, 0, 0, 0),
    (0, 0, 1, 0),
    (0, 3, 0, 0),
    (3, 0, 0, 0),
    (0, 0, 3, 0),
    (0, 1, 1, 1),
    (1, 0, 1, 1),
    (1, 1, 0, 1),
    (0, 3, 3, 1),
    (3, 0, 3, 1),
    (3, 3, 0, 1),
    (0, 1, 3, 1),
    (1, 0, 3, 1),
    (1, 3, 0, 1),
)
ROOM = (56, 8, 8, 8, 4, 4, 4) + (1,) * 9
BASE = tuple(sum(ROOM[:k]) for k in range(len(ROOM)))
LINKS = len(ROOM)
RELAYED = sum(ROOM)
AT_LOC, AT_SRC, AT_CODE, AT_LEFT, AT_STARTS = range(2 * LINKS, 2 * LINKS + 5)
AT_TABLE, AT_MINE, AT_ORDER = 2 * LINKS + 5, 2 * LINKS + 7, 2 * LINKS + 9
AT_KEPT = 2 * LINKS + 11
AT_COUNTS = AT_KEPT + 16
PLAN_ROWS = AT_COUNTS + 5


def point_features(raw_density, grad_sq):
    density = jnp.maximum(raw_density, 0.0) + jnp.log1p(jnp.exp(-jnp.abs(raw_density))) + density_floor
    ratio = grad_sq / (density * density)
    omega_zero = jnp.sqrt(gradient_coef * ratio * ratio + 4.0 * jnp.pi / 3.0 * density)
    kappa_point = kappa_coef * 1.5 * jnp.pi * jnp.exp(jnp.log(density / (9.0 * jnp.pi)) * (1.0 / 6.0))
    return density, omega_zero, kappa_point


def params(**more):
    return pltpu.CompilerParams(vmem_limit_bytes=VMEM_LIMIT, **more)


def moved(device, move):
    dy, dx, dz, dc = move
    y = (device // 32 + dy) % 4
    x = (device // 8 + dx) % 4
    z = (device // 2 + dz) % 4
    return y * 32 + x * 8 + z * 2 + (device + dc) % 2


def back(move):
    return tuple((4 - m) % 4 for m in move[:3]) + (move[3],)


def parity(device):
    return (device + device // 2 + device // 8 + device // 32) % 2


def this_device():
    return lax.axis_index("row") * 32 + lax.axis_index("col")


def inside(value, count):
    return jnp.minimum(jnp.maximum(value, 0), count - 1)


def place_of(device):
    return device // 32, lax.rem(device, 32)


def neighbour(step):
    move = (step // 32, lax.rem(step // 8, 4), lax.rem(step // 2, 4), lax.rem(step, 2))
    return moved(this_device(), move)


def narrow_step(turn):
    up = lax.rem(turn * STRIDE, 64)
    return 2 * up + lax.rem(up + up // 4 + up // 16 + 1, 2)


def wide_step(turn):
    up = lax.rem(turn * STRIDE, 64)
    return 2 * up + lax.rem(up + up // 4 + up // 16, 2)


def iotas(peers):
    return (
        lax.broadcasted_iota(jnp.int32, (peers, peers), 0).astype(jnp.float32),
        lax.broadcasted_iota(jnp.int32, (peers, peers), 1).astype(jnp.float32),
    )


def down(row, peers):
    sub, lane = iotas(peers)
    return jnp.sum(jnp.where(sub == lane, row, 0.0), axis=1, keepdims=True)


def across(hit, column):
    return jnp.sum(jnp.where(hit, column, 0.0), axis=0, keepdims=True)


def make_requests(want, asking):
    peers = want.shape[1]
    sub, lane = iotas(peers)
    owner_int = want[...] // 64
    owner = owner_int.astype(jnp.float32)
    within = (want[...] - owner_int * 64).astype(jnp.float32)
    owner_down = down(owner, peers)
    same = owner_down == owner
    rank = across(same & (sub < lane), jnp.ones_like(owner_down))
    columns = [
        jnp.sum(
            jnp.where((owner == sub) & (rank == slot), within + 1.0, 0.0), axis=1, keepdims=True
        )
        for slot in range(2)
    ]
    entries = jnp.where(lane == 0.0, columns[0], jnp.where(lane == 1.0, columns[1], 0.0))
    named = across(owner_down == lane, jnp.ones_like(owner_down))
    asking[:, 0, :] = entries.astype(jnp.int32)
    asking[:, 1, :] = jnp.broadcast_to(named, (peers, peers)).astype(jnp.int32)


def make_tables(want, spots, plan):
    peers = want.shape[1]
    sub, lane = iotas(peers)
    me = this_device()
    owner_int = want[...] // 64
    owner = owner_int.astype(jnp.float32)
    owner_down = down(owner, peers)
    rank = across((owner_down == owner) & (sub < lane), jnp.ones_like(owner_down))
    odd = parity(owner_int) != parity(me)
    found = jnp.where((rank == 1.0) & odd, 4.0 * peers + owner, 2.0 * owner + rank)
    pair = lax.broadcasted_iota(jnp.int32, (1, peers), 1)
    spot = (spots[...] + 64 * (pair // 32)).astype(jnp.float32)
    rank_down, found_down, spot_down = down(rank, peers), down(found, peers), down(spot, peers)
    for half in range(2):
        row = across(spot_down == lane + half * peers, found_down - 2.0 * peers) + 2.0 * peers
        plan[AT_TABLE + half : AT_TABLE + half + 1, :] = row.astype(jnp.int32)
        row = across((owner_down == lane) & (rank_down == half), spot_down)
        plan[AT_MINE + half : AT_MINE + half + 1, :] = row.astype(jnp.int32)


def make_order(entries, again, plan):
    peers = entries.shape[0]
    sub, lane = iotas(peers)
    me = this_device()
    asker = lax.broadcasted_iota(jnp.int32, (peers, 1), 0)
    wide = parity(asker) == parity(me)
    number = asker.astype(jnp.float32)
    asked = [
        jnp.sum(jnp.where(lane == slot, entries, 0.0), axis=1, keepdims=True) for slot in range(2)
    ]
    places = [number, jnp.where(wide, number + peers, again + 2.0 * peers)]
    keys = [
        jnp.where(asked[slot] > 0.0, asked[slot] - 1.0, 64.0) * (2.0 * peers) + 2.0 * number + slot
        for slot in range(2)
    ]
    rows = [across(sub == lane, key) for key in keys]
    ranks = [
        sum(
            jnp.sum(jnp.where(row < key, 1.0, 0.0), axis=1, keepdims=True) for row in rows
        )
        for key in keys
    ]
    for half in range(2):
        row = sum(
            across(ranks[slot] == lane + half * peers, places[slot]) for slot in range(2)
        )
        plan[AT_ORDER + half : AT_ORDER + half + 1, :] = row.astype(jnp.int32)
    row = sum(
        across((asked[slot] > 0.0) & (asked[slot] - 1.0 < lane), jnp.ones_like(number))
        for slot in range(2)
    )
    plan[AT_STARTS : AT_STARTS + 1, :] = row.astype(jnp.int32)


def make_kept(keep, plan):
    blocks = keep.shape[0]
    peers = 128
    sub, lane = iotas(peers)
    parts = keep.shape[1] // peers
    for b in range(blocks):
        before = jnp.zeros((1, 1), jnp.float32)
        ranks = []
        for g in range(parts):
            row = keep[b : b + 1, g * peers : (g + 1) * peers]
            rank = jnp.sum(jnp.where(lane < sub, row, 0.0), axis=1, keepdims=True) + before
            ranks.append(jnp.where(down(row, peers) > 0.0, rank, -1.0))
            before = before + jnp.sum(row, axis=1, keepdims=True)
        for h in range(parts):
            total = jnp.zeros((1, peers), jnp.float32)
            for g in range(parts):
                block = lax.broadcasted_iota(jnp.int32, (peers, 1), 0) + g * peers
                device = block // 4
                place = ((device % 2) * 64 + device // 2) * 4 + block % 4
                total = total + across(ranks[g] == lane + h * peers, place.astype(jnp.float32))
            at = AT_KEPT + parts * b + h
            plan[at : at + 1, :] = total.astype(jnp.int32)
        plan[AT_COUNTS + b : AT_COUNTS + b + 1, :] = jnp.broadcast_to(before, (1, peers)).astype(
            jnp.int32
        )


def greet_all(peers):
    barrier = pltpu.get_barrier_semaphore()
    for step in range(1, peers):
        pl.semaphore_signal(
            barrier, inc=1, device_id=place_of(neighbour(step)), device_id_type=MESH
        )


def wait_all(peers):
    pl.semaphore_wait(pltpu.get_barrier_semaphore(), peers - 1)


def remote(source, target, send, recv, at, device):
    return pltpu.make_async_remote_copy(
        src_ref=source,
        dst_ref=target,
        send_sem=send.at[at],
        recv_sem=recv.at[at],
        device_id=place_of(device),
        device_id_type=MESH,
    )


def make_plan(counts, plan):
    peers = counts.shape[0]
    me = this_device()
    asker = lax.broadcasted_iota(jnp.int32, (peers, peers), 0)
    owner = lax.broadcasted_iota(jnp.int32, (peers, peers), 1)
    wide = parity(asker) == parity(owner)
    zero = jnp.zeros((peers, peers), jnp.float32)
    left = jnp.where(wide | (counts < 2), 0.0, 1.0)
    free = jnp.where(wide & (counts < 2), 1.0, 0.0)
    earlier = jnp.where(owner < asker, 1.0, 0.0).astype(jnp.bfloat16)
    loc, src, code, again = zero, zero, zero, zero

    def dot(a, b):
        return jnp.dot(
            a.astype(jnp.bfloat16), b.astype(jnp.bfloat16), preferred_element_type=jnp.float32
        )

    def mine(values):
        return jnp.sum(jnp.where(owner == me, values, 0.0), axis=1, keepdims=True)

    def by_slot(column):
        hit = column == (owner + 1).astype(jnp.float32)
        return jnp.sum(jnp.where(hit, asker, 0), axis=0, keepdims=True)

    for k in range(LINKS):
        move, home = STEPS[k], back(STEPS[k])
        there = moved(owner, move)
        onto = jnp.where(asker == there, 1.0, 0.0)
        off = jnp.where(owner == moved(asker, move), 1.0, 0.0)
        want = left * dot(free, onto)
        rank = dot(earlier, want)
        numbered = jnp.where((want > 0.0) & (rank < ROOM[k]), rank + 1.0, 0.0)
        relay = dot(numbered, off)
        left = jnp.where(numbered > 0.0, 0.0, left)
        free = jnp.where(relay > 0.0, 0.0, free)
        loc = loc + jnp.where(numbered > 0.0, (2 * there + 1).astype(jnp.float32), 0.0)
        src = src + jnp.where(relay > 0.0, (moved(owner, home) + 1).astype(jnp.float32), 0.0)
        code = code + jnp.where(relay > 0.0, relay + BASE[k], 0.0)
        again = again + jnp.where(numbered > 0.0, numbered + (BASE[k] - 1.0), 0.0)
        plan[k : k + 1, :] = by_slot(mine(numbered))
        plan[LINKS + k : LINKS + k + 1, :] = by_slot(mine(relay))

    def row_of(values):
        return jnp.sum(jnp.where(asker == me, values, 0.0), axis=0, keepdims=True)

    def turned(values):
        return jnp.sum(jnp.where(asker == owner, mine(values), 0.0), axis=0, keepdims=True)

    plan[AT_LOC : AT_LOC + 1, :] = row_of(loc).astype(jnp.int32)
    plan[AT_SRC : AT_SRC + 1, :] = row_of(src).astype(jnp.int32)
    plan[AT_CODE : AT_CODE + 1, :] = turned(code).astype(jnp.int32)
    unplaced = jnp.sum(jnp.sum(left, axis=1, keepdims=True), axis=0, keepdims=True)
    plan[AT_LEFT : AT_LEFT + 1, :] = jnp.broadcast_to(unplaced, (1, peers)).astype(jnp.int32)
    plan[AT_COUNTS + 4 :, :] = jnp.zeros((PLAN_ROWS - AT_COUNTS - 4, peers), jnp.int32)
    return mine(again)


def fetch_kernel(
    home,
    pair_tiles,
    spots,
    pair_keep,
    weights,
    grad_sq,
    coords,
    tiles,
    basis,
    asked,
    plan,
    raw_all,
    source_all,
    wanted,
    route,
    want_smem,
    want,
    asking,
    keep,
    local,
    stage,
    arrived,
    link_out,
    link_in,
    dense,
    own_sems,
    ask_send,
    ask_recv,
    first_send,
    first_recv,
    second_send,
    second_recv,
    link_send,
    link_recv,
    share_send,
    share_recv,
    raw_send,
    raw_recv,
):
    peers = asked.shape[0]
    chips = peers // 2
    blocks, pairs = pair_tiles.shape
    orbs = basis.shape[1]
    rows = basis.shape[0] // blocks
    tile = tiles.shape[1]
    kt = orbs // tile
    me = this_device()
    chip, core = me // 2, lax.rem(me, 2)
    partner = 2 * chip + 1 - core

    def ask(step):
        to = neighbour(step)
        return remote(asking.at[to], asked.at[me], ask_send, ask_recv, step, to)

    def first(step):
        to = neighbour(step)
        return remote(stage.at[to, 0], arrived.at[me, 0], first_send, first_recv, step, to)

    def second(step):
        to = neighbour(step)
        return remote(stage.at[to, 1], arrived.at[me, 1], second_send, second_recv, step, to)

    def link(k):
        part = pl.ds(BASE[k], ROOM[k])
        return remote(
            link_out.at[part], link_in.at[part], link_send, link_recv, k, moved(me, STEPS[k])
        )

    def share(up):
        to = neighbour(2 * up)
        return remote(local, source_all.at[:, core, chip], share_send, share_recv, up, to)

    def share_on():
        part = source_all.at[:, core]
        return remote(part, part, share_send, share_recv, 0, partner)

    def tell_partner():
        part = raw_all.at[core, chip]
        return remote(part, part, raw_send, raw_recv, 0, partner)

    def tell(up):
        part = raw_all.at[:, chip]
        return remote(part, part, raw_send, raw_recv, up, neighbour(2 * up))

    def tile_for(device, slot):
        return tiles[inside(wanted[inside(device, peers), 0, slot] - 1, tiles.shape[0])]

    def second_for(device):
        at = route[AT_CODE, device]
        return jnp.where(at > 0, link_in[inside(at - 1, RELAYED)], tile_for(device, 1))

    def move(source, target, at):
        copy = pltpu.make_async_copy(source, target, own_sems.at[at])
        copy.start()
        return copy

    greet_all(peers)
    pair = lax.div(me, 2)
    keep_copy = move(pair_keep.at[pl.ds(pl.multiple_of(8 * pair, 8), 8)], keep, 0)

    for b in range(blocks):

        @pl.loop(0, pairs)
        def _(j):
            want_smem[0, b * pairs + j] = home[inside(pair_tiles[b, j], home.shape[0])]

    move(want_smem, want, 1).wait()
    make_requests(want, asking)
    local[0] = weights[...]
    local[1] = grad_sq[...]
    for axis in range(3):
        for b in range(blocks):
            local[2 + axis, b : b + 1, :] = coords[axis : axis + 1, b * rows : (b + 1) * rows]
    wait_all(peers)

    @pl.loop(1, peers)
    def _(step):
        ask(step).start()

    @pl.loop(1, chips)
    def _(up):
        share(up).start()

    asked[me] = asking[me]
    source_all[:, core, chip] = local[...]
    arrived[peers] = jnp.zeros(arrived.shape[1:], arrived.dtype)

    @pl.loop(1, peers)
    def _(step):
        ask(step).wait()

    move(asked, wanted, 2).wait()

    @pl.loop(0, 64)
    def _(turn):
        step = narrow_step(turn)
        to = neighbour(step)
        stage[to, 0] = tile_for(to, 0)
        first(step).start()

    again = make_plan(asked[:, 1, :], plan)
    move(plan, route, 3).wait()

    for k in range(LINKS):

        @pl.loop(0, ROOM[k])
        def _(s):
            link_out[BASE[k] + s] = tile_for(route[k, s], 1)

        link(k).start()

    @pl.loop(1, 64)
    def _(turn):
        step = wide_step(turn)
        to = neighbour(step)
        stage[to, 0] = tile_for(to, 0)
        first(step).start()

    arrived[me, 0] = tile_for(me, 0)

    for k in range(LINKS):
        link(k).wait()

    @pl.loop(1, 64)
    def _(turn):
        step = wide_step(turn)
        to = neighbour(step)
        stage[to, 1] = second_for(to)
        second(step).start()

    arrived[me, 1] = second_for(me)

    @pl.loop(1, chips)
    def _(up):
        share(up).wait()

    share_on().start()
    make_tables(want, spots, plan)
    make_order(asked[:, 0, :].astype(jnp.float32), again, plan)
    keep_copy.wait()
    kept = jnp.where(core == 0, keep[0:4, :], keep[4:8, :]).astype(jnp.float32)
    make_kept(kept, plan)
    move(plan, route, 4).wait()

    @pl.loop(1, peers)
    def _(step):
        first(step).wait()

    @pl.loop(1, 64)
    def _(turn):
        second(wide_step(turn)).wait()

    for b in range(blocks):

        @pl.loop(0, kt)
        def _(row):
            for column in range(kt):
                q = b * kt * kt + row * kt + column
                slot = route[AT_TABLE + q // peers, lax.rem(q, peers)]
                slot = jnp.where(
                    slot >= 4 * peers, route[AT_LOC, inside(slot - 4 * peers, peers)], slot
                )
                slot = inside(slot, 2 * peers + 1)
                dense[
                    b % 2,
                    pl.ds(pl.multiple_of(row * tile, tile), tile),
                    column * tile : (column + 1) * tile,
                ] = arrived[slot // 2, lax.rem(slot, 2)]

        chi = basis[b * rows : (b + 1) * rows, :]
        mixed = jnp.dot(chi, dense[b % 2], preferred_element_type=jnp.float32)
        both = mixed * chi.astype(jnp.float32)
        part = both[:, :tile]
        for m in range(1, kt):
            part = part + both[:, m * tile : (m + 1) * tile]
        raw_all[core, chip, b : b + 1, :] = jnp.sum(part.T, axis=0, keepdims=True)

    tell_partner().start()
    share_on().wait()
    tell_partner().wait()

    @pl.loop(1, chips)
    def _(up):
        tell(up).start()

    @pl.loop(1, chips)
    def _(up):
        tell(up).wait()


def fetch_and_density(home, pair_tiles, spots, pair_keep, weights, grad_sq, coords, tiles, basis):
    blocks, pairs = pair_tiles.shape
    tile = tiles.shape[1]
    peers = blocks * pairs
    rows = basis.shape[0] // blocks
    orbs = basis.shape[1]
    smem = pl.BlockSpec(memory_space=pltpu.SMEM)
    vmem = pl.BlockSpec(memory_space=pltpu.VMEM)
    pair = pltpu.SemaphoreType.DMA((peers,))
    half = pltpu.SemaphoreType.DMA((peers // 2,))
    return pl.pallas_call(
        fetch_kernel,
        in_specs=[smem, smem, vmem, pl.BlockSpec(memory_space=pl.ANY)] + [vmem] * 5,
        out_specs=[vmem, vmem, vmem, vmem],
        out_shape=[
            jax.ShapeDtypeStruct((peers, 2, peers), jnp.int32),
            jax.ShapeDtypeStruct((PLAN_ROWS, peers), jnp.int32),
            jax.ShapeDtypeStruct((2, peers // 2, blocks, rows), jnp.float32),
            jax.ShapeDtypeStruct((5, 2, peers // 2, blocks, rows), jnp.float32),
        ],
        scratch_shapes=[
            pltpu.SMEM((peers, 2, peers), jnp.int32),
            pltpu.SMEM((PLAN_ROWS, peers), jnp.int32),
            pltpu.SMEM((1, peers), jnp.int32),
            pltpu.VMEM((1, peers), jnp.int32),
            pltpu.VMEM((peers, 2, peers), jnp.int32),
            pltpu.VMEM((8, pair_keep.shape[1]), jnp.int32),
            pltpu.VMEM((5, blocks, rows), jnp.float32),
            pltpu.VMEM((peers, 2, tile, tile), tiles.dtype),
            pltpu.VMEM((peers + 1, 2, tile, tile), tiles.dtype),
            pltpu.VMEM((RELAYED, tile, tile), tiles.dtype),
            pltpu.VMEM((RELAYED, tile, tile), tiles.dtype),
            pltpu.VMEM((2, orbs, orbs), basis.dtype),
            pltpu.SemaphoreType.DMA((5,)),
            pair,
            pair,
            pair,
            pair,
            pair,
            pair,
            pltpu.SemaphoreType.DMA((LINKS,)),
            pltpu.SemaphoreType.DMA((LINKS,)),
            half,
            half,
            half,
            half,
        ],
        compiler_params=params(collective_id=0, has_side_effects=True),
        name="fetch_and_density",
    )(home, pair_tiles, spots, pair_keep, weights, grad_sq, coords, tiles, basis)


def field_only_kernel(plan, raw, source, field, factor, feats, column):
    blocks, rows = field.shape
    me = this_device()
    start = (lax.rem(me, 2) * 64 + me // 2) * blocks
    weights = source[0]
    density, omega, kappa = point_features(raw[...], source[1])
    feats[0] = weights * density
    feats[1] = omega
    feats[2] = kappa
    for axis in range(3):
        feats[3 + axis] = source[2 + axis]

    for b in range(blocks):
        at = start + b
        for f in range(5):
            row = feats[1 + f, pl.ds(at, 1), :]
            column[f] = jnp.broadcast_to(row, (rows, rows)).T

        def one_source(j, total):
            s = plan[AT_KEPT + 4 * b + j // rows, lax.rem(j, rows)]
            r2 = None
            for axis in range(3):
                gap = column[2 + axis] - feats[3 + axis, pl.ds(s, 1), :]
                r2 = gap * gap if r2 is None else r2 + gap * gap
            g = column[0] * r2 + column[1]
            h = feats[1, pl.ds(s, 1), :] * r2 + feats[2, pl.ds(s, 1), :]
            phi = -1.5 / (g * h * (g + h))
            return total + phi * feats[0, pl.ds(s, 1), :]

        total = lax.fori_loop(0, plan[AT_COUNTS + b, 0], one_source, jnp.zeros((rows, rows), jnp.float32))
        wide = jnp.broadcast_to(jnp.sum(total, axis=1, keepdims=True), (rows, rows))
        field[b : b + 1, :] = wide.T[0:1, :]
        weight = jnp.broadcast_to(source[0, pl.ds(at, 1), :], (rows, rows)).T
        factor[b * rows : (b + 1) * rows, :] = weight * wide


def field_only(plan, raw, source, blocks):
    total, rows = raw.shape
    smem = pl.BlockSpec(memory_space=pltpu.SMEM)
    vmem = pl.BlockSpec(memory_space=pltpu.VMEM)
    return pl.pallas_call(
        field_only_kernel,
        in_specs=[smem, vmem, vmem],
        out_specs=[vmem, vmem],
        out_shape=[
            jax.ShapeDtypeStruct((blocks, rows), jnp.float32),
            jax.ShapeDtypeStruct((blocks * rows, rows), jnp.float32),
        ],
        scratch_shapes=[
            pltpu.VMEM((6, total, rows), jnp.float32),
            pltpu.VMEM((5, rows, rows), jnp.float32),
        ],
        compiler_params=params(),
        name="field_only",
    )(plan, raw, source)


def return_kernel(
    route,
    factor,
    basis,
    land,
    seconds,
    products,
    stage,
    link_out,
    scaled,
    own_sems,
    first_send,
    first_recv,
    second_send,
    second_recv,
    link_send,
    link_recv,
):
    peers = route.shape[1]
    tile = land.shape[1]
    kt = basis.shape[1] // tile
    rows = tile
    blocks = basis.shape[0] // rows
    me = this_device()

    def first(step):
        to = neighbour(step)
        return remote(stage.at[to, 0], land.at[me], first_send, first_recv, step, to)

    def second(step):
        to = neighbour(step)
        return remote(stage.at[to, 1], seconds.at[me], second_send, second_recv, step, to)

    def link(k):
        return remote(
            link_out.at[pl.ds(BASE[k], ROOM[k])],
            land.at[pl.ds(2 * peers + BASE[k], ROOM[k])],
            link_send,
            link_recv,
            k,
            moved(me, back(STEPS[k])),
        )

    def product_for(device, slot):
        return products[inside(route[AT_MINE + slot, device], 2 * peers)]

    def second_for(device):
        via = route[AT_SRC, device]
        holder = inside(jnp.where(via > 0, via - 1, device), peers)
        return product_for(holder, 1)

    greet_all(peers)

    @pl.loop(0, blocks)
    def _(b):
        chi = basis[pl.ds(pl.multiple_of(b * rows, rows), rows), :]
        by = factor[pl.ds(pl.multiple_of(b * rows, rows), rows), :]
        for m in range(kt):
            part = chi[:, m * tile : (m + 1) * tile].astype(jnp.float32) * by
            scaled[...] = part.astype(jnp.bfloat16).T
            product = jnp.dot(scaled[...], chi, preferred_element_type=jnp.float32)
            for n in range(kt):
                products[b * kt * kt + m * kt + n] = product[
                    :, n * tile : (n + 1) * tile
                ].astype(jnp.bfloat16)

    wait_all(peers)

    @pl.loop(1, 64)
    def _(turn):
        step = wide_step(turn)
        to = neighbour(step)
        stage[to, 1] = second_for(to)
        second(step).start()

    seconds[me] = second_for(me)
    stage[me, 0] = product_for(me, 0)
    own = pltpu.make_async_copy(stage.at[me, 0], land.at[me], own_sems.at[0])
    own.start()

    @pl.loop(0, 64)
    def _(turn):
        step = narrow_step(turn)
        to = neighbour(step)
        stage[to, 0] = product_for(to, 0)
        first(step).start()

    @pl.loop(1, 64)
    def _(turn):
        second(wide_step(turn)).wait()

    for k in range(LINKS):

        @pl.loop(0, ROOM[k])
        def _(s):
            link_out[BASE[k] + s] = seconds[inside(route[LINKS + k, s], peers)]

        link(k).start()

    keep = pltpu.make_async_copy(seconds, land.at[pl.ds(peers, peers)], own_sems.at[1])
    keep.start()

    @pl.loop(1, 64)
    def _(turn):
        step = wide_step(turn)
        to = neighbour(step)
        stage[to, 0] = product_for(to, 0)
        first(step).start()

    for k in range(LINKS):
        link(k).wait()

    @pl.loop(1, peers)
    def _(step):
        first(step).wait()

    own.wait()
    keep.wait()


def return_tiles(plan, factor, basis):
    peers = plan.shape[1]
    tile = 128
    smem = pl.BlockSpec(memory_space=pltpu.SMEM)
    vmem = pl.BlockSpec(memory_space=pltpu.VMEM)
    pair = pltpu.SemaphoreType.DMA((peers,))
    return pl.pallas_call(
        return_kernel,
        in_specs=[smem, vmem, vmem],
        out_specs=pl.BlockSpec(memory_space=pl.ANY),
        out_shape=jax.ShapeDtypeStruct((2 * peers + RELAYED, tile, tile), jnp.bfloat16),
        scratch_shapes=[
            pltpu.VMEM((peers, tile, tile), jnp.bfloat16),
            pltpu.VMEM((2 * peers, tile, tile), jnp.bfloat16),
            pltpu.VMEM((peers, 2, tile, tile), jnp.bfloat16),
            pltpu.VMEM((RELAYED, tile, tile), jnp.bfloat16),
            pltpu.VMEM((tile, tile), jnp.bfloat16),
            pltpu.SemaphoreType.DMA((2,)),
            pair,
            pair,
            pair,
            pair,
            pltpu.SemaphoreType.DMA((LINKS,)),
            pltpu.SemaphoreType.DMA((LINKS,)),
        ],
        compiler_params=params(collective_id=1, has_side_effects=True),
        name="return_tiles",
    )(plan, factor, basis)


def pick_kernel(asked, tiles, out):
    step = pl.program_id(0)
    width = out.shape[0]

    @pl.loop(0, width)
    def _(slot):
        wanted = asked[step * width + slot]

        @pl.when(wanted >= 0)
        def _():
            out[slot] = tiles[wanted]


def pick_tiles(asked, tiles):
    count = asked.shape[0]
    group = 32
    return pl.pallas_call(
        pick_kernel,
        grid=(count // group,),
        in_specs=[
            pl.BlockSpec(memory_space=pltpu.SMEM),
            pl.BlockSpec(memory_space=pltpu.VMEM),
        ],
        out_specs=pl.BlockSpec((group,) + tiles.shape[1:], lambda i: (i, 0, 0)),
        out_shape=jax.ShapeDtypeStruct((count,) + tiles.shape[1:], tiles.dtype),
        compiler_params=params(),
        name="pick_tiles",
    )(asked, tiles)


def density_kernel(slots, positions, basis, arrived, raw, dense, sems):
    blocks, pairs = positions.shape
    rows = basis.shape[0] // blocks
    orbs = basis.shape[1]
    tile = arrived.shape[1]
    kt = orbs // tile

    dense[...] = jnp.zeros_like(dense)

    def fetch(b, k):
        q = positions[b, k]
        left = pl.multiple_of((q // kt) * tile, tile)
        right = pl.multiple_of((q % kt) * tile, tile)
        return pltpu.make_async_copy(
            arrived.at[slots[b * pairs + k]],
            dense.at[b, pl.ds(left, tile), pl.ds(right, tile)],
            sems.at[b * pairs + k],
        )

    for b in range(blocks):

        @pl.loop(0, pairs)
        def _(k):
            fetch(b, k).start()

    for b in range(blocks):

        @pl.loop(0, pairs)
        def _(k):
            fetch(b, k).wait()

        chi = basis[b * rows : (b + 1) * rows, :]
        mixed = jnp.dot(chi, dense[b], preferred_element_type=jnp.float32)
        both = mixed * chi.astype(jnp.float32)
        part = both[:, :tile]
        for m in range(1, kt):
            part = part + both[:, m * tile : (m + 1) * tile]
        raw[b : b + 1, :] = jnp.sum(part.T, axis=0, keepdims=True)


def block_density(slots, positions, basis, arrived):
    blocks = positions.shape[0]
    rows = basis.shape[0] // blocks
    orbs = basis.shape[1]
    return pl.pallas_call(
        density_kernel,
        in_specs=[
            pl.BlockSpec(memory_space=pltpu.SMEM),
            pl.BlockSpec(memory_space=pltpu.SMEM),
            pl.BlockSpec(memory_space=pltpu.VMEM),
            pl.BlockSpec(memory_space=pl.ANY),
        ],
        out_specs=pl.BlockSpec(memory_space=pltpu.VMEM),
        out_shape=jax.ShapeDtypeStruct((blocks, rows), jnp.float32),
        scratch_shapes=[
            pltpu.VMEM((blocks, orbs, orbs), basis.dtype),
            pltpu.SemaphoreType.DMA((positions.size,)),
        ],
        compiler_params=params(),
        name="block_density",
    )(slots, positions, basis, arrived)


def field_kernel(
    kept, counts, slots, positions, first, raw, source, basis, field, tiles_out, feats, column, scaled, staged, sems
):
    blocks, pairs = positions.shape
    rows = raw.shape[1]
    tile = tiles_out.shape[1]
    kt = basis.shape[1] // tile
    weights = source[:, 0]
    density, omega, kappa = point_features(raw[...], source[:, 1])
    feats[0] = weights * density
    feats[1] = omega
    feats[2] = kappa
    for axis in range(3):
        feats[3 + axis] = source[:, 2 + axis]

    def send(b, k):
        return pltpu.make_async_copy(
            staged.at[b * pairs + k], tiles_out.at[slots[b * pairs + k]], sems.at[b * pairs + k]
        )

    for b in range(blocks):
        at = first[0] + b
        for f in range(5):
            row = feats[1 + f, pl.ds(at, 1), :]
            column[f] = jnp.broadcast_to(row, (rows, rows)).T

        def one_source(j, total):
            s = kept[b, j]
            r2 = None
            for axis in range(3):
                gap = column[2 + axis] - feats[3 + axis, pl.ds(s, 1), :]
                r2 = gap * gap if r2 is None else r2 + gap * gap
            g = column[0] * r2 + column[1]
            h = feats[1, pl.ds(s, 1), :] * r2 + feats[2, pl.ds(s, 1), :]
            phi = -1.5 / (g * h * (g + h))
            return total + phi * feats[0, pl.ds(s, 1), :]

        total = lax.fori_loop(0, counts[b], one_source, jnp.zeros((rows, rows), jnp.float32))
        potential = jnp.sum(total, axis=1, keepdims=True)
        wide = jnp.broadcast_to(potential, (rows, rows))
        field[b : b + 1, :] = wide.T[0:1, :]
        weight = jnp.broadcast_to(source[pl.ds(at, 1), 0], (rows, rows)).T
        factor = weight * wide
        for m in range(kt):
            chi = basis[b * rows : (b + 1) * rows, m * tile : (m + 1) * tile]
            scaled[m] = (chi.astype(jnp.float32) * factor).astype(jnp.bfloat16).T
            scaled[kt + m] = chi

        @pl.loop(0, pairs)
        def _(k):
            q = positions[b, k]
            product = jnp.dot(
                scaled[q // kt], scaled[kt + q % kt], preferred_element_type=jnp.float32
            )
            staged[b * pairs + k] = product.astype(jnp.bfloat16)
            send(b, k).start()

    for b in range(blocks):

        @pl.loop(0, pairs)
        def _(k):
            send(b, k).wait()


def field_and_tiles(kept, counts, slots, positions, first, raw, source, basis, slot_count):
    blocks, pairs = positions.shape
    total, rows = raw.shape
    tile = 128
    kt = basis.shape[1] // tile
    smem = pl.BlockSpec(memory_space=pltpu.SMEM)
    vmem = pl.BlockSpec(memory_space=pltpu.VMEM)
    return pl.pallas_call(
        field_kernel,
        in_specs=[smem] * 5 + [vmem] * 3,
        out_specs=[vmem, pl.BlockSpec(memory_space=pl.ANY)],
        out_shape=[
            jax.ShapeDtypeStruct((blocks, rows), jnp.float32),
            jax.ShapeDtypeStruct((slot_count, tile, tile), jnp.bfloat16),
        ],
        scratch_shapes=[
            pltpu.VMEM((6, total, rows), jnp.float32),
            pltpu.VMEM((5, rows, rows), jnp.float32),
            pltpu.VMEM((2 * kt, tile, rows), jnp.bfloat16),
            pltpu.VMEM((blocks * pairs, tile, tile), jnp.bfloat16),
            pltpu.SemaphoreType.DMA((blocks * pairs,)),
        ],
        compiler_params=params(),
        name="field_and_tiles",
    )(kept, counts, slots, positions, first, raw, source, basis)


def collect_kernel(order, starts, landed, out):
    step = pl.program_id(0)
    width = out.shape[0]

    @pl.loop(0, width)
    def _(t):
        g = step * width + t

        def add(j, total):
            return total + landed[order[j]].astype(jnp.float32)

        out[t] = lax.fori_loop(
            starts[g], starts[g + 1], add, jnp.zeros(out.shape[1:], jnp.float32)
        )


def collect_tiles(order, starts, landed, store_count):
    tile = landed.shape[1]
    group = 8
    smem = pl.BlockSpec(memory_space=pltpu.SMEM)
    return pl.pallas_call(
        collect_kernel,
        grid=(store_count // group,),
        in_specs=[smem, smem, pl.BlockSpec(memory_space=pltpu.VMEM)],
        out_specs=pl.BlockSpec((group, tile, tile), lambda i: (i, 0, 0)),
        out_shape=jax.ShapeDtypeStruct((store_count, tile, tile), jnp.float32),
        compiler_params=params(),
        name="collect_tiles",
    )(order, starts, landed)


def collect_planned_kernel(plan, landed, out):
    step = pl.program_id(0)
    width = out.shape[0]
    peers = plan.shape[1]

    @pl.loop(0, width)
    def _(t):
        g = step * width + t

        def add(j, total):
            place = plan[AT_ORDER + j // peers, lax.rem(j, peers)]
            return total + landed[place].astype(jnp.float32)

        out[t] = lax.fori_loop(
            plan[AT_STARTS, g],
            plan[AT_STARTS, g + 1],
            add,
            jnp.zeros(out.shape[1:], jnp.float32),
        )


def collect_planned(plan, landed, store_count):
    tile = landed.shape[1]
    group = 8
    return pl.pallas_call(
        collect_planned_kernel,
        grid=(store_count // group,),
        in_specs=[
            pl.BlockSpec(memory_space=pltpu.SMEM),
            pl.BlockSpec(memory_space=pltpu.VMEM),
        ],
        out_specs=pl.BlockSpec((group, tile, tile), lambda i: (i, 0, 0)),
        out_shape=jax.ShapeDtypeStruct((store_count, tile, tile), jnp.float32),
        compiler_params=params(),
        name="collect_planned",
    )(plan, landed)


def kept_list(keep):
    width = keep.shape[1]
    places = jnp.arange(width, dtype=jnp.int32)
    rank = jnp.cumsum(keep, axis=1) - keep
    hit = (rank[:, :, None] == places[None, None, :]) & (keep[:, :, None] > 0)
    return (
        jnp.sum(jnp.where(hit, places[None, :, None], 0), axis=1),
        jnp.sum(keep, axis=1),
    )


def slot_order(asked, store_count):
    count = asked.shape[0]
    places = jnp.arange(count, dtype=jnp.int32)
    key = jnp.where(asked >= 0, asked, store_count) * count + places
    rank = jnp.sum((key[None, :] < key[:, None]).astype(jnp.int32), axis=1)
    order = jnp.sum(jnp.where(rank[:, None] == places[None, :], places[:, None], 0), axis=0)
    stores = jnp.arange(store_count + 1, dtype=jnp.int32)
    starts = jnp.sum(
        ((asked[None, :] >= 0) & (asked[None, :] < stores[:, None])).astype(jnp.int32), axis=1
    )
    return order, starts


def body(basis, dmat, tile_home, pair_tiles, pair_pos, coords, weights, grad_sq, pair_keep):
    peers = lax.axis_size(AXES)
    me = lax.axis_index(AXES)
    blocks, pairs = pair_tiles.shape
    store_count, tile = dmat.shape[0], dmat.shape[1]
    rows = basis.shape[0] // blocks
    capacity = 2
    slot_count = peers * capacity
    asked, plan, raw, source = fetch_and_density(
        tile_home,
        pair_tiles,
        pair_pos.reshape(1, blocks * pairs),
        pair_keep,
        weights.reshape(blocks, rows),
        grad_sq.reshape(blocks, rows),
        coords,
        dmat,
        basis,
    )

    def two_slots():
        wanted = tile_home[pair_tiles.reshape(-1)]
        owner = wanted // store_count
        same = owner[:, None] == owner[None, :]
        places = jnp.arange(blocks * pairs, dtype=jnp.int32)
        earlier = jnp.sum((same & (places[None, :] < places[:, None])).astype(jnp.int32), axis=1)
        slots = owner * capacity + earlier
        requests = asked[:, 0, :capacity].reshape(-1) - 1
        shape = (peers, capacity, tile, tile)

        def exchange(values):
            return lax.all_to_all(
                values.reshape(shape), AXES, split_axis=0, concat_axis=0, tiled=True
            ).reshape(slot_count, tile, tile)

        def spread(values):
            wide = jnp.broadcast_to(values[None], (peers,) + values.shape)
            return lax.all_to_all(wide, AXES, split_axis=0, concat_axis=0, tiled=True)

        arrived = exchange(pick_tiles(requests, dmat))
        again = spread(block_density(slots, pair_pos, basis, arrived))
        features = source.transpose(2, 1, 3, 0, 4).reshape(peers * blocks, 5, rows)
        keep = lax.dynamic_slice_in_dim(pair_keep, me * blocks, blocks, 0)
        kept, counts = kept_list(keep)
        first = (me * blocks).astype(jnp.int32).reshape(1)
        field, returning = field_and_tiles(
            kept,
            counts,
            slots,
            pair_pos,
            first,
            again.reshape(peers * blocks, rows),
            features,
            basis,
            slot_count,
        )
        order, starts = slot_order(requests, store_count)
        return collect_tiles(order, starts, exchange(returning), store_count), field

    def relays():
        field, factor = field_only(
            plan,
            raw.reshape(peers * blocks, rows),
            source.reshape(5, peers * blocks, rows),
            blocks,
        )
        land = return_tiles(plan, factor, basis)
        return collect_planned(plan, land, store_count), field

    pieces, field = lax.cond(plan[AT_LEFT, 0] > 0, two_slots, relays)
    return pieces, field.reshape(-1)


def solution(mesh):
    in_specs = (
        P(AXES, None),
        P(AXES, None, None),
        P(),
        P(AXES, None),
        P(AXES, None),
        P(None, AXES),
        P(AXES),
        P(AXES),
        P(),
    )
    out_specs = (P(AXES, None, None), P(AXES))
    return jax.shard_map(body, mesh=mesh, in_specs=in_specs, out_specs=out_specs, check_vma=False)
```

```python
import functools

import jax
import jax.numpy as jnp
from jax import lax
from jax.experimental import pallas as pl
from jax.experimental.pallas import tpu as pltpu
from jax.sharding import PartitionSpec as P

gradient_coef = 0.0093
kappa_coef = 6.3
density_floor = 0.1
AXES = ("row", "col")
VMEM_LIMIT = 56 * 2**20
MESH = pl.DeviceIdType.MESH
STRIDE = 7
STEPS = (
    (0, 0, 0, 1),
    (0, 1, 0, 0),
    (1, 0, 0, 0),
    (0, 0, 1, 0),
    (0, 3, 0, 0),
    (3, 0, 0, 0),
    (0, 0, 3, 0),
    (0, 1, 1, 1),
    (1, 0, 1, 1),
    (1, 1, 0, 1),
    (0, 3, 3, 1),
    (3, 0, 3, 1),
    (3, 3, 0, 1),
    (0, 1, 3, 1),
    (1, 0, 3, 1),
    (1, 3, 0, 1),
)
ROOM = (56, 8, 8, 8, 4, 4, 4) + (1,) * 9
BASE = tuple(sum(ROOM[:k]) for k in range(len(ROOM)))
LINKS = len(ROOM)
RELAYED = sum(ROOM)
AT_LOC, AT_SRC, AT_CODE, AT_LEFT, AT_STARTS = range(2 * LINKS, 2 * LINKS + 5)
AT_TABLE, AT_MINE, AT_ORDER = 2 * LINKS + 5, 2 * LINKS + 7, 2 * LINKS + 9
AT_KEPT, AT_BLOCK, AT_FIRST, AT_LAST = range(2 * LINKS + 11, 2 * LINKS + 15)
PLAN_ROWS = 2 * LINKS + 16
ENTRIES = 44


def point_features(raw_density, grad_sq):
    density = jnp.maximum(raw_density, 0.0) + jnp.log1p(jnp.exp(-jnp.abs(raw_density))) + density_floor
    ratio = grad_sq / (density * density)
    omega_zero = jnp.sqrt(gradient_coef * ratio * ratio + 4.0 * jnp.pi / 3.0 * density)
    kappa_point = kappa_coef * 1.5 * jnp.pi * jnp.exp(jnp.log(density / (9.0 * jnp.pi)) * (1.0 / 6.0))
    return density, omega_zero, kappa_point


def params(**more):
    return pltpu.CompilerParams(vmem_limit_bytes=VMEM_LIMIT, **more)


def moved(device, move):
    dy, dx, dz, dc = move
    y = (device // 32 + dy) % 4
    x = (device // 8 + dx) % 4
    z = (device // 2 + dz) % 4
    return y * 32 + x * 8 + z * 2 + (device + dc) % 2


def back(move):
    return tuple((4 - m) % 4 for m in move[:3]) + (move[3],)


def parity(device):
    return (device + device // 2 + device // 8 + device // 32) % 2


def this_device():
    return lax.axis_index("row") * 32 + lax.axis_index("col")


def inside(value, count):
    return jnp.minimum(jnp.maximum(value, 0), count - 1)


def place_of(device):
    return device // 32, lax.rem(device, 32)


def neighbour(step):
    move = (step // 32, lax.rem(step // 8, 4), lax.rem(step // 2, 4), lax.rem(step, 2))
    return moved(this_device(), move)


def narrow_step(turn):
    up = lax.rem(turn * STRIDE, 64)
    return 2 * up + lax.rem(up + up // 4 + up // 16 + 1, 2)


def wide_step(turn):
    up = lax.rem(turn * STRIDE, 64)
    return 2 * up + lax.rem(up + up // 4 + up // 16, 2)


def iotas(peers):
    return (
        lax.broadcasted_iota(jnp.int32, (peers, peers), 0).astype(jnp.float32),
        lax.broadcasted_iota(jnp.int32, (peers, peers), 1).astype(jnp.float32),
    )


def down(row, peers):
    sub, lane = iotas(peers)
    return jnp.sum(jnp.where(sub == lane, row, 0.0), axis=1, keepdims=True)


def across(hit, column):
    return jnp.sum(jnp.where(hit, column, 0.0), axis=0, keepdims=True)


def make_requests(want, asking):
    peers = want.shape[1]
    sub, lane = iotas(peers)
    owner_int = want[0:1, :] // 64
    owner = owner_int.astype(jnp.float32)
    within = (want[0:1, :] - owner_int * 64).astype(jnp.float32)
    owner_down = down(owner, peers)
    same = owner_down == owner
    rank = across(same & (sub < lane), jnp.ones_like(owner_down))
    columns = [
        jnp.sum(
            jnp.where((owner == sub) & (rank == slot), within + 1.0, 0.0), axis=1, keepdims=True
        )
        for slot in range(2)
    ]
    entries = jnp.where(lane == 0.0, columns[0], jnp.where(lane == 1.0, columns[1], 0.0))
    named = across(owner_down == lane, jnp.ones_like(owner_down))
    asking[:, 0, :] = entries.astype(jnp.int32)
    asking[:, 1, :] = jnp.broadcast_to(named, (peers, peers)).astype(jnp.int32)


def make_tables(want, plan):
    peers = want.shape[1]
    sub, lane = iotas(peers)
    me = this_device()
    owner_int = want[0:1, :] // 64
    owner = owner_int.astype(jnp.float32)
    owner_down = down(owner, peers)
    rank = across((owner_down == owner) & (sub < lane), jnp.ones_like(owner_down))
    odd = parity(owner_int) != parity(me)
    found = jnp.where((rank == 1.0) & odd, 4.0 * peers + owner, 2.0 * owner + rank)
    pair = lax.broadcasted_iota(jnp.int32, (1, peers), 1)
    spot = (want[1:2, :] + 64 * (pair // 32)).astype(jnp.float32)
    rank_down, found_down, spot_down = down(rank, peers), down(found, peers), down(spot, peers)
    for half in range(2):
        row = across(spot_down == lane + half * peers, found_down - 2.0 * peers) + 2.0 * peers
        plan[AT_TABLE + half : AT_TABLE + half + 1, :] = row.astype(jnp.int32)
        row = across((owner_down == lane) & (rank_down == half), spot_down)
        plan[AT_MINE + half : AT_MINE + half + 1, :] = row.astype(jnp.int32)


def make_order(entries, again, plan):
    peers = entries.shape[0]
    sub, lane = iotas(peers)
    me = this_device()
    asker = lax.broadcasted_iota(jnp.int32, (peers, 1), 0)
    wide = parity(asker) == parity(me)
    number = asker.astype(jnp.float32)
    asked = [
        jnp.sum(jnp.where(lane == slot, entries, 0.0), axis=1, keepdims=True) for slot in range(2)
    ]
    places = [number, jnp.where(wide, number + peers, again + 2.0 * peers)]
    keys = [
        jnp.where(asked[slot] > 0.0, asked[slot] - 1.0, 64.0) * (2.0 * peers) + 2.0 * number + slot
        for slot in range(2)
    ]
    rows = [across(sub == lane, key) for key in keys]
    ranks = [
        sum(
            jnp.sum(jnp.where(row < key, 1.0, 0.0), axis=1, keepdims=True) for row in rows
        )
        for key in keys
    ]
    for half in range(2):
        row = sum(
            across(ranks[slot] == lane + half * peers, places[slot]) for slot in range(2)
        )
        plan[AT_ORDER + half : AT_ORDER + half + 1, :] = row.astype(jnp.int32)
    row = sum(
        across((asked[slot] > 0.0) & (asked[slot] - 1.0 < lane), jnp.ones_like(number))
        for slot in range(2)
    )
    plan[AT_STARTS : AT_STARTS + 1, :] = row.astype(jnp.int32)


def make_kept(keep, plan):
    blocks = keep.shape[0]
    peers = 128
    sub, lane = iotas(peers)
    lanes = lane[0:1, :]
    parts = keep.shape[1] // peers
    before = jnp.zeros((1, 1), jnp.float32)
    places, block_of, first, last = (jnp.zeros((1, peers), jnp.float32) for _ in range(4))
    for b in range(blocks):
        first = first + jnp.where(lanes == before, 1.0, 0.0)
        if b:
            block_of = block_of + jnp.where(lanes >= before, 1.0, 0.0)
        for g in range(parts):
            row = keep[b : b + 1, g * peers : (g + 1) * peers]
            rank = jnp.sum(jnp.where(lane < sub, row, 0.0), axis=1, keepdims=True) + before
            rank = jnp.where(down(row, peers) > 0.0, rank, -1.0)
            block = lax.broadcasted_iota(jnp.int32, (peers, 1), 0) + g * peers
            device = block // 4
            place = ((device % 2) * 64 + device // 2) * 4 + block % 4
            places = places + across(rank == lane, place.astype(jnp.float32))
            before = before + jnp.sum(row, axis=1, keepdims=True)
        last = last + jnp.where(lanes == b, before - 1.0, 0.0)
    for at, row in ((AT_KEPT, places), (AT_BLOCK, block_of), (AT_FIRST, first), (AT_LAST, last)):
        plan[at : at + 1, :] = row.astype(jnp.int32)


def most_kept(keep):
    total = keep.shape[0]
    peers = total // 4
    row = lax.broadcasted_iota(jnp.int32, (peers, total), 1) // 4
    group = jnp.where(row == lax.broadcasted_iota(jnp.int32, (peers, total), 0), 1.0, 0.0)
    counts = jnp.dot(
        group.astype(jnp.bfloat16),
        keep[...].astype(jnp.float32).astype(jnp.bfloat16),
        preferred_element_type=jnp.float32,
    )
    return jnp.max(jnp.sum(counts, axis=1, keepdims=True), axis=0, keepdims=True)


def greet_all(peers):
    barrier = pltpu.get_barrier_semaphore()
    for step in range(1, peers):
        pl.semaphore_signal(
            barrier, inc=1, device_id=place_of(neighbour(step)), device_id_type=MESH
        )


def wait_all(peers):
    pl.semaphore_wait(pltpu.get_barrier_semaphore(), peers - 1)


def remote(source, target, send, recv, at, device):
    return pltpu.make_async_remote_copy(
        src_ref=source,
        dst_ref=target,
        send_sem=send.at[at],
        recv_sem=recv.at[at],
        device_id=place_of(device),
        device_id_type=MESH,
    )


def make_plan(counts, plan):
    peers = counts.shape[0]
    me = this_device()
    asker = lax.broadcasted_iota(jnp.int32, (peers, peers), 0)
    owner = lax.broadcasted_iota(jnp.int32, (peers, peers), 1)
    wide = parity(asker) == parity(owner)
    zero = jnp.zeros((peers, peers), jnp.float32)
    left = jnp.where(wide | (counts < 2), 0.0, 1.0)
    free = jnp.where(wide & (counts < 2), 1.0, 0.0)
    earlier = jnp.where(owner < asker, 1.0, 0.0).astype(jnp.bfloat16)
    loc, src, code, again = zero, zero, zero, zero

    def dot(a, b):
        return jnp.dot(
            a.astype(jnp.bfloat16), b.astype(jnp.bfloat16), preferred_element_type=jnp.float32
        )

    def mine(values):
        return jnp.sum(jnp.where(owner == me, values, 0.0), axis=1, keepdims=True)

    def by_slot(column):
        hit = column == (owner + 1).astype(jnp.float32)
        return jnp.sum(jnp.where(hit, asker, 0), axis=0, keepdims=True)

    for k in range(LINKS):
        move, home = STEPS[k], back(STEPS[k])
        there = moved(owner, move)
        onto = jnp.where(asker == there, 1.0, 0.0)
        off = jnp.where(owner == moved(asker, move), 1.0, 0.0)
        want = left * dot(free, onto)
        rank = dot(earlier, want)
        numbered = jnp.where((want > 0.0) & (rank < ROOM[k]), rank + 1.0, 0.0)
        relay = dot(numbered, off)
        left = jnp.where(numbered > 0.0, 0.0, left)
        free = jnp.where(relay > 0.0, 0.0, free)
        loc = loc + jnp.where(numbered > 0.0, (2 * there + 1).astype(jnp.float32), 0.0)
        src = src + jnp.where(relay > 0.0, (moved(owner, home) + 1).astype(jnp.float32), 0.0)
        code = code + jnp.where(relay > 0.0, relay + BASE[k], 0.0)
        again = again + jnp.where(numbered > 0.0, numbered + (BASE[k] - 1.0), 0.0)
        plan[k : k + 1, :] = by_slot(mine(numbered))
        plan[LINKS + k : LINKS + k + 1, :] = by_slot(mine(relay))

    def row_of(values):
        return jnp.sum(jnp.where(asker == me, values, 0.0), axis=0, keepdims=True)

    def turned(values):
        return jnp.sum(jnp.where(asker == owner, mine(values), 0.0), axis=0, keepdims=True)

    plan[AT_LOC : AT_LOC + 1, :] = row_of(loc).astype(jnp.int32)
    plan[AT_SRC : AT_SRC + 1, :] = row_of(src).astype(jnp.int32)
    plan[AT_CODE : AT_CODE + 1, :] = turned(code).astype(jnp.int32)
    unplaced = jnp.sum(jnp.sum(left, axis=1, keepdims=True), axis=0, keepdims=True)
    plan[PLAN_ROWS - 1 :, :] = jnp.zeros((1, peers), jnp.int32)
    return mine(again), unplaced


def exchange_kernel(
    home,
    pair_tiles,
    pair_pos,
    pair_keep,
    weights,
    grad_sq,
    coords,
    tiles,
    basis,
    asked,
    plan,
    field,
    land,
    wanted,
    route,
    want_smem,
    want,
    asking,
    keep,
    local,
    raw_all,
    source_all,
    feats,
    column,
    partial,
    scaled,
    chis,
    seconds,
    stage,
    arrived,
    link_out,
    link_in,
    dense,
    own_sems,
    ask_send,
    ask_recv,
    first_send,
    first_recv,
    second_send,
    second_recv,
    link_send,
    link_recv,
    share_send,
    share_recv,
    raw_send,
    raw_recv,
    first_back_send,
    first_back_recv,
    second_back_send,
    second_back_recv,
    link_back_send,
    link_back_recv,
):
    peers = asked.shape[0]
    chips = peers // 2
    blocks, pairs = pair_tiles.shape
    orbs = basis.shape[1]
    rows = basis.shape[0] // blocks
    tile = tiles.shape[1]
    kt = orbs // tile
    me = this_device()
    chip, core = me // 2, lax.rem(me, 2)
    partner = 2 * chip + 1 - core

    def ask(step):
        to = neighbour(step)
        return remote(asking.at[to], asked.at[me], ask_send, ask_recv, step, to)

    def first(step):
        to = neighbour(step)
        return remote(stage.at[to, 0], arrived.at[me, 0], first_send, first_recv, step, to)

    def second(step):
        to = neighbour(step)
        return remote(stage.at[to, 1], arrived.at[me, 1], second_send, second_recv, step, to)

    def link(k):
        part = pl.ds(BASE[k], ROOM[k])
        return remote(
            link_out.at[part], link_in.at[part], link_send, link_recv, k, moved(me, STEPS[k])
        )

    def share(up):
        to = neighbour(2 * up)
        return remote(local, source_all.at[:, core, chip], share_send, share_recv, up, to)

    def share_on():
        part = source_all.at[:, core]
        return remote(part, part, share_send, share_recv, 0, partner)

    def tell_partner():
        part = raw_all.at[core, chip]
        return remote(part, part, raw_send, raw_recv, 0, partner)

    def tell(up):
        part = raw_all.at[:, chip]
        return remote(part, part, raw_send, raw_recv, up, neighbour(2 * up))

    def tile_for(device, slot):
        return tiles[inside(wanted[inside(device, peers), 0, slot] - 1, tiles.shape[0])]

    def second_for(device):
        at = route[AT_CODE, device]
        return jnp.where(at > 0, link_in[inside(at - 1, RELAYED)], tile_for(device, 1))

    def move(source, target, at):
        copy = pltpu.make_async_copy(source, target, own_sems.at[at])
        copy.start()
        return copy

    greet_all(peers)
    keep_copy = move(pair_keep, keep, 0)

    for b in range(blocks):

        @pl.loop(0, pairs)
        def _(j):
            want_smem[0, b * pairs + j] = home[inside(pair_tiles[b, j], home.shape[0])]
            want_smem[1, b * pairs + j] = pair_pos[b, j]

    move(want_smem, want, 1).wait()
    make_requests(want, asking)
    local[0] = weights[...]
    local[1] = grad_sq[...]
    for axis in range(3):
        for b in range(blocks):
            local[2 + axis, b : b + 1, :] = coords[axis : axis + 1, b * rows : (b + 1) * rows]
    wait_all(peers)

    @pl.loop(1, peers)
    def _(step):
        ask(step).start()

    @pl.loop(1, chips)
    def _(up):
        share(up).start()

    asked[me] = asking[me]
    source_all[:, core, chip] = local[...]
    arrived[peers] = jnp.zeros(arrived.shape[1:], arrived.dtype)

    @pl.loop(1, peers)
    def _(step):
        ask(step).wait()

    move(asked, wanted, 2).wait()

    @pl.loop(0, 64)
    def _(turn):
        step = narrow_step(turn)
        to = neighbour(step)
        stage[to, 0] = tile_for(to, 0)
        first(step).start()

    again, unplaced = make_plan(asked[:, 1, :], plan)
    move(plan, route, 3).wait()

    for k in range(LINKS):

        @pl.loop(0, ROOM[k])
        def _(s):
            link_out[BASE[k] + s] = tile_for(route[k, s], 1)

        link(k).start()

    @pl.loop(1, 64)
    def _(turn):
        step = wide_step(turn)
        to = neighbour(step)
        stage[to, 0] = tile_for(to, 0)
        first(step).start()

    arrived[me, 0] = tile_for(me, 0)

    for k in range(LINKS):
        link(k).wait()

    @pl.loop(1, 64)
    def _(turn):
        step = wide_step(turn)
        to = neighbour(step)
        stage[to, 1] = second_for(to)
        second(step).start()

    arrived[me, 1] = second_for(me)

    @pl.loop(1, chips)
    def _(up):
        share(up).wait()

    share_on().start()
    make_tables(want, plan)
    make_order(asked[:, 0, :].astype(jnp.float32), again, plan)
    keep_copy.wait()
    mine = keep[pl.ds(pl.multiple_of(8 * chip, 8), 8), :]
    make_kept(jnp.where(core == 0, mine[0:4, :], mine[4:8, :]).astype(jnp.float32), plan)
    unplaced = unplaced + jnp.where(most_kept(keep) > ENTRIES, 1.0, 0.0)
    plan[AT_LEFT : AT_LEFT + 1, :] = jnp.broadcast_to(unplaced, (1, peers)).astype(jnp.int32)
    for b in range(blocks):
        for m in range(kt):
            chis[b * kt + m] = basis[b * rows : (b + 1) * rows, m * tile : (m + 1) * tile]
        for axis in range(3):
            row = local[2 + axis, b : b + 1, :]
            column[b * 6 + 2 + axis] = jnp.broadcast_to(row, (rows, rows)).T
        column[b * 6 + 5] = jnp.broadcast_to(local[0, b : b + 1, :], (rows, rows)).T
    move(plan, route, 4).wait()

    @pl.loop(1, peers)
    def _(step):
        first(step).wait()

    @pl.loop(1, 64)
    def _(turn):
        second(wide_step(turn)).wait()

    for b in range(blocks):

        @pl.loop(0, kt)
        def _(row):
            for column in range(kt):
                q = b * kt * kt + row * kt + column
                slot = route[AT_TABLE + q // peers, lax.rem(q, peers)]
                slot = jnp.where(
                    slot >= 4 * peers, route[AT_LOC, inside(slot - 4 * peers, peers)], slot
                )
                slot = inside(slot, 2 * peers + 1)
                dense[
                    b % 2,
                    pl.ds(pl.multiple_of(row * tile, tile), tile),
                    column * tile : (column + 1) * tile,
                ] = arrived[slot // 2, lax.rem(slot, 2)]

        chi = basis[b * rows : (b + 1) * rows, :]
        mixed = jnp.dot(chi, dense[b % 2], preferred_element_type=jnp.float32)
        both = mixed * chi.astype(jnp.float32)
        part = both[:, :tile]
        for m in range(1, kt):
            part = part + both[:, m * tile : (m + 1) * tile]
        raw_all[core, chip, b : b + 1, :] = jnp.sum(part.T, axis=0, keepdims=True)

    tell_partner().start()
    share_on().wait()
    tell_partner().wait()

    @pl.loop(1, chips)
    def _(up):
        tell(up).start()

    @pl.loop(1, chips)
    def _(up):
        tell(up).wait()

    density, omega, kappa = point_features(raw_all[...], source_all[1])
    feats[0] = (source_all[0] * density).reshape(blocks * peers, rows)
    feats[1] = omega.reshape(blocks * peers, rows)
    feats[2] = kappa.reshape(blocks * peers, rows)
    for axis in range(3):
        feats[3 + axis] = source_all[2 + axis].reshape(blocks * peers, rows)
    start = pl.multiple_of((core * chips + chip) * blocks, blocks)
    for b in range(blocks):
        for f in range(2):
            row = feats[1 + f, pl.ds(start + b, 1), :]
            column[b * 6 + f] = jnp.broadcast_to(row, (rows, rows)).T

    def one_pair(e, total):
        s = inside(route[AT_KEPT, e], blocks * peers)
        at = 6 * inside(route[AT_BLOCK, e], blocks)
        r2 = None
        for axis in range(3):
            gap = column[at + 2 + axis] - feats[3 + axis, pl.ds(s, 1), :]
            r2 = gap * gap if r2 is None else r2 + gap * gap
        g = column[at] * r2 + column[at + 1]
        h = feats[1, pl.ds(s, 1), :] * r2 + feats[2, pl.ds(s, 1), :]
        phi = -1.5 / (g * h * (g + h))
        total = jnp.where(route[AT_FIRST, e] > 0, 0.0, total) + phi * feats[0, pl.ds(s, 1), :]
        partial[e] = total
        return total

    lax.fori_loop(0, ENTRIES, one_pair, jnp.zeros((rows, rows), jnp.float32))
    for b in range(blocks):
        total = partial[inside(route[AT_LAST, b], ENTRIES)]
        wide = jnp.broadcast_to(jnp.sum(total, axis=1, keepdims=True), (rows, rows))
        field[b : b + 1, :] = wide.T[0:1, :]
        factor = column[b * 6 + 5] * wide
        for m in range(kt):
            part = chis[b * kt + m].astype(jnp.float32) * factor
            scaled[b * kt + m] = part.astype(jnp.bfloat16).T

    def first_back(step):
        to = neighbour(step)
        return remote(stage.at[to, 0], land.at[me], first_back_send, first_back_recv, step, to)

    def second_back(step):
        to = neighbour(step)
        return remote(
            stage.at[to, 1], seconds.at[me], second_back_send, second_back_recv, step, to
        )

    def link_back(k):
        return remote(
            link_out.at[pl.ds(BASE[k], ROOM[k])],
            land.at[pl.ds(2 * peers + BASE[k], ROOM[k])],
            link_back_send,
            link_back_recv,
            k,
            moved(me, back(STEPS[k])),
        )

    def product_for(device, slot):
        at = inside(route[AT_MINE + slot, device], 2 * peers)
        b, q = at // (kt * kt), lax.rem(at, kt * kt)
        return jnp.dot(
            scaled[b * kt + q // kt],
            chis[b * kt + lax.rem(q, kt)],
            preferred_element_type=jnp.float32,
        ).astype(jnp.bfloat16)

    def second_product(device):
        via = route[AT_SRC, device]
        return product_for(inside(jnp.where(via > 0, via - 1, device), peers), 1)

    @pl.loop(1, 64)
    def _(turn):
        step = wide_step(turn)
        to = neighbour(step)
        stage[to, 1] = second_product(to)
        second_back(step).start()

    seconds[me] = second_product(me)
    stage[me, 0] = product_for(me, 0)
    own = move(stage.at[me, 0], land.at[me], 5)

    @pl.loop(0, 64)
    def _(turn):
        step = narrow_step(turn)
        to = neighbour(step)
        stage[to, 0] = product_for(to, 0)
        first_back(step).start()

    @pl.loop(1, 64)
    def _(turn):
        second_back(wide_step(turn)).wait()

    for k in range(LINKS):

        @pl.loop(0, ROOM[k])
        def _(s):
            link_out[BASE[k] + s] = seconds[inside(route[LINKS + k, s], peers)]

        link_back(k).start()

    rest = move(seconds, land.at[pl.ds(peers, peers)], 6)

    @pl.loop(1, 64)
    def _(turn):
        step = wide_step(turn)
        to = neighbour(step)
        stage[to, 0] = product_for(to, 0)
        first_back(step).start()

    for k in range(LINKS):
        link_back(k).wait()

    @pl.loop(1, peers)
    def _(step):
        first_back(step).wait()

    own.wait()
    rest.wait()


def exchange(home, pair_tiles, pair_pos, pair_keep, weights, grad_sq, coords, tiles, basis):
    blocks, pairs = pair_tiles.shape
    tile = tiles.shape[1]
    peers = blocks * pairs
    rows = basis.shape[0] // blocks
    orbs = basis.shape[1]
    kt = orbs // tile
    smem = pl.BlockSpec(memory_space=pltpu.SMEM)
    vmem = pl.BlockSpec(memory_space=pltpu.VMEM)
    hbm = pl.BlockSpec(memory_space=pl.ANY)
    pair = pltpu.SemaphoreType.DMA((peers,))
    half = pltpu.SemaphoreType.DMA((peers // 2,))
    links = pltpu.SemaphoreType.DMA((LINKS,))
    return pl.pallas_call(
        exchange_kernel,
        in_specs=[smem, smem, smem, hbm] + [vmem] * 5,
        out_specs=[vmem, vmem, vmem, hbm],
        out_shape=[
            jax.ShapeDtypeStruct((peers, 2, peers), jnp.int32),
            jax.ShapeDtypeStruct((PLAN_ROWS, peers), jnp.int32),
            jax.ShapeDtypeStruct((blocks, rows), jnp.float32),
            jax.ShapeDtypeStruct((2 * peers + RELAYED, tile, tile), tiles.dtype),
        ],
        scratch_shapes=[
            pltpu.SMEM((peers, 2, peers), jnp.int32),
            pltpu.SMEM((PLAN_ROWS, peers), jnp.int32),
            pltpu.SMEM((2, peers), jnp.int32),
            pltpu.VMEM((2, peers), jnp.int32),
            pltpu.VMEM((peers, 2, peers), jnp.int32),
            pltpu.VMEM(pair_keep.shape, jnp.int32),
            pltpu.VMEM((5, blocks, rows), jnp.float32),
            pltpu.VMEM((2, peers // 2, blocks, rows), jnp.float32),
            pltpu.VMEM((5, 2, peers // 2, blocks, rows), jnp.float32),
            pltpu.VMEM((6, blocks * peers, rows), jnp.float32),
            pltpu.VMEM((6 * blocks, rows, rows), jnp.float32),
            pltpu.VMEM((ENTRIES, rows, rows), jnp.float32),
            pltpu.VMEM((blocks * kt, tile, rows), basis.dtype),
            pltpu.VMEM((blocks * kt, rows, tile), basis.dtype),
            pltpu.VMEM((peers, tile, tile), basis.dtype),
            pltpu.VMEM((peers, 2, tile, tile), tiles.dtype),
            pltpu.VMEM((peers + 1, 2, tile, tile), tiles.dtype),
            pltpu.VMEM((RELAYED, tile, tile), tiles.dtype),
            pltpu.VMEM((RELAYED, tile, tile), tiles.dtype),
            pltpu.VMEM((2, orbs, orbs), basis.dtype),
            pltpu.SemaphoreType.DMA((7,)),
        ]
        + [pair] * 6
        + [links] * 2
        + [half] * 4
        + [pair] * 4
        + [links] * 2,
        compiler_params=params(collective_id=0, has_side_effects=True),
        name="exchange",
    )(home, pair_tiles, pair_pos, pair_keep, weights, grad_sq, coords, tiles, basis)


def pick_kernel(asked, tiles, out):
    step = pl.program_id(0)
    width = out.shape[0]

    @pl.loop(0, width)
    def _(slot):
        wanted = asked[step * width + slot]

        @pl.when(wanted >= 0)
        def _():
            out[slot] = tiles[wanted]


def pick_tiles(asked, tiles):
    count = asked.shape[0]
    group = 32
    return pl.pallas_call(
        pick_kernel,
        grid=(count // group,),
        in_specs=[
            pl.BlockSpec(memory_space=pltpu.SMEM),
            pl.BlockSpec(memory_space=pltpu.VMEM),
        ],
        out_specs=pl.BlockSpec((group,) + tiles.shape[1:], lambda i: (i, 0, 0)),
        out_shape=jax.ShapeDtypeStruct((count,) + tiles.shape[1:], tiles.dtype),
        compiler_params=params(),
        name="pick_tiles",
    )(asked, tiles)


def density_kernel(slots, positions, basis, arrived, raw, dense, sems):
    blocks, pairs = positions.shape
    rows = basis.shape[0] // blocks
    orbs = basis.shape[1]
    tile = arrived.shape[1]
    kt = orbs // tile

    dense[...] = jnp.zeros_like(dense)

    def fetch(b, k):
        q = positions[b, k]
        left = pl.multiple_of((q // kt) * tile, tile)
        right = pl.multiple_of((q % kt) * tile, tile)
        return pltpu.make_async_copy(
            arrived.at[slots[b * pairs + k]],
            dense.at[b, pl.ds(left, tile), pl.ds(right, tile)],
            sems.at[b * pairs + k],
        )

    for b in range(blocks):

        @pl.loop(0, pairs)
        def _(k):
            fetch(b, k).start()

    for b in range(blocks):

        @pl.loop(0, pairs)
        def _(k):
            fetch(b, k).wait()

        chi = basis[b * rows : (b + 1) * rows, :]
        mixed = jnp.dot(chi, dense[b], preferred_element_type=jnp.float32)
        both = mixed * chi.astype(jnp.float32)
        part = both[:, :tile]
        for m in range(1, kt):
            part = part + both[:, m * tile : (m + 1) * tile]
        raw[b : b + 1, :] = jnp.sum(part.T, axis=0, keepdims=True)


def block_density(slots, positions, basis, arrived):
    blocks = positions.shape[0]
    rows = basis.shape[0] // blocks
    orbs = basis.shape[1]
    return pl.pallas_call(
        density_kernel,
        in_specs=[
            pl.BlockSpec(memory_space=pltpu.SMEM),
            pl.BlockSpec(memory_space=pltpu.SMEM),
            pl.BlockSpec(memory_space=pltpu.VMEM),
            pl.BlockSpec(memory_space=pl.ANY),
        ],
        out_specs=pl.BlockSpec(memory_space=pltpu.VMEM),
        out_shape=jax.ShapeDtypeStruct((blocks, rows), jnp.float32),
        scratch_shapes=[
            pltpu.VMEM((blocks, orbs, orbs), basis.dtype),
            pltpu.SemaphoreType.DMA((positions.size,)),
        ],
        compiler_params=params(),
        name="block_density",
    )(slots, positions, basis, arrived)


def field_kernel(
    kept, counts, slots, positions, first, raw, source, basis, field, tiles_out, feats, column, scaled, staged, sems
):
    blocks, pairs = positions.shape
    rows = raw.shape[1]
    tile = tiles_out.shape[1]
    kt = basis.shape[1] // tile
    weights = source[:, 0]
    density, omega, kappa = point_features(raw[...], source[:, 1])
    feats[0] = weights * density
    feats[1] = omega
    feats[2] = kappa
    for axis in range(3):
        feats[3 + axis] = source[:, 2 + axis]

    def send(b, k):
        return pltpu.make_async_copy(
            staged.at[b * pairs + k], tiles_out.at[slots[b * pairs + k]], sems.at[b * pairs + k]
        )

    for b in range(blocks):
        at = first[0] + b
        for f in range(5):
            row = feats[1 + f, pl.ds(at, 1), :]
            column[f] = jnp.broadcast_to(row, (rows, rows)).T

        def one_source(j, total):
            s = kept[b, j]
            r2 = None
            for axis in range(3):
                gap = column[2 + axis] - feats[3 + axis, pl.ds(s, 1), :]
                r2 = gap * gap if r2 is None else r2 + gap * gap
            g = column[0] * r2 + column[1]
            h = feats[1, pl.ds(s, 1), :] * r2 + feats[2, pl.ds(s, 1), :]
            phi = -1.5 / (g * h * (g + h))
            return total + phi * feats[0, pl.ds(s, 1), :]

        total = lax.fori_loop(0, counts[b], one_source, jnp.zeros((rows, rows), jnp.float32))
        potential = jnp.sum(total, axis=1, keepdims=True)
        wide = jnp.broadcast_to(potential, (rows, rows))
        field[b : b + 1, :] = wide.T[0:1, :]
        weight = jnp.broadcast_to(source[pl.ds(at, 1), 0], (rows, rows)).T
        factor = weight * wide
        for m in range(kt):
            chi = basis[b * rows : (b + 1) * rows, m * tile : (m + 1) * tile]
            scaled[m] = (chi.astype(jnp.float32) * factor).astype(jnp.bfloat16).T
            scaled[kt + m] = chi

        @pl.loop(0, pairs)
        def _(k):
            q = positions[b, k]
            product = jnp.dot(
                scaled[q // kt], scaled[kt + q % kt], preferred_element_type=jnp.float32
            )
            staged[b * pairs + k] = product.astype(jnp.bfloat16)
            send(b, k).start()

    for b in range(blocks):

        @pl.loop(0, pairs)
        def _(k):
            send(b, k).wait()


def field_and_tiles(kept, counts, slots, positions, first, raw, source, basis, slot_count):
    blocks, pairs = positions.shape
    total, rows = raw.shape
    tile = 128
    kt = basis.shape[1] // tile
    smem = pl.BlockSpec(memory_space=pltpu.SMEM)
    vmem = pl.BlockSpec(memory_space=pltpu.VMEM)
    return pl.pallas_call(
        field_kernel,
        in_specs=[smem] * 5 + [vmem] * 3,
        out_specs=[vmem, pl.BlockSpec(memory_space=pl.ANY)],
        out_shape=[
            jax.ShapeDtypeStruct((blocks, rows), jnp.float32),
            jax.ShapeDtypeStruct((slot_count, tile, tile), jnp.bfloat16),
        ],
        scratch_shapes=[
            pltpu.VMEM((6, total, rows), jnp.float32),
            pltpu.VMEM((5, rows, rows), jnp.float32),
            pltpu.VMEM((2 * kt, tile, rows), jnp.bfloat16),
            pltpu.VMEM((blocks * pairs, tile, tile), jnp.bfloat16),
            pltpu.SemaphoreType.DMA((blocks * pairs,)),
        ],
        compiler_params=params(),
        name="field_and_tiles",
    )(kept, counts, slots, positions, first, raw, source, basis)


def collect_kernel(order, starts, landed, out):
    step = pl.program_id(0)
    width = out.shape[0]

    @pl.loop(0, width)
    def _(t):
        g = step * width + t

        def add(j, total):
            return total + landed[order[j]].astype(jnp.float32)

        out[t] = lax.fori_loop(
            starts[g], starts[g + 1], add, jnp.zeros(out.shape[1:], jnp.float32)
        )


def collect_tiles(order, starts, landed, store_count):
    tile = landed.shape[1]
    group = 8
    smem = pl.BlockSpec(memory_space=pltpu.SMEM)
    return pl.pallas_call(
        collect_kernel,
        grid=(store_count // group,),
        in_specs=[smem, smem, pl.BlockSpec(memory_space=pltpu.VMEM)],
        out_specs=pl.BlockSpec((group, tile, tile), lambda i: (i, 0, 0)),
        out_shape=jax.ShapeDtypeStruct((store_count, tile, tile), jnp.float32),
        compiler_params=params(),
        name="collect_tiles",
    )(order, starts, landed)


def collect_planned_kernel(plan, landed, out):
    step = pl.program_id(0)
    width = out.shape[0]
    peers = plan.shape[1]

    @pl.loop(0, width)
    def _(t):
        g = step * width + t

        def add(j, total):
            place = plan[AT_ORDER + j // peers, lax.rem(j, peers)]
            return total + landed[place].astype(jnp.float32)

        out[t] = lax.fori_loop(
            plan[AT_STARTS, g],
            plan[AT_STARTS, g + 1],
            add,
            jnp.zeros(out.shape[1:], jnp.float32),
        )


def collect_planned(plan, landed, store_count):
    tile = landed.shape[1]
    group = 8
    return pl.pallas_call(
        collect_planned_kernel,
        grid=(store_count // group,),
        in_specs=[
            pl.BlockSpec(memory_space=pltpu.SMEM),
            pl.BlockSpec(memory_space=pltpu.VMEM),
        ],
        out_specs=pl.BlockSpec((group, tile, tile), lambda i: (i, 0, 0)),
        out_shape=jax.ShapeDtypeStruct((store_count, tile, tile), jnp.float32),
        compiler_params=params(),
        name="collect_planned",
    )(plan, landed)


def kept_list(keep):
    width = keep.shape[1]
    places = jnp.arange(width, dtype=jnp.int32)
    rank = jnp.cumsum(keep, axis=1) - keep
    hit = (rank[:, :, None] == places[None, None, :]) & (keep[:, :, None] > 0)
    return (
        jnp.sum(jnp.where(hit, places[None, :, None], 0), axis=1),
        jnp.sum(keep, axis=1),
    )


def slot_order(asked, store_count):
    count = asked.shape[0]
    places = jnp.arange(count, dtype=jnp.int32)
    key = jnp.where(asked >= 0, asked, store_count) * count + places
    rank = jnp.sum((key[None, :] < key[:, None]).astype(jnp.int32), axis=1)
    order = jnp.sum(jnp.where(rank[:, None] == places[None, :], places[:, None], 0), axis=0)
    stores = jnp.arange(store_count + 1, dtype=jnp.int32)
    starts = jnp.sum(
        ((asked[None, :] >= 0) & (asked[None, :] < stores[:, None])).astype(jnp.int32), axis=1
    )
    return order, starts


def body(basis, dmat, tile_home, pair_tiles, pair_pos, coords, weights, grad_sq, pair_keep):
    peers = lax.axis_size(AXES)
    me = lax.axis_index(AXES)
    blocks, pairs = pair_tiles.shape
    store_count, tile = dmat.shape[0], dmat.shape[1]
    rows = basis.shape[0] // blocks
    capacity = 2
    slot_count = peers * capacity
    asked, plan, field, land = exchange(
        tile_home,
        pair_tiles,
        pair_pos,
        pair_keep,
        weights.reshape(blocks, rows),
        grad_sq.reshape(blocks, rows),
        coords,
        dmat,
        basis,
    )

    def two_slots():
        wanted = tile_home[pair_tiles.reshape(-1)]
        owner = wanted // store_count
        same = owner[:, None] == owner[None, :]
        places = jnp.arange(blocks * pairs, dtype=jnp.int32)
        earlier = jnp.sum((same & (places[None, :] < places[:, None])).astype(jnp.int32), axis=1)
        slots = owner * capacity + earlier
        requests = asked[:, 0, :capacity].reshape(-1) - 1
        shape = (peers, capacity, tile, tile)

        def swap(values):
            return lax.all_to_all(
                values.reshape(shape), AXES, split_axis=0, concat_axis=0, tiled=True
            ).reshape(slot_count, tile, tile)

        def spread(values):
            wide = jnp.broadcast_to(values[None], (peers,) + values.shape)
            return lax.all_to_all(wide, AXES, split_axis=0, concat_axis=0, tiled=True)

        arrived = swap(pick_tiles(requests, dmat))
        again = spread(block_density(slots, pair_pos, basis, arrived))
        local = jnp.concatenate([weights[None], grad_sq[None], coords], axis=0)
        features = spread(local.reshape(5, blocks, rows).transpose(1, 0, 2))
        keep = lax.dynamic_slice_in_dim(pair_keep, me * blocks, blocks, 0)
        kept, counts = kept_list(keep)
        first = (me * blocks).astype(jnp.int32).reshape(1)
        again, returning = field_and_tiles(
            kept,
            counts,
            slots,
            pair_pos,
            first,
            again.reshape(peers * blocks, rows),
            features.reshape(peers * blocks, 5, rows),
            basis,
            slot_count,
        )
        order, starts = slot_order(requests, store_count)
        return collect_tiles(order, starts, swap(returning), store_count), again

    def relays():
        return collect_planned(plan, land, store_count), field

    pieces, potential = lax.cond(plan[AT_LEFT, 0] > 0, two_slots, relays)
    return pieces, potential.reshape(-1)


def solution(mesh):
    in_specs = (
        P(AXES, None),
        P(AXES, None, None),
        P(),
        P(AXES, None),
        P(AXES, None),
        P(None, AXES),
        P(AXES),
        P(AXES),
        P(),
    )
    out_specs = (P(AXES, None, None), P(AXES))
    return jax.shard_map(body, mesh=mesh, in_specs=in_specs, out_specs=out_specs, check_vma=False)
```

```python
import functools

import jax
import jax.numpy as jnp
from jax import lax
from jax.experimental import pallas as pl
from jax.experimental.pallas import tpu as pltpu
from jax.sharding import PartitionSpec as P

gradient_coef = 0.0093
kappa_coef = 6.3
density_floor = 0.1
AXES = ("row", "col")
VMEM_LIMIT = 56 * 2**20
MESH = pl.DeviceIdType.MESH
STRIDE = 7
STEPS = (
    (0, 0, 0, 1),
    (0, 1, 0, 0),
    (1, 0, 0, 0),
    (0, 0, 1, 0),
    (0, 3, 0, 0),
    (3, 0, 0, 0),
    (0, 0, 3, 0),
    (0, 1, 1, 1),
    (1, 0, 1, 1),
    (1, 1, 0, 1),
    (0, 3, 3, 1),
    (3, 0, 3, 1),
    (3, 3, 0, 1),
    (0, 1, 3, 1),
    (1, 0, 3, 1),
    (1, 3, 0, 1),
)
ROOM = (56, 8, 8, 8, 4, 4, 4) + (1,) * 9
BASE = tuple(sum(ROOM[:k]) for k in range(len(ROOM)))
LINKS = len(ROOM)
RELAYED = sum(ROOM)
AT_LOC, AT_SRC, AT_CODE, AT_LEFT, AT_STARTS = range(2 * LINKS, 2 * LINKS + 5)
AT_TABLE, AT_MINE, AT_ORDER = 2 * LINKS + 5, 2 * LINKS + 7, 2 * LINKS + 9
AT_KEPT, AT_BLOCK, AT_FIRST, AT_LAST = range(2 * LINKS + 11, 2 * LINKS + 15)
PLAN_ROWS = 2 * LINKS + 16
ENTRIES = 44


def point_features(raw_density, grad_sq):
    density = jnp.maximum(raw_density, 0.0) + jnp.log1p(jnp.exp(-jnp.abs(raw_density))) + density_floor
    ratio = grad_sq / (density * density)
    omega_zero = jnp.sqrt(gradient_coef * ratio * ratio + 4.0 * jnp.pi / 3.0 * density)
    kappa_point = kappa_coef * 1.5 * jnp.pi * jnp.exp(jnp.log(density / (9.0 * jnp.pi)) * (1.0 / 6.0))
    return density, omega_zero, kappa_point


def params(**more):
    return pltpu.CompilerParams(vmem_limit_bytes=VMEM_LIMIT, **more)


def moved(device, move):
    dy, dx, dz, dc = move
    y = (device // 32 + dy) % 4
    x = (device // 8 + dx) % 4
    z = (device // 2 + dz) % 4
    return y * 32 + x * 8 + z * 2 + (device + dc) % 2


def back(move):
    return tuple((4 - m) % 4 for m in move[:3]) + (move[3],)


def parity(device):
    return (device + device // 2 + device // 8 + device // 32) % 2


def this_device():
    return lax.axis_index("row") * 32 + lax.axis_index("col")


def inside(value, count):
    return jnp.minimum(jnp.maximum(value, 0), count - 1)


def place_of(device):
    return device // 32, lax.rem(device, 32)


def neighbour(step):
    move = (step // 32, lax.rem(step // 8, 4), lax.rem(step // 2, 4), lax.rem(step, 2))
    return moved(this_device(), move)


def narrow_step(turn):
    up = lax.rem(turn * STRIDE, 64)
    return 2 * up + lax.rem(up + up // 4 + up // 16 + 1, 2)


def wide_step(turn):
    up = lax.rem(turn * STRIDE, 64)
    return 2 * up + lax.rem(up + up // 4 + up // 16, 2)


def iotas(peers):
    return (
        lax.broadcasted_iota(jnp.int32, (peers, peers), 0).astype(jnp.float32),
        lax.broadcasted_iota(jnp.int32, (peers, peers), 1).astype(jnp.float32),
    )


def down(row, peers):
    sub, lane = iotas(peers)
    return jnp.sum(jnp.where(sub == lane, row, 0.0), axis=1, keepdims=True)


def across(hit, column):
    return jnp.sum(jnp.where(hit, column, 0.0), axis=0, keepdims=True)


def one_column(values):
    blocks, pairs = values.shape
    wide = jnp.concatenate(
        [jnp.broadcast_to(values[b : b + 1, :], (pairs, pairs)) for b in range(blocks)], axis=0
    ).astype(jnp.float32)
    sub = lax.broadcasted_iota(jnp.int32, wide.shape, 0) % pairs
    lane = lax.broadcasted_iota(jnp.int32, wide.shape, 1)
    return jnp.sum(jnp.where(sub == lane, wide, 0.0), axis=1, keepdims=True)


def find_owners(home, pair_tiles):
    named = one_column(pair_tiles).astype(jnp.int32)
    peers, groups = named.shape[0], home.shape[0]
    sub, lane = iotas(peers)
    group = lax.broadcasted_iota(jnp.int32, (peers, groups), 1)
    pick = jnp.where(group == named // peers, 1.0, 0.0).astype(jnp.bfloat16)
    rest = (named % peers).astype(jnp.float32)

    def look(table):
        found = jnp.dot(
            pick, table.astype(jnp.float32).astype(jnp.bfloat16), preferred_element_type=jnp.float32
        )
        return jnp.sum(jnp.where(lane == rest, found, 0.0), axis=1, keepdims=True)

    device = home // 64
    return look(device), look(home - device * 64)


def make_requests(owner_down, within_down, asking):
    peers = owner_down.shape[0]
    sub, lane = iotas(peers)
    owner = across(sub == lane, owner_down)
    within = across(sub == lane, within_down)
    rank = across((owner_down == owner) & (sub < lane), jnp.ones_like(owner_down))
    columns = [
        jnp.sum(
            jnp.where((owner == sub) & (rank == slot), within + 1.0, 0.0), axis=1, keepdims=True
        )
        for slot in range(2)
    ]
    entries = jnp.where(lane == 0.0, columns[0], jnp.where(lane == 1.0, columns[1], 0.0))
    named = across(owner_down == lane, jnp.ones_like(owner_down))
    asking[:, 0, :] = entries.astype(jnp.int32)
    asking[:, 1, :] = jnp.broadcast_to(named, (peers, peers)).astype(jnp.int32)


def make_tables(owner_down, spots_down, plan):
    peers = owner_down.shape[0]
    sub, lane = iotas(peers)
    me = this_device()
    owner = across(sub == lane, owner_down)
    rank_down = jnp.sum(
        jnp.where((owner_down == owner) & (lane < sub), 1.0, 0.0), axis=1, keepdims=True
    )
    odd = parity(owner_down.astype(jnp.int32)) != parity(me)
    found_down = jnp.where(
        (rank_down == 1.0) & odd, 4.0 * peers + owner_down, 2.0 * owner_down + rank_down
    )
    pair = lax.broadcasted_iota(jnp.int32, (peers, 1), 0)
    spot_down = spots_down + (64 * (pair // 32)).astype(jnp.float32)
    for half in range(2):
        row = across(spot_down == lane + half * peers, found_down - 2.0 * peers) + 2.0 * peers
        plan[AT_TABLE + half : AT_TABLE + half + 1, :] = row.astype(jnp.int32)
        row = across((owner_down == lane) & (rank_down == half), spot_down)
        plan[AT_MINE + half : AT_MINE + half + 1, :] = row.astype(jnp.int32)


def make_order(entries, again, plan):
    peers = entries.shape[0]
    sub, lane = iotas(peers)
    me = this_device()
    asker = lax.broadcasted_iota(jnp.int32, (peers, 1), 0)
    wide = parity(asker) == parity(me)
    number = asker.astype(jnp.float32)
    asked = [
        jnp.sum(jnp.where(lane == slot, entries, 0.0), axis=1, keepdims=True) for slot in range(2)
    ]
    places = [number, jnp.where(wide, number + peers, again + 2.0 * peers)]
    keys = [
        jnp.where(asked[slot] > 0.0, asked[slot] - 1.0, 64.0) * (2.0 * peers) + 2.0 * number + slot
        for slot in range(2)
    ]
    rows = [across(sub == lane, key) for key in keys]
    ranks = [
        sum(
            jnp.sum(jnp.where(row < key, 1.0, 0.0), axis=1, keepdims=True) for row in rows
        )
        for key in keys
    ]
    for half in range(2):
        row = sum(
            across(ranks[slot] == lane + half * peers, places[slot]) for slot in range(2)
        )
        plan[AT_ORDER + half : AT_ORDER + half + 1, :] = row.astype(jnp.int32)
    row = sum(
        across((asked[slot] > 0.0) & (asked[slot] - 1.0 < lane), jnp.ones_like(number))
        for slot in range(2)
    )
    plan[AT_STARTS : AT_STARTS + 1, :] = row.astype(jnp.int32)


def make_kept(keep, plan):
    blocks = keep.shape[0]
    peers = 128
    sub, lane = iotas(peers)
    lanes = lane[0:1, :]
    parts = keep.shape[1] // peers
    before = jnp.zeros((1, 1), jnp.float32)
    places, block_of, first, last = (jnp.zeros((1, peers), jnp.float32) for _ in range(4))
    for b in range(blocks):
        first = first + jnp.where(lanes == before, 1.0, 0.0)
        if b:
            block_of = block_of + jnp.where(lanes >= before, 1.0, 0.0)
        for g in range(parts):
            row = keep[b : b + 1, g * peers : (g + 1) * peers]
            rank = jnp.sum(jnp.where(lane < sub, row, 0.0), axis=1, keepdims=True) + before
            rank = jnp.where(down(row, peers) > 0.0, rank, -1.0)
            block = lax.broadcasted_iota(jnp.int32, (peers, 1), 0) + g * peers
            device = block // 4
            place = ((device % 2) * 64 + device // 2) * 4 + block % 4
            places = places + across(rank == lane, place.astype(jnp.float32))
            before = before + jnp.sum(row, axis=1, keepdims=True)
        last = last + jnp.where(lanes == b, before - 1.0, 0.0)
    for at, row in ((AT_KEPT, places), (AT_BLOCK, block_of), (AT_FIRST, first), (AT_LAST, last)):
        plan[at : at + 1, :] = row.astype(jnp.int32)


def most_kept(keep):
    total = keep.shape[0]
    peers = total // 4
    row = lax.broadcasted_iota(jnp.int32, (peers, total), 1) // 4
    group = jnp.where(row == lax.broadcasted_iota(jnp.int32, (peers, total), 0), 1.0, 0.0)
    counts = jnp.dot(
        group.astype(jnp.bfloat16),
        keep[...].astype(jnp.float32).astype(jnp.bfloat16),
        preferred_element_type=jnp.float32,
    )
    return jnp.max(jnp.sum(counts, axis=1, keepdims=True), axis=0, keepdims=True)


def greet_all(peers):
    barrier = pltpu.get_barrier_semaphore()
    for step in range(1, peers):
        pl.semaphore_signal(
            barrier, inc=1, device_id=place_of(neighbour(step)), device_id_type=MESH
        )


def wait_all(peers):
    pl.semaphore_wait(pltpu.get_barrier_semaphore(), peers - 1)


def remote(source, target, send, recv, at, device):
    return pltpu.make_async_remote_copy(
        src_ref=source,
        dst_ref=target,
        send_sem=send.at[at],
        recv_sem=recv.at[at],
        device_id=place_of(device),
        device_id_type=MESH,
    )


def make_plan(counts, plan):
    peers = counts.shape[0]
    me = this_device()
    asker = lax.broadcasted_iota(jnp.int32, (peers, peers), 0)
    owner = lax.broadcasted_iota(jnp.int32, (peers, peers), 1)
    wide = parity(asker) == parity(owner)
    zero = jnp.zeros((peers, peers), jnp.float32)
    left = jnp.where(wide | (counts < 2), 0.0, 1.0)
    free = jnp.where(wide & (counts < 2), 1.0, 0.0)
    earlier = jnp.where(owner < asker, 1.0, 0.0).astype(jnp.bfloat16)
    loc, src, code, again = zero, zero, zero, zero

    def dot(a, b):
        return jnp.dot(
            a.astype(jnp.bfloat16), b.astype(jnp.bfloat16), preferred_element_type=jnp.float32
        )

    def mine(values):
        return jnp.sum(jnp.where(owner == me, values, 0.0), axis=1, keepdims=True)

    def by_slot(column):
        hit = column == (owner + 1).astype(jnp.float32)
        return jnp.sum(jnp.where(hit, asker, 0), axis=0, keepdims=True)

    for k in range(LINKS):
        move, home = STEPS[k], back(STEPS[k])
        there = moved(owner, move)
        onto = jnp.where(asker == there, 1.0, 0.0)
        off = jnp.where(owner == moved(asker, move), 1.0, 0.0)
        want = left * dot(free, onto)
        rank = dot(earlier, want)
        numbered = jnp.where((want > 0.0) & (rank < ROOM[k]), rank + 1.0, 0.0)
        relay = dot(numbered, off)
        left = jnp.where(numbered > 0.0, 0.0, left)
        free = jnp.where(relay > 0.0, 0.0, free)
        loc = loc + jnp.where(numbered > 0.0, (2 * there + 1).astype(jnp.float32), 0.0)
        src = src + jnp.where(relay > 0.0, (moved(owner, home) + 1).astype(jnp.float32), 0.0)
        code = code + jnp.where(relay > 0.0, relay + BASE[k], 0.0)
        again = again + jnp.where(numbered > 0.0, numbered + (BASE[k] - 1.0), 0.0)
        plan[k : k + 1, :] = by_slot(mine(numbered))
        plan[LINKS + k : LINKS + k + 1, :] = by_slot(mine(relay))

    def row_of(values):
        return jnp.sum(jnp.where(asker == me, values, 0.0), axis=0, keepdims=True)

    def turned(values):
        return jnp.sum(jnp.where(asker == owner, mine(values), 0.0), axis=0, keepdims=True)

    plan[AT_LOC : AT_LOC + 1, :] = row_of(loc).astype(jnp.int32)
    plan[AT_SRC : AT_SRC + 1, :] = row_of(src).astype(jnp.int32)
    plan[AT_CODE : AT_CODE + 1, :] = turned(code).astype(jnp.int32)
    unplaced = jnp.sum(jnp.sum(left, axis=1, keepdims=True), axis=0, keepdims=True)
    plan[PLAN_ROWS - 1 :, :] = jnp.zeros((1, peers), jnp.int32)
    return mine(again), unplaced


def exchange_kernel(
    home,
    pair_tiles,
    pair_pos,
    pair_keep,
    weights,
    grad_sq,
    coords,
    tiles_far,
    basis_far,
    asked,
    plan,
    field,
    land,
    wanted,
    route,
    tiles,
    basis,
    wanted_rows,
    asking,
    keep,
    local,
    raw_all,
    source_all,
    feats,
    column,
    partial,
    scaled,
    chis,
    seconds,
    stage,
    arrived,
    link_out,
    link_in,
    dense,
    own_sems,
    ask_send,
    ask_recv,
    first_send,
    first_recv,
    second_send,
    second_recv,
    link_send,
    link_recv,
    share_send,
    share_recv,
    raw_send,
    raw_recv,
    first_back_send,
    first_back_recv,
    second_back_send,
    second_back_recv,
    link_back_send,
    link_back_recv,
):
    peers = asked.shape[0]
    chips = peers // 2
    blocks, pairs = pair_tiles.shape
    orbs = basis.shape[1]
    rows = basis.shape[0] // blocks
    tile = tiles.shape[1]
    kt = orbs // tile
    me = this_device()
    chip, core = me // 2, lax.rem(me, 2)
    partner = 2 * chip + 1 - core

    def ask(step):
        to = neighbour(step)
        return remote(asking.at[to], asked.at[me], ask_send, ask_recv, step, to)

    def first(step):
        to = neighbour(step)
        return remote(stage.at[to, 0], arrived.at[me, 0], first_send, first_recv, step, to)

    def second(step):
        to = neighbour(step)
        return remote(stage.at[to, 1], arrived.at[me, 1], second_send, second_recv, step, to)

    def link(k):
        part = pl.ds(BASE[k], ROOM[k])
        return remote(
            link_out.at[part], link_in.at[part], link_send, link_recv, k, moved(me, STEPS[k])
        )

    def share(up):
        to = neighbour(2 * up)
        return remote(local, source_all.at[:, core, chip], share_send, share_recv, up, to)

    def share_on():
        part = source_all.at[:, core]
        return remote(part, part, share_send, share_recv, 0, partner)

    def tell_partner():
        part = raw_all.at[core, chip]
        return remote(part, part, raw_send, raw_recv, 0, partner)

    def tell(up):
        part = raw_all.at[:, chip]
        return remote(part, part, raw_send, raw_recv, up, neighbour(2 * up))

    def tile_for(device, slot):
        return tiles[inside(wanted[slot, inside(device, peers)] - 1, tiles.shape[0])]

    def second_for(device):
        at = route[AT_CODE, device]
        return jnp.where(at > 0, link_in[inside(at - 1, RELAYED)], tile_for(device, 1))

    def move(source, target, at):
        copy = pltpu.make_async_copy(source, target, own_sems.at[at])
        copy.start()
        return copy

    greet_all(peers)
    tiles_copy = move(tiles_far, tiles, 1)
    basis_copy = move(basis_far, basis, 2)
    keep_copy = move(pair_keep, keep, 0)
    owner_down, within_down = find_owners(home[...], pair_tiles[...])
    make_requests(owner_down, within_down, asking)
    local[0] = weights[...]
    local[1] = grad_sq[...]
    for axis in range(3):
        for b in range(blocks):
            local[2 + axis, b : b + 1, :] = coords[axis : axis + 1, b * rows : (b + 1) * rows]
    wait_all(peers)

    @pl.loop(1, peers)
    def _(step):
        ask(step).start()

    @pl.loop(1, chips)
    def _(up):
        share(up).start()

    asked[me] = asking[me]
    source_all[:, core, chip] = local[...]
    arrived[peers] = jnp.zeros(arrived.shape[1:], arrived.dtype)

    @pl.loop(1, peers)
    def _(step):
        ask(step).wait()

    entries = asked[:, 0, :].astype(jnp.float32)
    sub, lane = iotas(peers)
    for slot in range(2):
        column_of = jnp.sum(jnp.where(lane == slot, entries, 0.0), axis=1, keepdims=True)
        wanted_rows[slot : slot + 1, :] = across(sub == lane, column_of).astype(jnp.int32)
    move(wanted_rows, wanted, 7).wait()
    tiles_copy.wait()

    @pl.loop(0, 64)
    def _(turn):
        step = narrow_step(turn)
        to = neighbour(step)
        stage[to, 0] = tile_for(to, 0)
        first(step).start()

    again, unplaced = make_plan(asked[:, 1, :], plan)
    move(plan, route, 3).wait()

    for k in range(LINKS):

        @pl.loop(0, ROOM[k])
        def _(s):
            link_out[BASE[k] + s] = tile_for(route[k, s], 1)

        link(k).start()

    @pl.loop(1, 64)
    def _(turn):
        step = wide_step(turn)
        to = neighbour(step)
        stage[to, 0] = tile_for(to, 0)
        first(step).start()

    arrived[me, 0] = tile_for(me, 0)

    for k in range(LINKS):
        link(k).wait()

    @pl.loop(1, 64)
    def _(turn):
        step = wide_step(turn)
        to = neighbour(step)
        stage[to, 1] = second_for(to)
        second(step).start()

    arrived[me, 1] = second_for(me)

    @pl.loop(1, chips)
    def _(up):
        share(up).wait()

    share_on().start()
    make_tables(owner_down, one_column(pair_pos[...]), plan)
    make_order(asked[:, 0, :].astype(jnp.float32), again, plan)
    keep_copy.wait()
    basis_copy.wait()
    mine = keep[pl.ds(pl.multiple_of(8 * chip, 8), 8), :]
    make_kept(jnp.where(core == 0, mine[0:4, :], mine[4:8, :]).astype(jnp.float32), plan)
    unplaced = unplaced + jnp.where(most_kept(keep) > ENTRIES, 1.0, 0.0)
    plan[AT_LEFT : AT_LEFT + 1, :] = jnp.broadcast_to(unplaced, (1, peers)).astype(jnp.int32)
    for b in range(blocks):
        for m in range(kt):
            chis[b * kt + m] = basis[b * rows : (b + 1) * rows, m * tile : (m + 1) * tile]
        for axis in range(3):
            row = local[2 + axis, b : b + 1, :]
            column[b * 6 + 2 + axis] = jnp.broadcast_to(row, (rows, rows)).T
        column[b * 6 + 5] = jnp.broadcast_to(local[0, b : b + 1, :], (rows, rows)).T
    move(plan, route, 4).wait()

    @pl.loop(1, peers)
    def _(step):
        first(step).wait()

    @pl.loop(1, 64)
    def _(turn):
        second(wide_step(turn)).wait()

    for b in range(blocks):

        @pl.loop(0, kt)
        def _(row):
            for column in range(kt):
                q = b * kt * kt + row * kt + column
                slot = route[AT_TABLE + q // peers, lax.rem(q, peers)]
                slot = jnp.where(
                    slot >= 4 * peers, route[AT_LOC, inside(slot - 4 * peers, peers)], slot
                )
                slot = inside(slot, 2 * peers + 1)
                dense[
                    b % 2,
                    pl.ds(pl.multiple_of(row * tile, tile), tile),
                    column * tile : (column + 1) * tile,
                ] = arrived[slot // 2, lax.rem(slot, 2)]

        chi = basis[b * rows : (b + 1) * rows, :]
        mixed = jnp.dot(chi, dense[b % 2], preferred_element_type=jnp.float32)
        both = mixed * chi.astype(jnp.float32)
        part = both[:, :tile]
        for m in range(1, kt):
            part = part + both[:, m * tile : (m + 1) * tile]
        raw_all[core, chip, b : b + 1, :] = jnp.sum(part.T, axis=0, keepdims=True)

    tell_partner().start()
    share_on().wait()
    tell_partner().wait()

    @pl.loop(1, chips)
    def _(up):
        tell(up).start()

    @pl.loop(1, chips)
    def _(up):
        tell(up).wait()

    density, omega, kappa = point_features(raw_all[...], source_all[1])
    feats[0] = (source_all[0] * density).reshape(blocks * peers, rows)
    feats[1] = omega.reshape(blocks * peers, rows)
    feats[2] = kappa.reshape(blocks * peers, rows)
    for axis in range(3):
        feats[3 + axis] = source_all[2 + axis].reshape(blocks * peers, rows)
    start = pl.multiple_of((core * chips + chip) * blocks, blocks)
    for b in range(blocks):
        for f in range(2):
            row = feats[1 + f, pl.ds(start + b, 1), :]
            column[b * 6 + f] = jnp.broadcast_to(row, (rows, rows)).T

    def one_pair(e, total):
        s = inside(route[AT_KEPT, e], blocks * peers)
        at = 6 * inside(route[AT_BLOCK, e], blocks)
        r2 = None
        for axis in range(3):
            gap = column[at + 2 + axis] - feats[3 + axis, pl.ds(s, 1), :]
            r2 = gap * gap if r2 is None else r2 + gap * gap
        g = column[at] * r2 + column[at + 1]
        h = feats[1, pl.ds(s, 1), :] * r2 + feats[2, pl.ds(s, 1), :]
        phi = -1.5 / (g * h * (g + h))
        total = jnp.where(route[AT_FIRST, e] > 0, 0.0, total) + phi * feats[0, pl.ds(s, 1), :]
        partial[e] = total
        return total

    lax.fori_loop(0, ENTRIES, one_pair, jnp.zeros((rows, rows), jnp.float32))
    for b in range(blocks):
        total = partial[inside(route[AT_LAST, b], ENTRIES)]
        wide = jnp.broadcast_to(jnp.sum(total, axis=1, keepdims=True), (rows, rows))
        field[b : b + 1, :] = wide.T[0:1, :]
        factor = column[b * 6 + 5] * wide
        for m in range(kt):
            part = chis[b * kt + m].astype(jnp.float32) * factor
            scaled[b * kt + m] = part.astype(jnp.bfloat16).T

    def first_back(step):
        to = neighbour(step)
        return remote(stage.at[to, 0], land.at[me], first_back_send, first_back_recv, step, to)

    def second_back(step):
        to = neighbour(step)
        return remote(
            stage.at[to, 1], seconds.at[me], second_back_send, second_back_recv, step, to
        )

    def link_back(k):
        return remote(
            link_out.at[pl.ds(BASE[k], ROOM[k])],
            land.at[pl.ds(2 * peers + BASE[k], ROOM[k])],
            link_back_send,
            link_back_recv,
            k,
            moved(me, back(STEPS[k])),
        )

    def product_for(device, slot):
        at = inside(route[AT_MINE + slot, device], 2 * peers)
        b, q = at // (kt * kt), lax.rem(at, kt * kt)
        return jnp.dot(
            scaled[b * kt + q // kt],
            chis[b * kt + lax.rem(q, kt)],
            preferred_element_type=jnp.float32,
        ).astype(jnp.bfloat16)

    def second_product(device):
        via = route[AT_SRC, device]
        return product_for(inside(jnp.where(via > 0, via - 1, device), peers), 1)

    @pl.loop(1, 64)
    def _(turn):
        step = wide_step(turn)
        to = neighbour(step)
        stage[to, 1] = second_product(to)
        second_back(step).start()

    seconds[me] = second_product(me)
    stage[me, 0] = product_for(me, 0)
    own = move(stage.at[me, 0], land.at[me], 5)

    @pl.loop(0, 64)
    def _(turn):
        step = narrow_step(turn)
        to = neighbour(step)
        stage[to, 0] = product_for(to, 0)
        first_back(step).start()

    @pl.loop(1, 64)
    def _(turn):
        second_back(wide_step(turn)).wait()

    for k in range(LINKS):

        @pl.loop(0, ROOM[k])
        def _(s):
            link_out[BASE[k] + s] = seconds[inside(route[LINKS + k, s], peers)]

        link_back(k).start()

    rest = move(seconds, land.at[pl.ds(peers, peers)], 6)

    @pl.loop(1, 64)
    def _(turn):
        step = wide_step(turn)
        to = neighbour(step)
        stage[to, 0] = product_for(to, 0)
        first_back(step).start()

    for k in range(LINKS):
        link_back(k).wait()

    @pl.loop(1, peers)
    def _(step):
        first_back(step).wait()

    own.wait()
    rest.wait()


def exchange(home, pair_tiles, pair_pos, pair_keep, weights, grad_sq, coords, tiles, basis):
    blocks, pairs = pair_tiles.shape
    tile = tiles.shape[1]
    peers = blocks * pairs
    rows = basis.shape[0] // blocks
    orbs = basis.shape[1]
    kt = orbs // tile
    smem = pl.BlockSpec(memory_space=pltpu.SMEM)
    vmem = pl.BlockSpec(memory_space=pltpu.VMEM)
    hbm = pl.BlockSpec(memory_space=pl.ANY)
    pair = pltpu.SemaphoreType.DMA((peers,))
    half = pltpu.SemaphoreType.DMA((peers // 2,))
    links = pltpu.SemaphoreType.DMA((LINKS,))
    return pl.pallas_call(
        exchange_kernel,
        in_specs=[vmem, vmem, vmem, hbm, vmem, vmem, vmem, hbm, hbm],
        out_specs=[vmem, vmem, vmem, hbm],
        out_shape=[
            jax.ShapeDtypeStruct((peers, 2, peers), jnp.int32),
            jax.ShapeDtypeStruct((PLAN_ROWS, peers), jnp.int32),
            jax.ShapeDtypeStruct((blocks, rows), jnp.float32),
            jax.ShapeDtypeStruct((2 * peers + RELAYED, tile, tile), tiles.dtype),
        ],
        scratch_shapes=[
            pltpu.SMEM((2, peers), jnp.int32),
            pltpu.SMEM((PLAN_ROWS, peers), jnp.int32),
            pltpu.VMEM(tiles.shape, tiles.dtype),
            pltpu.VMEM(basis.shape, basis.dtype),
            pltpu.VMEM((2, peers), jnp.int32),
            pltpu.VMEM((peers, 2, peers), jnp.int32),
            pltpu.VMEM(pair_keep.shape, jnp.int32),
            pltpu.VMEM((5, blocks, rows), jnp.float32),
            pltpu.VMEM((2, peers // 2, blocks, rows), jnp.float32),
            pltpu.VMEM((5, 2, peers // 2, blocks, rows), jnp.float32),
            pltpu.VMEM((6, blocks * peers, rows), jnp.float32),
            pltpu.VMEM((6 * blocks, rows, rows), jnp.float32),
            pltpu.VMEM((ENTRIES, rows, rows), jnp.float32),
            pltpu.VMEM((blocks * kt, tile, rows), basis.dtype),
            pltpu.VMEM((blocks * kt, rows, tile), basis.dtype),
            pltpu.VMEM((peers, tile, tile), basis.dtype),
            pltpu.VMEM((peers, 2, tile, tile), tiles.dtype),
            pltpu.VMEM((peers + 1, 2, tile, tile), tiles.dtype),
            pltpu.VMEM((RELAYED, tile, tile), tiles.dtype),
            pltpu.VMEM((RELAYED, tile, tile), tiles.dtype),
            pltpu.VMEM((2, orbs, orbs), basis.dtype),
            pltpu.SemaphoreType.DMA((8,)),
        ]
        + [pair] * 6
        + [links] * 2
        + [half] * 4
        + [pair] * 4
        + [links] * 2,
        compiler_params=params(collective_id=0, has_side_effects=True),
        name="exchange",
    )(home, pair_tiles, pair_pos, pair_keep, weights, grad_sq, coords, tiles, basis)


def pick_kernel(asked, tiles, out):
    step = pl.program_id(0)
    width = out.shape[0]

    @pl.loop(0, width)
    def _(slot):
        wanted = asked[step * width + slot]

        @pl.when(wanted >= 0)
        def _():
            out[slot] = tiles[wanted]


def pick_tiles(asked, tiles):
    count = asked.shape[0]
    group = 32
    return pl.pallas_call(
        pick_kernel,
        grid=(count // group,),
        in_specs=[
            pl.BlockSpec(memory_space=pltpu.SMEM),
            pl.BlockSpec(memory_space=pltpu.VMEM),
        ],
        out_specs=pl.BlockSpec((group,) + tiles.shape[1:], lambda i: (i, 0, 0)),
        out_shape=jax.ShapeDtypeStruct((count,) + tiles.shape[1:], tiles.dtype),
        compiler_params=params(),
        name="pick_tiles",
    )(asked, tiles)


def density_kernel(slots, positions, basis, arrived, raw, dense, sems):
    blocks, pairs = positions.shape
    rows = basis.shape[0] // blocks
    orbs = basis.shape[1]
    tile = arrived.shape[1]
    kt = orbs // tile

    dense[...] = jnp.zeros_like(dense)

    def fetch(b, k):
        q = positions[b, k]
        left = pl.multiple_of((q // kt) * tile, tile)
        right = pl.multiple_of((q % kt) * tile, tile)
        return pltpu.make_async_copy(
            arrived.at[slots[b * pairs + k]],
            dense.at[b, pl.ds(left, tile), pl.ds(right, tile)],
            sems.at[b * pairs + k],
        )

    for b in range(blocks):

        @pl.loop(0, pairs)
        def _(k):
            fetch(b, k).start()

    for b in range(blocks):

        @pl.loop(0, pairs)
        def _(k):
            fetch(b, k).wait()

        chi = basis[b * rows : (b + 1) * rows, :]
        mixed = jnp.dot(chi, dense[b], preferred_element_type=jnp.float32)
        both = mixed * chi.astype(jnp.float32)
        part = both[:, :tile]
        for m in range(1, kt):
            part = part + both[:, m * tile : (m + 1) * tile]
        raw[b : b + 1, :] = jnp.sum(part.T, axis=0, keepdims=True)


def block_density(slots, positions, basis, arrived):
    blocks = positions.shape[0]
    rows = basis.shape[0] // blocks
    orbs = basis.shape[1]
    return pl.pallas_call(
        density_kernel,
        in_specs=[
            pl.BlockSpec(memory_space=pltpu.SMEM),
            pl.BlockSpec(memory_space=pltpu.SMEM),
            pl.BlockSpec(memory_space=pltpu.VMEM),
            pl.BlockSpec(memory_space=pl.ANY),
        ],
        out_specs=pl.BlockSpec(memory_space=pltpu.VMEM),
        out_shape=jax.ShapeDtypeStruct((blocks, rows), jnp.float32),
        scratch_shapes=[
            pltpu.VMEM((blocks, orbs, orbs), basis.dtype),
            pltpu.SemaphoreType.DMA((positions.size,)),
        ],
        compiler_params=params(),
        name="block_density",
    )(slots, positions, basis, arrived)


def field_kernel(
    kept, counts, slots, positions, first, raw, source, basis, field, tiles_out, feats, column, scaled, staged, sems
):
    blocks, pairs = positions.shape
    rows = raw.shape[1]
    tile = tiles_out.shape[1]
    kt = basis.shape[1] // tile
    weights = source[:, 0]
    density, omega, kappa = point_features(raw[...], source[:, 1])
    feats[0] = weights * density
    feats[1] = omega
    feats[2] = kappa
    for axis in range(3):
        feats[3 + axis] = source[:, 2 + axis]

    def send(b, k):
        return pltpu.make_async_copy(
            staged.at[b * pairs + k], tiles_out.at[slots[b * pairs + k]], sems.at[b * pairs + k]
        )

    for b in range(blocks):
        at = first[0] + b
        for f in range(5):
            row = feats[1 + f, pl.ds(at, 1), :]
            column[f] = jnp.broadcast_to(row, (rows, rows)).T

        def one_source(j, total):
            s = kept[b, j]
            r2 = None
            for axis in range(3):
                gap = column[2 + axis] - feats[3 + axis, pl.ds(s, 1), :]
                r2 = gap * gap if r2 is None else r2 + gap * gap
            g = column[0] * r2 + column[1]
            h = feats[1, pl.ds(s, 1), :] * r2 + feats[2, pl.ds(s, 1), :]
            phi = -1.5 / (g * h * (g + h))
            return total + phi * feats[0, pl.ds(s, 1), :]

        total = lax.fori_loop(0, counts[b], one_source, jnp.zeros((rows, rows), jnp.float32))
        potential = jnp.sum(total, axis=1, keepdims=True)
        wide = jnp.broadcast_to(potential, (rows, rows))
        field[b : b + 1, :] = wide.T[0:1, :]
        weight = jnp.broadcast_to(source[pl.ds(at, 1), 0], (rows, rows)).T
        factor = weight * wide
        for m in range(kt):
            chi = basis[b * rows : (b + 1) * rows, m * tile : (m + 1) * tile]
            scaled[m] = (chi.astype(jnp.float32) * factor).astype(jnp.bfloat16).T
            scaled[kt + m] = chi

        @pl.loop(0, pairs)
        def _(k):
            q = positions[b, k]
            product = jnp.dot(
                scaled[q // kt], scaled[kt + q % kt], preferred_element_type=jnp.float32
            )
            staged[b * pairs + k] = product.astype(jnp.bfloat16)
            send(b, k).start()

    for b in range(blocks):

        @pl.loop(0, pairs)
        def _(k):
            send(b, k).wait()


def field_and_tiles(kept, counts, slots, positions, first, raw, source, basis, slot_count):
    blocks, pairs = positions.shape
    total, rows = raw.shape
    tile = 128
    kt = basis.shape[1] // tile
    smem = pl.BlockSpec(memory_space=pltpu.SMEM)
    vmem = pl.BlockSpec(memory_space=pltpu.VMEM)
    return pl.pallas_call(
        field_kernel,
        in_specs=[smem] * 5 + [vmem] * 3,
        out_specs=[vmem, pl.BlockSpec(memory_space=pl.ANY)],
        out_shape=[
            jax.ShapeDtypeStruct((blocks, rows), jnp.float32),
            jax.ShapeDtypeStruct((slot_count, tile, tile), jnp.bfloat16),
        ],
        scratch_shapes=[
            pltpu.VMEM((6, total, rows), jnp.float32),
            pltpu.VMEM((5, rows, rows), jnp.float32),
            pltpu.VMEM((2 * kt, tile, rows), jnp.bfloat16),
            pltpu.VMEM((blocks * pairs, tile, tile), jnp.bfloat16),
            pltpu.SemaphoreType.DMA((blocks * pairs,)),
        ],
        compiler_params=params(),
        name="field_and_tiles",
    )(kept, counts, slots, positions, first, raw, source, basis)


def collect_kernel(order, starts, landed, out):
    step = pl.program_id(0)
    width = out.shape[0]

    @pl.loop(0, width)
    def _(t):
        g = step * width + t

        def add(j, total):
            return total + landed[order[j]].astype(jnp.float32)

        out[t] = lax.fori_loop(
            starts[g], starts[g + 1], add, jnp.zeros(out.shape[1:], jnp.float32)
        )


def collect_tiles(order, starts, landed, store_count):
    tile = landed.shape[1]
    group = 8
    smem = pl.BlockSpec(memory_space=pltpu.SMEM)
    return pl.pallas_call(
        collect_kernel,
        grid=(store_count // group,),
        in_specs=[smem, smem, pl.BlockSpec(memory_space=pltpu.VMEM)],
        out_specs=pl.BlockSpec((group, tile, tile), lambda i: (i, 0, 0)),
        out_shape=jax.ShapeDtypeStruct((store_count, tile, tile), jnp.float32),
        compiler_params=params(),
        name="collect_tiles",
    )(order, starts, landed)


def collect_planned_kernel(plan, landed, out):
    step = pl.program_id(0)
    width = out.shape[0]
    peers = plan.shape[1]

    @pl.loop(0, width)
    def _(t):
        g = step * width + t

        def add(j, total):
            place = plan[AT_ORDER + j // peers, lax.rem(j, peers)]
            return total + landed[place].astype(jnp.float32)

        out[t] = lax.fori_loop(
            plan[AT_STARTS, g],
            plan[AT_STARTS, g + 1],
            add,
            jnp.zeros(out.shape[1:], jnp.float32),
        )


def collect_planned(plan, landed, store_count):
    tile = landed.shape[1]
    group = 8
    return pl.pallas_call(
        collect_planned_kernel,
        grid=(store_count // group,),
        in_specs=[
            pl.BlockSpec(memory_space=pltpu.SMEM),
            pl.BlockSpec(memory_space=pltpu.VMEM),
        ],
        out_specs=pl.BlockSpec((group, tile, tile), lambda i: (i, 0, 0)),
        out_shape=jax.ShapeDtypeStruct((store_count, tile, tile), jnp.float32),
        compiler_params=params(),
        name="collect_planned",
    )(plan, landed)


def kept_list(keep):
    width = keep.shape[1]
    places = jnp.arange(width, dtype=jnp.int32)
    rank = jnp.cumsum(keep, axis=1) - keep
    hit = (rank[:, :, None] == places[None, None, :]) & (keep[:, :, None] > 0)
    return (
        jnp.sum(jnp.where(hit, places[None, :, None], 0), axis=1),
        jnp.sum(keep, axis=1),
    )


def slot_order(asked, store_count):
    count = asked.shape[0]
    places = jnp.arange(count, dtype=jnp.int32)
    key = jnp.where(asked >= 0, asked, store_count) * count + places
    rank = jnp.sum((key[None, :] < key[:, None]).astype(jnp.int32), axis=1)
    order = jnp.sum(jnp.where(rank[:, None] == places[None, :], places[:, None], 0), axis=0)
    stores = jnp.arange(store_count + 1, dtype=jnp.int32)
    starts = jnp.sum(
        ((asked[None, :] >= 0) & (asked[None, :] < stores[:, None])).astype(jnp.int32), axis=1
    )
    return order, starts


def body(basis, dmat, tile_home, pair_tiles, pair_pos, coords, weights, grad_sq, pair_keep):
    peers = lax.axis_size(AXES)
    me = lax.axis_index(AXES)
    blocks, pairs = pair_tiles.shape
    store_count, tile = dmat.shape[0], dmat.shape[1]
    rows = basis.shape[0] // blocks
    capacity = 2
    slot_count = peers * capacity
    asked, plan, field, land = exchange(
        tile_home.reshape(-1, tile),
        pair_tiles,
        pair_pos,
        pair_keep,
        weights.reshape(blocks, rows),
        grad_sq.reshape(blocks, rows),
        coords,
        dmat,
        basis,
    )

    def two_slots():
        wanted = tile_home[pair_tiles.reshape(-1)]
        owner = wanted // store_count
        same = owner[:, None] == owner[None, :]
        places = jnp.arange(blocks * pairs, dtype=jnp.int32)
        earlier = jnp.sum((same & (places[None, :] < places[:, None])).astype(jnp.int32), axis=1)
        slots = owner * capacity + earlier
        requests = asked[:, 0, :capacity].reshape(-1) - 1
        shape = (peers, capacity, tile, tile)

        def swap(values):
            return lax.all_to_all(
                values.reshape(shape), AXES, split_axis=0, concat_axis=0, tiled=True
            ).reshape(slot_count, tile, tile)

        def spread(values):
            wide = jnp.broadcast_to(values[None], (peers,) + values.shape)
            return lax.all_to_all(wide, AXES, split_axis=0, concat_axis=0, tiled=True)

        arrived = swap(pick_tiles(requests, dmat))
        again = spread(block_density(slots, pair_pos, basis, arrived))
        local = jnp.concatenate([weights[None], grad_sq[None], coords], axis=0)
        features = spread(local.reshape(5, blocks, rows).transpose(1, 0, 2))
        keep = lax.dynamic_slice_in_dim(pair_keep, me * blocks, blocks, 0)
        kept, counts = kept_list(keep)
        first = (me * blocks).astype(jnp.int32).reshape(1)
        again, returning = field_and_tiles(
            kept,
            counts,
            slots,
            pair_pos,
            first,
            again.reshape(peers * blocks, rows),
            features.reshape(peers * blocks, 5, rows),
            basis,
            slot_count,
        )
        order, starts = slot_order(requests, store_count)
        return collect_tiles(order, starts, swap(returning), store_count), again

    def relays():
        return collect_planned(plan, land, store_count), field

    pieces, potential = lax.cond(plan[AT_LEFT, 0] > 0, two_slots, relays)
    return pieces, potential.reshape(-1)


def solution(mesh):
    in_specs = (
        P(AXES, None),
        P(AXES, None, None),
        P(),
        P(AXES, None),
        P(AXES, None),
        P(None, AXES),
        P(AXES),
        P(AXES),
        P(),
    )
    out_specs = (P(AXES, None, None), P(AXES))
    return jax.shard_map(body, mesh=mesh, in_specs=in_specs, out_specs=out_specs, check_vma=False)
```

```python
import functools

import jax
import jax.numpy as jnp
from jax import lax
from jax.experimental import pallas as pl
from jax.experimental.pallas import tpu as pltpu
from jax.sharding import PartitionSpec as P

gradient_coef = 0.0093
kappa_coef = 6.3
density_floor = 0.1
AXES = ("row", "col")
VMEM_LIMIT = 56 * 2**20
MESH = pl.DeviceIdType.MESH
STRIDE = 7
STEPS = (
    (0, 0, 0, 1),
    (0, 1, 0, 0),
    (1, 0, 0, 0),
    (0, 0, 1, 0),
    (0, 3, 0, 0),
    (3, 0, 0, 0),
    (0, 0, 3, 0),
    (0, 1, 1, 1),
    (1, 0, 1, 1),
    (1, 1, 0, 1),
    (0, 3, 3, 1),
    (3, 0, 3, 1),
    (3, 3, 0, 1),
    (0, 1, 3, 1),
    (1, 0, 3, 1),
    (1, 3, 0, 1),
)
ROOM = (48, 6, 6, 6, 4, 4, 4) + (1,) * 9
BASE = tuple(sum(ROOM[:k]) for k in range(len(ROOM)))
LINKS = len(ROOM)
RELAYED = sum(ROOM)
AT_LOC, AT_SRC, AT_CODE, AT_LEFT, AT_STARTS = range(2 * LINKS, 2 * LINKS + 5)
AT_TABLE, AT_MINE, AT_ORDER = 2 * LINKS + 5, 2 * LINKS + 7, 2 * LINKS + 9
AT_KEPT, AT_BLOCK, AT_FIRST, AT_LAST = range(2 * LINKS + 11, 2 * LINKS + 15)
PLAN_ROWS = 2 * LINKS + 16
ENTRIES = 44


def point_features(raw_density, grad_sq):
    density = jnp.maximum(raw_density, 0.0) + jnp.log1p(jnp.exp(-jnp.abs(raw_density))) + density_floor
    ratio = grad_sq / (density * density)
    omega_zero = jnp.sqrt(gradient_coef * ratio * ratio + 4.0 * jnp.pi / 3.0 * density)
    kappa_point = kappa_coef * 1.5 * jnp.pi * jnp.exp(jnp.log(density / (9.0 * jnp.pi)) * (1.0 / 6.0))
    return density, omega_zero, kappa_point


def params(limit=VMEM_LIMIT, **more):
    return pltpu.CompilerParams(vmem_limit_bytes=limit, **more)


def moved(device, move):
    dy, dx, dz, dc = move
    y = (device // 32 + dy) % 4
    x = (device // 8 + dx) % 4
    z = (device // 2 + dz) % 4
    return y * 32 + x * 8 + z * 2 + (device + dc) % 2


def back(move):
    return tuple((4 - m) % 4 for m in move[:3]) + (move[3],)


def parity(device):
    return (device + device // 2 + device // 8 + device // 32) % 2


def this_device():
    return lax.axis_index("row") * 32 + lax.axis_index("col")


def inside(value, count):
    return jnp.minimum(jnp.maximum(value, 0), count - 1)


def place_of(device):
    return device // 32, lax.rem(device, 32)


def neighbour(step):
    move = (step // 32, lax.rem(step // 8, 4), lax.rem(step // 2, 4), lax.rem(step, 2))
    return moved(this_device(), move)


def narrow_step(turn):
    up = lax.rem(turn * STRIDE, 64)
    return 2 * up + lax.rem(up + up // 4 + up // 16 + 1, 2)


def wide_step(turn):
    up = lax.rem(turn * STRIDE, 64)
    return 2 * up + lax.rem(up + up // 4 + up // 16, 2)


def iotas(peers):
    return (
        lax.broadcasted_iota(jnp.int32, (peers, peers), 0).astype(jnp.float32),
        lax.broadcasted_iota(jnp.int32, (peers, peers), 1).astype(jnp.float32),
    )


def down(row, peers):
    sub, lane = iotas(peers)
    return jnp.sum(jnp.where(sub == lane, row, 0.0), axis=1, keepdims=True)


def across(hit, column):
    return jnp.sum(jnp.where(hit, column, 0.0), axis=0, keepdims=True)


def one_column(values):
    blocks, pairs = values.shape
    wide = jnp.concatenate(
        [jnp.broadcast_to(values[b : b + 1, :], (pairs, pairs)) for b in range(blocks)], axis=0
    ).astype(jnp.float32)
    sub = lax.broadcasted_iota(jnp.int32, wide.shape, 0) % pairs
    lane = lax.broadcasted_iota(jnp.int32, wide.shape, 1)
    return jnp.sum(jnp.where(sub == lane, wide, 0.0), axis=1, keepdims=True)


def find_owners(home, pair_tiles):
    named = one_column(pair_tiles).astype(jnp.int32)
    peers, groups = named.shape[0], home.shape[0]
    sub, lane = iotas(peers)
    group = lax.broadcasted_iota(jnp.int32, (peers, groups), 1)
    pick = jnp.where(group == named // peers, 1.0, 0.0).astype(jnp.bfloat16)
    rest = (named % peers).astype(jnp.float32)

    def look(table):
        found = jnp.dot(
            pick, table.astype(jnp.float32).astype(jnp.bfloat16), preferred_element_type=jnp.float32
        )
        return jnp.sum(jnp.where(lane == rest, found, 0.0), axis=1, keepdims=True)

    device = home // 64
    return look(device), look(home - device * 64)


def make_requests(owner_down, within_down, asking):
    peers = owner_down.shape[0]
    sub, lane = iotas(peers)
    owner = across(sub == lane, owner_down)
    within = across(sub == lane, within_down)
    rank = across((owner_down == owner) & (sub < lane), jnp.ones_like(owner_down))
    columns = [
        jnp.sum(
            jnp.where((owner == sub) & (rank == slot), within + 1.0, 0.0), axis=1, keepdims=True
        )
        for slot in range(2)
    ]
    entries = jnp.where(lane == 0.0, columns[0], jnp.where(lane == 1.0, columns[1], 0.0))
    named = across(owner_down == lane, jnp.ones_like(owner_down))
    asking[:, 0, :] = entries.astype(jnp.int32)
    asking[:, 1, :] = jnp.broadcast_to(named, (peers, peers)).astype(jnp.int32)


def make_tables(owner_down, spots_down, plan):
    peers = owner_down.shape[0]
    sub, lane = iotas(peers)
    me = this_device()
    owner = across(sub == lane, owner_down)
    rank_down = jnp.sum(
        jnp.where((owner_down == owner) & (lane < sub), 1.0, 0.0), axis=1, keepdims=True
    )
    odd = parity(owner_down.astype(jnp.int32)) != parity(me)
    found_down = jnp.where(
        (rank_down == 1.0) & odd, 4.0 * peers + owner_down, 2.0 * owner_down + rank_down
    )
    pair = lax.broadcasted_iota(jnp.int32, (peers, 1), 0)
    spot_down = spots_down + (64 * (pair // 32)).astype(jnp.float32)
    for half in range(2):
        row = across(spot_down == lane + half * peers, found_down - 2.0 * peers) + 2.0 * peers
        plan[AT_TABLE + half : AT_TABLE + half + 1, :] = row.astype(jnp.int32)
        row = across((owner_down == lane) & (rank_down == half), spot_down)
        plan[AT_MINE + half : AT_MINE + half + 1, :] = row.astype(jnp.int32)


def make_order(entries, again, plan):
    peers = entries.shape[0]
    sub, lane = iotas(peers)
    me = this_device()
    asker = lax.broadcasted_iota(jnp.int32, (peers, 1), 0)
    wide = parity(asker) == parity(me)
    number = asker.astype(jnp.float32)
    asked = [
        jnp.sum(jnp.where(lane == slot, entries, 0.0), axis=1, keepdims=True) for slot in range(2)
    ]
    places = [number, jnp.where(wide, number + peers, again + 2.0 * peers)]
    keys = [
        jnp.where(asked[slot] > 0.0, asked[slot] - 1.0, 64.0) * (2.0 * peers) + 2.0 * number + slot
        for slot in range(2)
    ]
    rows = [across(sub == lane, key) for key in keys]
    ranks = [
        sum(
            jnp.sum(jnp.where(row < key, 1.0, 0.0), axis=1, keepdims=True) for row in rows
        )
        for key in keys
    ]
    for half in range(2):
        row = sum(
            across(ranks[slot] == lane + half * peers, places[slot]) for slot in range(2)
        )
        plan[AT_ORDER + half : AT_ORDER + half + 1, :] = row.astype(jnp.int32)
    row = sum(
        across((asked[slot] > 0.0) & (asked[slot] - 1.0 < lane), jnp.ones_like(number))
        for slot in range(2)
    )
    plan[AT_STARTS : AT_STARTS + 1, :] = row.astype(jnp.int32)


def make_kept(keep, plan):
    blocks = keep.shape[0]
    peers = 128
    sub, lane = iotas(peers)
    lanes = lane[0:1, :]
    parts = keep.shape[1] // peers
    before = jnp.zeros((1, 1), jnp.float32)
    places, block_of, first, last = (jnp.zeros((1, peers), jnp.float32) for _ in range(4))
    for b in range(blocks):
        first = first + jnp.where(lanes == before, 1.0, 0.0)
        if b:
            block_of = block_of + jnp.where(lanes >= before, 1.0, 0.0)
        for g in range(parts):
            row = keep[b : b + 1, g * peers : (g + 1) * peers]
            rank = jnp.sum(jnp.where(lane < sub, row, 0.0), axis=1, keepdims=True) + before
            rank = jnp.where(down(row, peers) > 0.0, rank, -1.0)
            block = lax.broadcasted_iota(jnp.int32, (peers, 1), 0) + g * peers
            device = block // 4
            place = ((device % 2) * 64 + device // 2) * 4 + block % 4
            places = places + across(rank == lane, place.astype(jnp.float32))
            before = before + jnp.sum(row, axis=1, keepdims=True)
        last = last + jnp.where(lanes == b, before - 1.0, 0.0)
    for at, row in ((AT_KEPT, places), (AT_BLOCK, block_of), (AT_FIRST, first), (AT_LAST, last)):
        plan[at : at + 1, :] = row.astype(jnp.int32)


def most_kept(keep):
    total = keep.shape[0]
    peers = total // 4
    row = lax.broadcasted_iota(jnp.int32, (peers, total), 1) // 4
    group = jnp.where(row == lax.broadcasted_iota(jnp.int32, (peers, total), 0), 1.0, 0.0)
    counts = jnp.dot(
        group.astype(jnp.bfloat16),
        keep[...].astype(jnp.float32).astype(jnp.bfloat16),
        preferred_element_type=jnp.float32,
    )
    return jnp.max(jnp.sum(counts, axis=1, keepdims=True), axis=0, keepdims=True)


def greet_all(peers):
    barrier = pltpu.get_barrier_semaphore()
    for step in range(1, peers):
        pl.semaphore_signal(
            barrier, inc=1, device_id=place_of(neighbour(step)), device_id_type=MESH
        )


def wait_all(peers):
    pl.semaphore_wait(pltpu.get_barrier_semaphore(), peers - 1)


def remote(source, target, send, recv, at, device):
    return pltpu.make_async_remote_copy(
        src_ref=source,
        dst_ref=target,
        send_sem=send.at[at],
        recv_sem=recv.at[at],
        device_id=place_of(device),
        device_id_type=MESH,
    )


def make_plan(counts, plan):
    peers = counts.shape[0]
    me = this_device()
    asker = lax.broadcasted_iota(jnp.int32, (peers, peers), 0)
    owner = lax.broadcasted_iota(jnp.int32, (peers, peers), 1)
    wide = parity(asker) == parity(owner)
    zero = jnp.zeros((peers, peers), jnp.float32)
    left = jnp.where(wide | (counts < 2), 0.0, 1.0)
    free = jnp.where(wide & (counts < 2), 1.0, 0.0)
    earlier = jnp.where(owner < asker, 1.0, 0.0).astype(jnp.bfloat16)
    loc, src, code, again = zero, zero, zero, zero

    def dot(a, b):
        return jnp.dot(
            a.astype(jnp.bfloat16), b.astype(jnp.bfloat16), preferred_element_type=jnp.float32
        )

    def mine(values):
        return jnp.sum(jnp.where(owner == me, values, 0.0), axis=1, keepdims=True)

    def by_slot(column):
        hit = column == (owner + 1).astype(jnp.float32)
        return jnp.sum(jnp.where(hit, asker, 0), axis=0, keepdims=True)

    for k in range(LINKS):
        move, home = STEPS[k], back(STEPS[k])
        there = moved(owner, move)
        onto = jnp.where(asker == there, 1.0, 0.0)
        off = jnp.where(owner == moved(asker, move), 1.0, 0.0)
        want = left * dot(free, onto)
        rank = dot(earlier, want)
        numbered = jnp.where((want > 0.0) & (rank < ROOM[k]), rank + 1.0, 0.0)
        relay = dot(numbered, off)
        left = jnp.where(numbered > 0.0, 0.0, left)
        free = jnp.where(relay > 0.0, 0.0, free)
        loc = loc + jnp.where(numbered > 0.0, (2 * there + 1).astype(jnp.float32), 0.0)
        src = src + jnp.where(relay > 0.0, (moved(owner, home) + 1).astype(jnp.float32), 0.0)
        code = code + jnp.where(relay > 0.0, relay + BASE[k], 0.0)
        again = again + jnp.where(numbered > 0.0, numbered + (BASE[k] - 1.0), 0.0)
        plan[k : k + 1, :] = by_slot(mine(numbered))
        plan[LINKS + k : LINKS + k + 1, :] = by_slot(mine(relay))

    def row_of(values):
        return jnp.sum(jnp.where(asker == me, values, 0.0), axis=0, keepdims=True)

    def turned(values):
        return jnp.sum(jnp.where(asker == owner, mine(values), 0.0), axis=0, keepdims=True)

    plan[AT_LOC : AT_LOC + 1, :] = row_of(loc).astype(jnp.int32)
    plan[AT_SRC : AT_SRC + 1, :] = row_of(src).astype(jnp.int32)
    plan[AT_CODE : AT_CODE + 1, :] = turned(code).astype(jnp.int32)
    unplaced = jnp.sum(jnp.sum(left, axis=1, keepdims=True), axis=0, keepdims=True)
    plan[PLAN_ROWS - 1 :, :] = jnp.zeros((1, peers), jnp.int32)
    return mine(again), unplaced


def exchange_kernel(
    home,
    pair_tiles,
    pair_pos,
    pair_keep,
    weights,
    grad_sq,
    coords,
    tiles_far,
    basis_far,
    asked,
    plan,
    field,
    land,
    wanted,
    route,
    tiles,
    basis,
    wanted_rows,
    asking,
    keep,
    local,
    raw_all,
    source_all,
    feats,
    column,
    partial,
    scaled,
    chis,
    seconds,
    stage,
    arrived,
    link_out,
    link_in,
    dense,
    own_sems,
    ask_send,
    ask_recv,
    first_send,
    first_recv,
    second_send,
    second_recv,
    link_send,
    link_recv,
    share_send,
    share_recv,
    raw_send,
    raw_recv,
    first_back_send,
    first_back_recv,
    second_back_send,
    second_back_recv,
    link_back_send,
    link_back_recv,
):
    peers = asked.shape[0]
    chips = peers // 2
    blocks, pairs = pair_tiles.shape
    orbs = basis.shape[1]
    rows = basis.shape[0] // blocks
    tile = tiles.shape[1]
    kt = orbs // tile
    me = this_device()
    chip, core = me // 2, lax.rem(me, 2)
    partner = 2 * chip + 1 - core

    def ask(step):
        to = neighbour(step)
        return remote(asking.at[to], asked.at[me], ask_send, ask_recv, step, to)

    def first(step):
        to = neighbour(step)
        return remote(stage.at[to, 0], arrived.at[me, 0], first_send, first_recv, step, to)

    def second(step):
        to = neighbour(step)
        return remote(stage.at[to, 1], arrived.at[me, 1], second_send, second_recv, step, to)

    def link(k):
        part = pl.ds(BASE[k], ROOM[k])
        return remote(
            link_out.at[part], link_in.at[part], link_send, link_recv, k, moved(me, STEPS[k])
        )

    def share(up):
        to = neighbour(2 * up)
        return remote(local, source_all.at[:, core, chip], share_send, share_recv, up, to)

    def share_on():
        part = source_all.at[:, core]
        return remote(part, part, share_send, share_recv, 0, partner)

    def tell_partner():
        part = raw_all.at[core, chip]
        return remote(part, part, raw_send, raw_recv, 0, partner)

    def tell(up):
        part = raw_all.at[:, chip]
        return remote(part, part, raw_send, raw_recv, up, neighbour(2 * up))

    def tile_for(device, slot):
        return tiles[inside(wanted[slot, inside(device, peers)] - 1, tiles.shape[0])]

    def second_for(device):
        at = route[AT_CODE, device]
        return jnp.where(at > 0, link_in[inside(at - 1, RELAYED)], tile_for(device, 1))

    def move(source, target, at):
        copy = pltpu.make_async_copy(source, target, own_sems.at[at])
        copy.start()
        return copy

    greet_all(peers)
    tiles_copy = move(tiles_far, tiles, 1)
    basis_copy = move(basis_far, basis, 2)
    keep_copy = move(pair_keep, keep, 0)
    owner_down, within_down = find_owners(home[...], pair_tiles[...])
    make_requests(owner_down, within_down, asking)
    local[0] = weights[...]
    local[1] = grad_sq[...]
    for axis in range(3):
        for b in range(blocks):
            local[2 + axis, b : b + 1, :] = coords[axis : axis + 1, b * rows : (b + 1) * rows]
    wait_all(peers)

    @pl.loop(1, peers)
    def _(step):
        ask(step).start()

    @pl.loop(1, chips)
    def _(up):
        share(up).start()

    asked[me] = asking[me]
    source_all[:, core, chip] = local[...]
    arrived[peers] = jnp.zeros(arrived.shape[1:], arrived.dtype)

    @pl.loop(1, peers)
    def _(step):
        ask(step).wait()

    entries = asked[:, 0, :].astype(jnp.float32)
    sub, lane = iotas(peers)
    for slot in range(2):
        column_of = jnp.sum(jnp.where(lane == slot, entries, 0.0), axis=1, keepdims=True)
        wanted_rows[slot : slot + 1, :] = across(sub == lane, column_of).astype(jnp.int32)
    move(wanted_rows, wanted, 7).wait()
    tiles_copy.wait()

    @pl.loop(0, 64)
    def _(turn):
        step = narrow_step(turn)
        to = neighbour(step)
        stage[to, 0] = tile_for(to, 0)
        first(step).start()

    again, unplaced = make_plan(asked[:, 1, :], plan)
    move(plan, route, 3).wait()

    for k in range(LINKS):

        @pl.loop(0, ROOM[k])
        def _(s):
            link_out[BASE[k] + s] = tile_for(route[k, s], 1)

        link(k).start()

    @pl.loop(1, 64)
    def _(turn):
        step = wide_step(turn)
        to = neighbour(step)
        stage[to, 0] = tile_for(to, 0)
        first(step).start()

    arrived[me, 0] = tile_for(me, 0)

    for k in range(LINKS):
        link(k).wait()

    @pl.loop(1, 64)
    def _(turn):
        step = wide_step(turn)
        to = neighbour(step)
        stage[to, 1] = second_for(to)
        second(step).start()

    arrived[me, 1] = second_for(me)

    @pl.loop(1, chips)
    def _(up):
        share(up).wait()

    share_on().start()
    make_tables(owner_down, one_column(pair_pos[...]), plan)
    make_order(asked[:, 0, :].astype(jnp.float32), again, plan)
    keep_copy.wait()
    basis_copy.wait()
    mine = keep[pl.ds(pl.multiple_of(8 * chip, 8), 8), :]
    make_kept(jnp.where(core == 0, mine[0:4, :], mine[4:8, :]).astype(jnp.float32), plan)
    unplaced = unplaced + jnp.where(most_kept(keep) > ENTRIES, 1.0, 0.0)
    plan[AT_LEFT : AT_LEFT + 1, :] = jnp.broadcast_to(unplaced, (1, peers)).astype(jnp.int32)
    for b in range(blocks):
        for m in range(kt):
            chis[b * kt + m] = basis[b * rows : (b + 1) * rows, m * tile : (m + 1) * tile]
        for axis in range(3):
            row = local[2 + axis, b : b + 1, :]
            column[b * 6 + 2 + axis] = jnp.broadcast_to(row, (rows, rows)).T
        column[b * 6 + 5] = jnp.broadcast_to(local[0, b : b + 1, :], (rows, rows)).T
    move(plan, route, 4).wait()

    @pl.loop(1, peers)
    def _(step):
        first(step).wait()

    @pl.loop(1, 64)
    def _(turn):
        second(wide_step(turn)).wait()

    for b in range(blocks):

        @pl.loop(0, kt)
        def _(row):
            for column in range(kt):
                q = b * kt * kt + row * kt + column
                slot = route[AT_TABLE + q // peers, lax.rem(q, peers)]
                slot = jnp.where(
                    slot >= 4 * peers, route[AT_LOC, inside(slot - 4 * peers, peers)], slot
                )
                slot = inside(slot, 2 * peers + 1)
                dense[
                    b % 2,
                    pl.ds(pl.multiple_of(row * tile, tile), tile),
                    column * tile : (column + 1) * tile,
                ] = arrived[slot // 2, lax.rem(slot, 2)]

        chi = basis[b * rows : (b + 1) * rows, :]
        mixed = jnp.dot(chi, dense[b % 2], preferred_element_type=jnp.float32)
        both = mixed * chi.astype(jnp.float32)
        part = both[:, :tile]
        for m in range(1, kt):
            part = part + both[:, m * tile : (m + 1) * tile]
        raw_all[core, chip, b : b + 1, :] = jnp.sum(part.T, axis=0, keepdims=True)

    tell_partner().start()
    share_on().wait()
    tell_partner().wait()

    @pl.loop(1, chips)
    def _(up):
        tell(up).start()

    @pl.loop(1, chips)
    def _(up):
        tell(up).wait()

    density, omega, kappa = point_features(raw_all[...], source_all[1])
    feats[0] = (source_all[0] * density).reshape(blocks * peers, rows)
    feats[1] = omega.reshape(blocks * peers, rows)
    feats[2] = kappa.reshape(blocks * peers, rows)
    for axis in range(3):
        feats[3 + axis] = source_all[2 + axis].reshape(blocks * peers, rows)
    start = pl.multiple_of((core * chips + chip) * blocks, blocks)
    for b in range(blocks):
        for f in range(2):
            row = feats[1 + f, pl.ds(start + b, 1), :]
            column[b * 6 + f] = jnp.broadcast_to(row, (rows, rows)).T

    def one_pair(e, total):
        s = inside(route[AT_KEPT, e], blocks * peers)
        at = 6 * inside(route[AT_BLOCK, e], blocks)
        r2 = None
        for axis in range(3):
            gap = column[at + 2 + axis] - feats[3 + axis, pl.ds(s, 1), :]
            r2 = gap * gap if r2 is None else r2 + gap * gap
        g = column[at] * r2 + column[at + 1]
        h = feats[1, pl.ds(s, 1), :] * r2 + feats[2, pl.ds(s, 1), :]
        phi = -1.5 / (g * h * (g + h))
        total = jnp.where(route[AT_FIRST, e] > 0, 0.0, total) + phi * feats[0, pl.ds(s, 1), :]
        partial[e] = total
        return total

    lax.fori_loop(0, ENTRIES, one_pair, jnp.zeros((rows, rows), jnp.float32))
    for b in range(blocks):
        total = partial[inside(route[AT_LAST, b], ENTRIES)]
        wide = jnp.broadcast_to(jnp.sum(total, axis=1, keepdims=True), (rows, rows))
        field[b : b + 1, :] = wide.T[0:1, :]
        factor = column[b * 6 + 5] * wide
        for m in range(kt):
            part = chis[b * kt + m].astype(jnp.float32) * factor
            scaled[b * kt + m] = part.astype(jnp.bfloat16).T

    def first_back(step):
        to = neighbour(step)
        return remote(stage.at[to, 0], land.at[me], first_back_send, first_back_recv, step, to)

    def second_back(step):
        to = neighbour(step)
        return remote(
            stage.at[to, 1], seconds.at[me], second_back_send, second_back_recv, step, to
        )

    def link_back(k):
        return remote(
            link_out.at[pl.ds(BASE[k], ROOM[k])],
            land.at[pl.ds(2 * peers + BASE[k], ROOM[k])],
            link_back_send,
            link_back_recv,
            k,
            moved(me, back(STEPS[k])),
        )

    def product_for(device, slot):
        at = inside(route[AT_MINE + slot, device], 2 * peers)
        b, q = at // (kt * kt), lax.rem(at, kt * kt)
        return jnp.dot(
            scaled[b * kt + q // kt],
            chis[b * kt + lax.rem(q, kt)],
            preferred_element_type=jnp.float32,
        ).astype(jnp.bfloat16)

    def second_product(device):
        via = route[AT_SRC, device]
        return product_for(inside(jnp.where(via > 0, via - 1, device), peers), 1)

    @pl.loop(1, 64)
    def _(turn):
        step = wide_step(turn)
        to = neighbour(step)
        stage[to, 1] = second_product(to)
        second_back(step).start()

    seconds[me] = second_product(me)
    stage[me, 0] = product_for(me, 0)
    own = move(stage.at[me, 0], land.at[me], 5)

    @pl.loop(0, 64)
    def _(turn):
        step = narrow_step(turn)
        to = neighbour(step)
        stage[to, 0] = product_for(to, 0)
        first_back(step).start()

    @pl.loop(1, 64)
    def _(turn):
        second_back(wide_step(turn)).wait()

    for k in range(LINKS):

        @pl.loop(0, ROOM[k])
        def _(s):
            link_out[BASE[k] + s] = seconds[inside(route[LINKS + k, s], peers)]

        link_back(k).start()

    rest = move(seconds, land.at[pl.ds(peers, peers)], 6)

    @pl.loop(1, 64)
    def _(turn):
        step = wide_step(turn)
        to = neighbour(step)
        stage[to, 0] = product_for(to, 0)
        first_back(step).start()

    for k in range(LINKS):
        link_back(k).wait()

    @pl.loop(1, peers)
    def _(step):
        first_back(step).wait()

    own.wait()
    rest.wait()


def exchange(home, pair_tiles, pair_pos, pair_keep, weights, grad_sq, coords, tiles, basis):
    blocks, pairs = pair_tiles.shape
    tile = tiles.shape[1]
    peers = blocks * pairs
    rows = basis.shape[0] // blocks
    orbs = basis.shape[1]
    kt = orbs // tile
    smem = pl.BlockSpec(memory_space=pltpu.SMEM)
    vmem = pl.BlockSpec(memory_space=pltpu.VMEM)
    hbm = pl.BlockSpec(memory_space=pl.ANY)
    pair = pltpu.SemaphoreType.DMA((peers,))
    half = pltpu.SemaphoreType.DMA((peers // 2,))
    links = pltpu.SemaphoreType.DMA((LINKS,))
    return pl.pallas_call(
        exchange_kernel,
        in_specs=[vmem, vmem, vmem, hbm, vmem, vmem, vmem, hbm, hbm],
        out_specs=[vmem, vmem, vmem, hbm],
        out_shape=[
            jax.ShapeDtypeStruct((peers, 2, peers), jnp.int32),
            jax.ShapeDtypeStruct((PLAN_ROWS, peers), jnp.int32),
            jax.ShapeDtypeStruct((blocks, rows), jnp.float32),
            jax.ShapeDtypeStruct((2 * peers + RELAYED, tile, tile), tiles.dtype),
        ],
        scratch_shapes=[
            pltpu.SMEM((2, peers), jnp.int32),
            pltpu.SMEM((PLAN_ROWS, peers), jnp.int32),
            pltpu.VMEM(tiles.shape, tiles.dtype),
            pltpu.VMEM(basis.shape, basis.dtype),
            pltpu.VMEM((2, peers), jnp.int32),
            pltpu.VMEM((peers, 2, peers), jnp.int32),
            pltpu.VMEM(pair_keep.shape, jnp.int32),
            pltpu.VMEM((5, blocks, rows), jnp.float32),
            pltpu.VMEM((2, peers // 2, blocks, rows), jnp.float32),
            pltpu.VMEM((5, 2, peers // 2, blocks, rows), jnp.float32),
            pltpu.VMEM((6, blocks * peers, rows), jnp.float32),
            pltpu.VMEM((6 * blocks, rows, rows), jnp.float32),
            pltpu.VMEM((ENTRIES, rows, rows), jnp.float32),
            pltpu.VMEM((blocks * kt, tile, rows), basis.dtype),
            pltpu.VMEM((blocks * kt, rows, tile), basis.dtype),
            pltpu.VMEM((peers, tile, tile), basis.dtype),
            pltpu.VMEM((peers, 2, tile, tile), tiles.dtype),
            pltpu.VMEM((peers + 1, 2, tile, tile), tiles.dtype),
            pltpu.VMEM((RELAYED, tile, tile), tiles.dtype),
            pltpu.VMEM((RELAYED, tile, tile), tiles.dtype),
            pltpu.VMEM((2, orbs, orbs), basis.dtype),
            pltpu.SemaphoreType.DMA((8,)),
        ]
        + [pair] * 6
        + [links] * 2
        + [half] * 4
        + [pair] * 4
        + [links] * 2,
        compiler_params=params(collective_id=0, has_side_effects=True),
        name="exchange",
    )(home, pair_tiles, pair_pos, pair_keep, weights, grad_sq, coords, tiles, basis)


def pick_kernel(asked, tiles, out):
    step = pl.program_id(0)
    width = out.shape[0]

    @pl.loop(0, width)
    def _(slot):
        wanted = asked[step * width + slot]

        @pl.when(wanted >= 0)
        def _():
            out[slot] = tiles[wanted]


def pick_tiles(asked, tiles):
    count = asked.shape[0]
    group = 32
    return pl.pallas_call(
        pick_kernel,
        grid=(count // group,),
        in_specs=[
            pl.BlockSpec(memory_space=pltpu.SMEM),
            pl.BlockSpec(memory_space=pltpu.VMEM),
        ],
        out_specs=pl.BlockSpec((group,) + tiles.shape[1:], lambda i: (i, 0, 0)),
        out_shape=jax.ShapeDtypeStruct((count,) + tiles.shape[1:], tiles.dtype),
        compiler_params=params(),
        name="pick_tiles",
    )(asked, tiles)


def density_kernel(slots, positions, basis, arrived, raw, dense, sems):
    blocks, pairs = positions.shape
    rows = basis.shape[0] // blocks
    orbs = basis.shape[1]
    tile = arrived.shape[1]
    kt = orbs // tile

    dense[...] = jnp.zeros_like(dense)

    def fetch(b, k):
        q = positions[b, k]
        left = pl.multiple_of((q // kt) * tile, tile)
        right = pl.multiple_of((q % kt) * tile, tile)
        return pltpu.make_async_copy(
            arrived.at[slots[b * pairs + k]],
            dense.at[b, pl.ds(left, tile), pl.ds(right, tile)],
            sems.at[b * pairs + k],
        )

    for b in range(blocks):

        @pl.loop(0, pairs)
        def _(k):
            fetch(b, k).start()

    for b in range(blocks):

        @pl.loop(0, pairs)
        def _(k):
            fetch(b, k).wait()

        chi = basis[b * rows : (b + 1) * rows, :]
        mixed = jnp.dot(chi, dense[b], preferred_element_type=jnp.float32)
        both = mixed * chi.astype(jnp.float32)
        part = both[:, :tile]
        for m in range(1, kt):
            part = part + both[:, m * tile : (m + 1) * tile]
        raw[b : b + 1, :] = jnp.sum(part.T, axis=0, keepdims=True)


def block_density(slots, positions, basis, arrived):
    blocks = positions.shape[0]
    rows = basis.shape[0] // blocks
    orbs = basis.shape[1]
    return pl.pallas_call(
        density_kernel,
        in_specs=[
            pl.BlockSpec(memory_space=pltpu.SMEM),
            pl.BlockSpec(memory_space=pltpu.SMEM),
            pl.BlockSpec(memory_space=pltpu.VMEM),
            pl.BlockSpec(memory_space=pl.ANY),
        ],
        out_specs=pl.BlockSpec(memory_space=pltpu.VMEM),
        out_shape=jax.ShapeDtypeStruct((blocks, rows), jnp.float32),
        scratch_shapes=[
            pltpu.VMEM((blocks, orbs, orbs), basis.dtype),
            pltpu.SemaphoreType.DMA((positions.size,)),
        ],
        compiler_params=params(),
        name="block_density",
    )(slots, positions, basis, arrived)


def field_kernel(
    kept, counts, slots, positions, first, raw, source, basis, field, tiles_out, feats, column, scaled, staged, sems
):
    blocks, pairs = positions.shape
    rows = raw.shape[1]
    tile = tiles_out.shape[1]
    kt = basis.shape[1] // tile
    weights = source[:, 0]
    density, omega, kappa = point_features(raw[...], source[:, 1])
    feats[0] = weights * density
    feats[1] = omega
    feats[2] = kappa
    for axis in range(3):
        feats[3 + axis] = source[:, 2 + axis]

    def send(b, k):
        return pltpu.make_async_copy(
            staged.at[b * pairs + k], tiles_out.at[slots[b * pairs + k]], sems.at[b * pairs + k]
        )

    for b in range(blocks):
        at = first[0] + b
        for f in range(5):
            row = feats[1 + f, pl.ds(at, 1), :]
            column[f] = jnp.broadcast_to(row, (rows, rows)).T

        def one_source(j, total):
            s = kept[b, j]
            r2 = None
            for axis in range(3):
                gap = column[2 + axis] - feats[3 + axis, pl.ds(s, 1), :]
                r2 = gap * gap if r2 is None else r2 + gap * gap
            g = column[0] * r2 + column[1]
            h = feats[1, pl.ds(s, 1), :] * r2 + feats[2, pl.ds(s, 1), :]
            phi = -1.5 / (g * h * (g + h))
            return total + phi * feats[0, pl.ds(s, 1), :]

        total = lax.fori_loop(0, counts[b], one_source, jnp.zeros((rows, rows), jnp.float32))
        potential = jnp.sum(total, axis=1, keepdims=True)
        wide = jnp.broadcast_to(potential, (rows, rows))
        field[b : b + 1, :] = wide.T[0:1, :]
        weight = jnp.broadcast_to(source[pl.ds(at, 1), 0], (rows, rows)).T
        factor = weight * wide
        for m in range(kt):
            chi = basis[b * rows : (b + 1) * rows, m * tile : (m + 1) * tile]
            scaled[m] = (chi.astype(jnp.float32) * factor).astype(jnp.bfloat16).T
            scaled[kt + m] = chi

        @pl.loop(0, pairs)
        def _(k):
            q = positions[b, k]
            product = jnp.dot(
                scaled[q // kt], scaled[kt + q % kt], preferred_element_type=jnp.float32
            )
            staged[b * pairs + k] = product.astype(jnp.bfloat16)
            send(b, k).start()

    for b in range(blocks):

        @pl.loop(0, pairs)
        def _(k):
            send(b, k).wait()


def field_and_tiles(kept, counts, slots, positions, first, raw, source, basis, slot_count):
    blocks, pairs = positions.shape
    total, rows = raw.shape
    tile = 128
    kt = basis.shape[1] // tile
    smem = pl.BlockSpec(memory_space=pltpu.SMEM)
    vmem = pl.BlockSpec(memory_space=pltpu.VMEM)
    return pl.pallas_call(
        field_kernel,
        in_specs=[smem] * 5 + [vmem] * 3,
        out_specs=[vmem, pl.BlockSpec(memory_space=pl.ANY)],
        out_shape=[
            jax.ShapeDtypeStruct((blocks, rows), jnp.float32),
            jax.ShapeDtypeStruct((slot_count, tile, tile), jnp.bfloat16),
        ],
        scratch_shapes=[
            pltpu.VMEM((6, total, rows), jnp.float32),
            pltpu.VMEM((5, rows, rows), jnp.float32),
            pltpu.VMEM((2 * kt, tile, rows), jnp.bfloat16),
            pltpu.VMEM((blocks * pairs, tile, tile), jnp.bfloat16),
            pltpu.SemaphoreType.DMA((blocks * pairs,)),
        ],
        compiler_params=params(),
        name="field_and_tiles",
    )(kept, counts, slots, positions, first, raw, source, basis)


def collect_kernel(order, starts, landed, out):
    step = pl.program_id(0)
    width = out.shape[0]

    @pl.loop(0, width)
    def _(t):
        g = step * width + t

        def add(j, total):
            return total + landed[order[j]].astype(jnp.float32)

        out[t] = lax.fori_loop(
            starts[g], starts[g + 1], add, jnp.zeros(out.shape[1:], jnp.float32)
        )


def collect_tiles(order, starts, landed, store_count):
    tile = landed.shape[1]
    group = 8
    smem = pl.BlockSpec(memory_space=pltpu.SMEM)
    return pl.pallas_call(
        collect_kernel,
        grid=(store_count // group,),
        in_specs=[smem, smem, pl.BlockSpec(memory_space=pltpu.VMEM)],
        out_specs=pl.BlockSpec((group, tile, tile), lambda i: (i, 0, 0)),
        out_shape=jax.ShapeDtypeStruct((store_count, tile, tile), jnp.float32),
        compiler_params=params(limit=61 * 2**20),
        name="collect_tiles",
    )(order, starts, landed)


def collect_planned_kernel(plan, landed, out, sums, sems):
    count = sums.shape[0]
    group = 8
    peers = plan.shape[1]

    def write(g):
        part = pl.ds(pl.multiple_of(g * group, group), group)
        return pltpu.make_async_copy(sums.at[part], out.at[part], sems.at[g])

    @pl.loop(0, count // group)
    def _(g):
        for t in range(group):
            at = g * group + t

            def add(j, total):
                place = plan[AT_ORDER + j // peers, lax.rem(j, peers)]
                return total + landed[place].astype(jnp.float32)

            sums[at] = lax.fori_loop(
                plan[AT_STARTS, at],
                plan[AT_STARTS, at + 1],
                add,
                jnp.zeros(sums.shape[1:], jnp.float32),
            )
        write(g).start()

    @pl.loop(0, count // group)
    def _(g):
        write(g).wait()


def collect_planned(plan, landed, store_count):
    tile = landed.shape[1]
    return pl.pallas_call(
        collect_planned_kernel,
        in_specs=[
            pl.BlockSpec(memory_space=pltpu.SMEM),
            pl.BlockSpec(memory_space=pltpu.VMEM),
        ],
        out_specs=pl.BlockSpec(memory_space=pl.ANY),
        out_shape=jax.ShapeDtypeStruct((store_count, tile, tile), jnp.float32),
        scratch_shapes=[
            pltpu.VMEM((store_count, tile, tile), jnp.float32),
            pltpu.SemaphoreType.DMA((store_count // 8,)),
        ],
        compiler_params=params(limit=61 * 2**20),
        name="collect_planned",
    )(plan, landed)


def kept_list(keep):
    width = keep.shape[1]
    places = jnp.arange(width, dtype=jnp.int32)
    rank = jnp.cumsum(keep, axis=1) - keep
    hit = (rank[:, :, None] == places[None, None, :]) & (keep[:, :, None] > 0)
    return (
        jnp.sum(jnp.where(hit, places[None, :, None], 0), axis=1),
        jnp.sum(keep, axis=1),
    )


def slot_order(asked, store_count):
    count = asked.shape[0]
    places = jnp.arange(count, dtype=jnp.int32)
    key = jnp.where(asked >= 0, asked, store_count) * count + places
    rank = jnp.sum((key[None, :] < key[:, None]).astype(jnp.int32), axis=1)
    order = jnp.sum(jnp.where(rank[:, None] == places[None, :], places[:, None], 0), axis=0)
    stores = jnp.arange(store_count + 1, dtype=jnp.int32)
    starts = jnp.sum(
        ((asked[None, :] >= 0) & (asked[None, :] < stores[:, None])).astype(jnp.int32), axis=1
    )
    return order, starts


def body(basis, dmat, tile_home, pair_tiles, pair_pos, coords, weights, grad_sq, pair_keep):
    peers = lax.axis_size(AXES)
    me = lax.axis_index(AXES)
    blocks, pairs = pair_tiles.shape
    store_count, tile = dmat.shape[0], dmat.shape[1]
    rows = basis.shape[0] // blocks
    capacity = 2
    slot_count = peers * capacity
    asked, plan, field, land = exchange(
        tile_home.reshape(-1, tile),
        pair_tiles,
        pair_pos,
        pair_keep,
        weights.reshape(blocks, rows),
        grad_sq.reshape(blocks, rows),
        coords,
        dmat,
        basis,
    )

    def two_slots():
        wanted = tile_home[pair_tiles.reshape(-1)]
        owner = wanted // store_count
        same = owner[:, None] == owner[None, :]
        places = jnp.arange(blocks * pairs, dtype=jnp.int32)
        earlier = jnp.sum((same & (places[None, :] < places[:, None])).astype(jnp.int32), axis=1)
        slots = owner * capacity + earlier
        requests = asked[:, 0, :capacity].reshape(-1) - 1
        shape = (peers, capacity, tile, tile)

        def swap(values):
            return lax.all_to_all(
                values.reshape(shape), AXES, split_axis=0, concat_axis=0, tiled=True
            ).reshape(slot_count, tile, tile)

        def spread(values):
            wide = jnp.broadcast_to(values[None], (peers,) + values.shape)
            return lax.all_to_all(wide, AXES, split_axis=0, concat_axis=0, tiled=True)

        arrived = swap(pick_tiles(requests, dmat))
        again = spread(block_density(slots, pair_pos, basis, arrived))
        local = jnp.concatenate([weights[None], grad_sq[None], coords], axis=0)
        features = spread(local.reshape(5, blocks, rows).transpose(1, 0, 2))
        keep = lax.dynamic_slice_in_dim(pair_keep, me * blocks, blocks, 0)
        kept, counts = kept_list(keep)
        first = (me * blocks).astype(jnp.int32).reshape(1)
        again, returning = field_and_tiles(
            kept,
            counts,
            slots,
            pair_pos,
            first,
            again.reshape(peers * blocks, rows),
            features.reshape(peers * blocks, 5, rows),
            basis,
            slot_count,
        )
        order, starts = slot_order(requests, store_count)
        return collect_tiles(order, starts, swap(returning), store_count), again

    def relays():
        return collect_planned(plan, land, store_count), field

    pieces, potential = lax.cond(plan[AT_LEFT, 0] > 0, two_slots, relays)
    return pieces, potential.reshape(-1)


def solution(mesh):
    in_specs = (
        P(AXES, None),
        P(AXES, None, None),
        P(),
        P(AXES, None),
        P(AXES, None),
        P(None, AXES),
        P(AXES),
        P(AXES),
        P(),
    )
    out_specs = (P(AXES, None, None), P(AXES))
    return jax.shard_map(body, mesh=mesh, in_specs=in_specs, out_specs=out_specs, check_vma=False)
```
